32 devices in a mesh: dp: 16 (over z, y, x), blk: 2 (over core).
Axes of the slice: x: 2, y: 2, z: 4, core: 2. Of those that a mesh axis runs over, the one named last changes fastest.
Arguments:
- token_ids: int32 [32, 1024], P('dp', 'blk'), may hold values from 0 to 31999
- seq_lengths: int32 [32], P('dp'), may hold values from 32 to 1024, as said below
- diffusion_time: int32 [32], P('dp'), may hold values from 1 to 300
- embed_table: bfloat16 [32000, 256], replicated, may hold values from -6 to 6
- w_embed: bfloat16 [256, 1024], replicated, may hold values from -0.375 to 0.375
- w_time: bfloat16 [256, 4096], replicated, may hold values from -0.1875 to 0.1875
- gain_attn: float32 [1024], replicated, may hold values from 0.1 to 1.9
- bias_attn: float32 [1024], replicated, may hold values from -3 to 3
- gain_mlp: float32 [1024], replicated, may hold values from 0.1 to 1.9
- bias_mlp: float32 [1024], replicated, may hold values from -3 to 3
- w_qkv: bfloat16 [1024, 3072], replicated, may hold values from -0.1875 to 0.1875
- w_out: bfloat16 [1024, 1024], replicated, may hold values from -0.75 to 0.75
- w_up: bfloat16 [1024, 4096], replicated, may hold values from -0.1875 to 0.1875
- w_down: bfloat16 [4096, 1024], replicated, may hold values from -0.09375 to 0.09375
- cotangent: bfloat16 [32, 1024, 1024], P('dp', 'blk'), may hold values from -6 to 6
Outputs:
- layer_out: bfloat16 [32, 1024, 1024], P('dp', 'blk')
- grad_input: bfloat16 [32, 1024, 1024], P('dp', 'blk')
- grad_table: float32 [32000, 256], P(('dp', 'blk'))
- grad_w_embed: float32 [256, 1024], P(None, ('dp', 'blk'))
- grad_w_time: float32 [256, 4096], P(None, ('dp', 'blk'))
- grad_gain_attn: float32 [1024], P(('dp', 'blk'))
- grad_bias_attn: float32 [1024], P(('dp', 'blk'))
- grad_gain_mlp: float32 [1024], P(('dp', 'blk'))
- grad_bias_mlp: float32 [1024], P(('dp', 'blk'))
- grad_w_qkv: float32 [1024, 3072], P(None, ('dp', 'blk'))
- grad_w_out: float32 [1024, 1024], P(None, ('dp', 'blk'))
- grad_w_up: float32 [1024, 4096], P(None, ('dp', 'blk'))
- grad_w_down: float32 [4096, 1024], P(None, ('dp', 'blk'))
The draws below stay inside these ranges and needn't reach their ends.
Inputs may be any that keep to these rules, and one draw needn't show every extreme that they name: `seq_lengths`: of the 2 sequences of one index of dp, one has exactly 1024 real tokens; positions at or past a sequence's length are padding.
All inputs are finite; a program needn't handle non-finite values.
Results may differ from the reference program's by a relative error of at most 0.02.
Values may be sent and summed in bfloat16 or wider, within the bound.
No kernel may reach another device: no remote copies, remote signals or barrier semaphores. Data moves between devices by JAX's collectives and lax.ppermute only.
A program may use at most 384 MiB of HBM per device.

```python
import math
import jax
import jax.numpy as jnp
from jax import lax

D = 1024
HEADS = 16
HEAD_DIM = 64
FF = 4096
EMB = 256
VOCAB = 32000
TIME_WIDTH = 256
SEQ_LEN = 1024
GROUP_SEQS = 2
SEQS = 32
SHORTEST = 32


def draw_seq_lengths(key, part):
    key = jax.random.fold_in(key, 11)
    first_key, second_key = jax.random.split(key)
    group_count = SEQS // GROUP_SEQS
    others = jax.random.randint(first_key, (group_count, GROUP_SEQS), SHORTEST, SEQ_LEN + 1)
    full_slot = jax.random.randint(second_key, (group_count,), 0, GROUP_SEQS)
    is_full = jnp.arange(GROUP_SEQS)[None, :] == full_slot[:, None]
    return jnp.where(is_full, SEQ_LEN, others).reshape(SEQS).astype(jnp.int32)


def touch_ends(entries, own_key, least, top_value):
    dims = entries.shape
    spot = [jax.random.randint(jax.random.fold_in(own_key, axis), (), 0, dims[axis]) for axis in range(len(dims))]
    entries = entries.at[tuple(spot)].set(least)
    longest = dims.index(max(dims))
    spot[longest] = (spot[longest] + 1) % dims[longest]
    return entries.at[tuple(spot)].set(top_value)


def with_spikes(values, stream_key, source, target, blocks, factor):
    owner, partner = [(jnp.arange(values.shape[dim]) // (values.shape[dim] // blocks)).reshape([-1 if axis == dim else 1 for axis in range(values.ndim)]) for dim in (source, target)]
    chosen = jax.random.permutation(stream_key, blocks)[partner]
    strong = (owner == chosen) | (owner == (partner + blocks // 2) % blocks)
    return jnp.where(strong, factor * values, values)


def levels(key, extent, cuts, smallest, top_value):
    gain, own = 1.0, jax.random.fold_in(key, 6)
    for position, parts in cuts:
        draws = jnp.exp(jax.random.uniform(jax.random.fold_in(own, position), (parts,), jnp.float32, smallest / len(cuts), top_value / len(cuts)))
        gain = gain * jnp.repeat(draws, extent[position] // parts).reshape([-1 if axis == position else 1 for axis in range(len(extent))])
    return gain


def scatter_about(key, dims, deviation, bound, cuts=(), held_as=jnp.bfloat16):
    factor_of = levels(key, dims, cuts, -0.22, 0.18) if cuts else 1.0
    values = jax.random.normal(key, dims, jnp.float32) * deviation * factor_of
    return jnp.minimum(jnp.maximum(values, -bound), bound).astype(held_as)


def noise_with(rng, shape, scale, most, cuts, heavy, held_as=jnp.bfloat16):
    array = scale * jax.random.normal(rng, shape, jnp.float32)
    if cuts:
        array = array * levels(rng, shape, cuts, -0.22, 0.18)
    return jnp.clip(with_spikes(array, jax.random.fold_in(rng, 3), *heavy), -most, most).astype(held_as)


def setup_inputs(seed: int = 0) -> dict:
    arg_keys = jax.random.split(jax.random.key(seed), 16)
    token_ids = touch_ends(jax.random.randint(arg_keys[0], (SEQS, SEQ_LEN), 0, VOCAB), jax.random.fold_in(arg_keys[0], 1), 0, VOCAB - 1).astype(jnp.int32)
    seq_lengths = draw_seq_lengths(jax.random.fold_in(arg_keys[15], 71), 0)
    diffusion_time = touch_ends(jax.random.randint(arg_keys[2], (SEQS,), 1, 301), jax.random.fold_in(arg_keys[2], 1), 1, 300).astype(jnp.int32)
    embed_table = scatter_about(arg_keys[3], (VOCAB, EMB), 1.0, 6.0)
    w_embed = scatter_about(arg_keys[4], (EMB, D), EMB ** -0.5, 0.375)
    w_time = scatter_about(arg_keys[5], (TIME_WIDTH, 4 * D), (4 * TIME_WIDTH) ** -0.5, 0.1875)
    gain_attn = jnp.clip(1.0 + 0.18 * jax.random.normal(arg_keys[6], (D,), jnp.float32), 0.1, 1.9)
    bias_attn = scatter_about(arg_keys[7], (D,), 0.5, 3.0, (), jnp.float32)
    gain_mlp = jnp.clip(1.0 + 0.18 * jax.random.normal(arg_keys[8], (D,), jnp.float32), 0.1, 1.9)
    bias_mlp = scatter_about(arg_keys[9], (D,), 0.5, 3.0, (), jnp.float32)
    w_qkv = scatter_about(arg_keys[10], (D, 3 * D), D ** -0.5, 0.1875)
    w_out = scatter_about(arg_keys[11], (D, D), (D // 16) ** -0.5, 0.75)
    w_up = scatter_about(arg_keys[12], (D, FF), D ** -0.5, 0.1875)
    w_down = scatter_about(arg_keys[13], (FF, D), FF ** -0.5, 0.09375)
    cotangent = noise_with(arg_keys[14], (SEQS, SEQ_LEN, D), 1.0, 6.0, ((0, 16), (1, 2)), (0, 2, 16, 2.0))
    return {"token_ids": token_ids, "seq_lengths": seq_lengths, "diffusion_time": diffusion_time, "embed_table": embed_table, "w_embed": w_embed, "w_time": w_time, "gain_attn": gain_attn, "bias_attn": bias_attn, "gain_mlp": gain_mlp, "bias_mlp": bias_mlp, "w_qkv": w_qkv, "w_out": w_out, "w_up": w_up, "w_down": w_down, "cotangent": cotangent}


NEG_FILL = -1000000000.0

@jax.custom_vjp
def low(v):
    return lax.optimization_barrier(v.astype(jnp.bfloat16)).astype(jnp.float32)

@jax.custom_vjp
def low_back(v):
    return v

def low_keep(v):
    return (low(v), None)

def low_pass(kept, grad):
    return (grad,)

def back_keep(v):
    return (v, None)

def back_low(kept, grad):
    return (low(grad),)
low.defvjp(low_keep, low_pass)
low_back.defvjp(back_keep, back_low)

def time_features(diffusion_time, feature_width):
    half_width = feature_width // 2
    frequency = jnp.exp(-math.log(1000.0) * jnp.arange(half_width, dtype=jnp.float32) / half_width)
    angles = diffusion_time.astype(jnp.float32)[:, None] * frequency[None, :]
    return jnp.concatenate([jnp.sin(angles), jnp.cos(angles)], axis=1)

def modulated_norm(features, gain_vec, bias_vec, scale_rows, shift_rows):
    center = features - lax.optimization_barrier(jnp.mean(features, axis=-1, keepdims=True))
    spread = lax.optimization_barrier(jnp.mean(center * center, axis=-1, keepdims=True))
    return center * lax.rsqrt(spread + 1e-05) * (gain_vec + scale_rows[:, None, :]) + (bias_vec + shift_rows[:, None, :])

def matmul_rows(left_side, right_side):
    return jnp.einsum('spd,df->spf', left_side, right_side, precision=lax.Precision.HIGHEST)

def attend_one(packed):
    query_seq, key_seq, value_seq, seq_len = packed
    scores = low_back(jnp.einsum('qhd,khd->hqk', query_seq, key_seq, precision=lax.Precision.HIGHEST)) * HEAD_DIM ** (-0.5)
    key_keep = (jnp.arange(SEQ_LEN) < seq_len)[None, None, :]
    scores = jnp.where(key_keep, scores, NEG_FILL)
    weights = low(jax.nn.softmax(scores, axis=-1))
    return jnp.einsum('hqk,khd->qhd', weights, value_seq, precision=lax.Precision.HIGHEST)

def forward(embed_table, w_embed, w_time, gain_attn, bias_attn, gain_mlp, bias_mlp, w_qkv, w_out, w_up, w_down, zero_input, group_ids, group_lengths, group_time):
    seq_count = group_ids.shape[0]
    emb_rows = embed_table[group_ids]
    normed = emb_rows * lax.rsqrt(lax.optimization_barrier(jnp.mean(emb_rows * emb_rows, axis=-1, keepdims=True)) + 1e-06)
    inputs = low_back(matmul_rows(low(normed), w_embed)) + zero_input
    modulation = jnp.dot(low(time_features(group_time, TIME_WIDTH)), w_time, precision=lax.Precision.HIGHEST)
    scale_attn, shift_attn, scale_mlp, shift_mlp = jnp.split(modulation, 4, axis=1)
    normed_attn = low(modulated_norm(inputs, gain_attn, bias_attn, scale_attn, shift_attn))
    qkv = low(low_back(matmul_rows(normed_attn, w_qkv)))
    queries = qkv[:, :, :D].reshape(seq_count, SEQ_LEN, HEADS, HEAD_DIM)
    key_heads = qkv[:, :, D:2 * D].reshape(seq_count, SEQ_LEN, HEADS, HEAD_DIM)
    value_heads = qkv[:, :, 2 * D:].reshape(seq_count, SEQ_LEN, HEADS, HEAD_DIM)
    attended = lax.map(jax.checkpoint(attend_one), (queries, key_heads, value_heads, group_lengths))
    attended = low(low_back(attended.reshape(seq_count, SEQ_LEN, D)))
    residual = inputs + low_back(matmul_rows(attended, w_out))
    normed_mlp = low(modulated_norm(residual, gain_mlp, bias_mlp, scale_mlp, shift_mlp))
    hidden = low(jax.nn.gelu(low_back(matmul_rows(normed_mlp, w_up))))
    final_sum = residual + low_back(matmul_rows(hidden, w_down))
    valid_rows = (jnp.arange(SEQ_LEN)[None, :] < group_lengths[:, None]).astype(jnp.float32)
    return final_sum * valid_rows[:, :, None]

def reference(token_ids, seq_lengths, diffusion_time, embed_table, w_embed, w_time, gain_attn, bias_attn, gain_mlp, bias_mlp, w_qkv, w_out, w_up, w_down, cotangent):
    params = tuple((p.astype(jnp.float32) for p in (embed_table, w_embed, w_time, gain_attn, bias_attn, gain_mlp, bias_mlp, w_qkv, w_out, w_up, w_down)))
    group_count = SEQS // GROUP_SEQS
    ids_grouped = token_ids.reshape(group_count, GROUP_SEQS, SEQ_LEN)
    lengths_grouped = seq_lengths.reshape(group_count, GROUP_SEQS)
    time_grouped = diffusion_time.reshape(group_count, GROUP_SEQS)
    cot_grouped = cotangent.reshape(group_count, GROUP_SEQS, SEQ_LEN, D)

    def group_step(running_total, group):
        group_ids, group_lengths, group_time, group_cot = group
        zero_input = jnp.zeros((GROUP_SEQS, SEQ_LEN, D), jnp.float32)

        def layer_fn(*arguments):
            return forward(*arguments, group_ids, group_lengths, group_time)
        result, pull_back = jax.vjp(layer_fn, *params, zero_input)
        gradients = pull_back(group_cot.astype(jnp.float32))
        running_total = tuple((t + g for t, g in zip(running_total, gradients[:-1])))
        return (running_total, (result.astype(jnp.bfloat16), gradients[-1].astype(jnp.bfloat16)))
    start_total = tuple((jnp.zeros_like(p) for p in params))
    totals, (outputs, input_grads) = lax.scan(group_step, start_total, (ids_grouped, lengths_grouped, time_grouped, cot_grouped))
    layer_out = outputs.reshape(SEQS, SEQ_LEN, D)
    grad_input = input_grads.reshape(SEQS, SEQ_LEN, D)
    return (layer_out, grad_input, totals[0], totals[1], totals[2], totals[3], totals[4], totals[5], totals[6], totals[7], totals[8], totals[9], totals[10])
```

```python
import functools
import math

import jax
import jax.numpy as jnp
from jax import lax
from jax.experimental import pallas as pl
from jax.experimental.pallas import tpu as pltpu
from jax.sharding import PartitionSpec as P

D = 1024
HEADS = 16
HEAD_DIM = 64
EMB = 256
VOCAB = 32000
TIME_WIDTH = 256


NEG_FILL = -1000000000.0


def from_behind(value, axis, steps):
    count = lax.axis_size(axis)
    pairs = [(source, (source + steps) % count) for source in range(count)]
    return lax.ppermute(value, axis, pairs)


def time_features(diffusion_time, feature_width):
    half_width = feature_width // 2
    frequency = jnp.exp(-math.log(1000.0) * jnp.arange(half_width, dtype=jnp.float32) / half_width)
    angles = diffusion_time.astype(jnp.float32)[:, None] * frequency[None, :]
    return jnp.concatenate([jnp.sin(angles), jnp.cos(angles)], axis=1)


def modulated_norm(features, gain_vec, bias_vec, scale_rows, shift_rows):
    center = features - jnp.mean(features, axis=-1, keepdims=True)
    spread = jnp.mean(center * center, axis=-1, keepdims=True)
    return center * lax.rsqrt(spread + 1e-05) * (gain_vec + scale_rows[:, None, :]) + (
        bias_vec + shift_rows[:, None, :]
    )


def normalize_rows(row_values):
    return row_values * lax.rsqrt(jnp.mean(row_values * row_values, axis=-1, keepdims=True) + 1e-06)


def project(left_side, right_side):
    return lax.dot_general(
        left_side,
        right_side,
        (((left_side.ndim - 1,), (0,)), ((), ())),
        preferred_element_type=jnp.float32,
    )


def project_back(left_side, right_side):
    return lax.dot_general(
        left_side,
        right_side,
        (((left_side.ndim - 1,), (1,)), ((), ())),
        preferred_element_type=jnp.float32,
    )


def outer_sum(left_side, right_side):
    return lax.dot_general(
        left_side, right_side, (((0, 1), (0, 1)), ((), ())), preferred_element_type=jnp.float32
    )


def scatter_rows(running_total, offsets, grad_values):
    row_span = running_total.shape[0]
    inside = (offsets >= 0) & (offsets < row_span)
    return running_total.at[jnp.where(inside, offsets, row_span)].add(grad_values, mode="drop")


def group_columns(matrix, group_count):
    if matrix.ndim == 1:
        return matrix.reshape(1, group_count, matrix.shape[0] // group_count)
    return matrix.reshape(matrix.shape[0], group_count, matrix.shape[1] // group_count)


def split_position_shards(
    token_ids,
    seq_lengths,
    diffusion_time,
    embed_table,
    w_embed,
    w_time,
    gain_attn,
    bias_attn,
    gain_mlp,
    bias_mlp,
    w_qkv,
    w_out,
    w_up,
    w_down,
    cotangent,
):
    seq_count, pos_count = token_ids.shape
    scale_factor = HEAD_DIM ** (-0.5)
    cycle_size = lax.axis_size("blk")
    cycle_index = lax.axis_index("blk")
    positions = cycle_index * pos_count + jnp.arange(pos_count, dtype=jnp.int32)
    valid_rows = (positions[None, :] < seq_lengths[:, None]).astype(jnp.float32)[:, :, None]
    emb_rows = embed_table[token_ids].astype(jnp.float32)
    normed, norm_pull = jax.vjp(normalize_rows, emb_rows)
    normed_low = normed.astype(jnp.bfloat16)
    inputs = project(normed_low, w_embed)
    time_low = time_features(diffusion_time, TIME_WIDTH).astype(jnp.bfloat16)
    modulation = jnp.dot(time_low, w_time, preferred_element_type=jnp.float32)
    scale_attn, shift_attn, scale_mlp, shift_mlp = jnp.split(modulation, 4, axis=1)
    normed_attn, attn_pull = jax.vjp(
        modulated_norm, inputs, gain_attn, bias_attn, scale_attn, shift_attn
    )
    attn_low = normed_attn.astype(jnp.bfloat16)
    qkv_low = project(attn_low, w_qkv).astype(jnp.bfloat16)
    queries = qkv_low[:, :, :D].reshape(seq_count, pos_count, HEADS, HEAD_DIM)
    kv_local = qkv_low[:, :, D:]

    def masked_scores(key_heads, key_start):
        key_count = key_heads.shape[1]
        key_pos = key_start + jnp.arange(key_count, dtype=jnp.int32)
        key_keep = (key_pos[None, :] < seq_lengths[:, None])[:, None, None, :]
        scores = (
            jnp.einsum("sqhd,skhd->shqk", queries, key_heads, preferred_element_type=jnp.float32)
            * scale_factor
        )
        return jnp.where(key_keep, scores, NEG_FILL)

    key_piece = lax.all_gather(kv_local, "blk", axis=1, tiled=True)
    run_max = jnp.full((seq_count, HEADS, pos_count), -1e30, jnp.float32)
    key_count = key_piece.shape[1]
    key_heads = key_piece[:, :, :D].reshape(seq_count, key_count, HEADS, HEAD_DIM)
    value_heads = key_piece[:, :, D:].reshape(seq_count, key_count, HEADS, HEAD_DIM)
    scores = masked_scores(key_heads, jnp.int32(0))
    new_max = jnp.maximum(run_max, jnp.max(scores, axis=-1))
    softmax_weights = jnp.exp(scores - new_max[..., None])
    run_sum = jnp.sum(softmax_weights, axis=-1)
    contrib = jnp.einsum(
        "shqk,skhd->sqhd",
        softmax_weights.astype(jnp.bfloat16),
        value_heads,
        preferred_element_type=jnp.float32,
    )
    run_acc = contrib
    run_max, run_sum, run_acc = (new_max, run_sum, run_acc)
    log_total = run_max + jnp.log(run_sum)
    attended = run_acc / jnp.transpose(run_sum, (0, 2, 1))[..., None]
    attended_low = attended.reshape(seq_count, pos_count, D).astype(jnp.bfloat16)
    residual = inputs + project(attended_low, w_out)
    normed_mlp, mlp_pull = jax.vjp(
        modulated_norm, residual, gain_mlp, bias_mlp, scale_mlp, shift_mlp
    )
    mlp_low = normed_mlp.astype(jnp.bfloat16)
    pre_act = project(mlp_low, w_up)
    activated, gelu_pull = jax.vjp(jax.nn.gelu, pre_act)
    hidden_low = activated.astype(jnp.bfloat16)
    final_sum = (residual + project(hidden_low, w_down)) * valid_rows
    layer_out = final_sum.astype(jnp.bfloat16)
    grad_final = cotangent.astype(jnp.float32) * valid_rows
    final_low = grad_final.astype(jnp.bfloat16)
    grad_w_down = outer_sum(hidden_low, final_low)
    (grad_pre,) = gelu_pull(project_back(final_low, w_down))
    pre_low = grad_pre.astype(jnp.bfloat16)
    grad_w_up = outer_sum(mlp_low, pre_low)
    grad_res_norm, grad_gain_mlp, grad_bias_mlp, grad_scale_mlp, grad_shift_mlp = mlp_pull(
        project_back(pre_low, w_up)
    )
    residual_grad = grad_final + grad_res_norm
    residual_low = residual_grad.astype(jnp.bfloat16)
    grad_w_out = outer_sum(attended_low, residual_low)
    grad_att = (
        project_back(residual_low, w_out)
        .astype(jnp.bfloat16)
        .reshape(seq_count, pos_count, HEADS, HEAD_DIM)
    )
    row_delta = jnp.transpose(jnp.sum(grad_att * attended, axis=-1), (0, 2, 1))

    def key_block(kv_block, owner_index):
        key_heads = kv_block[:, :, :D].reshape(seq_count, pos_count, HEADS, HEAD_DIM)
        value_heads = kv_block[:, :, D:].reshape(seq_count, pos_count, HEADS, HEAD_DIM)
        scores = masked_scores(key_heads, owner_index * pos_count)
        softmax_weights = jnp.exp(scores - log_total[..., None])
        grad_weights = jnp.einsum(
            "sqhd,skhd->shqk", grad_att, value_heads, preferred_element_type=jnp.float32
        )
        grad_scores = (
            softmax_weights * (grad_weights - row_delta[..., None]) * scale_factor
        ).astype(jnp.bfloat16)
        grad_queries = jnp.einsum(
            "shqk,skhd->sqhd", grad_scores, key_heads, preferred_element_type=jnp.float32
        )
        grad_keys = jnp.einsum(
            "shqk,sqhd->skhd", grad_scores, queries, preferred_element_type=jnp.float32
        )
        grad_values = jnp.einsum(
            "shqk,sqhd->skhd",
            softmax_weights.astype(jnp.bfloat16),
            grad_att,
            preferred_element_type=jnp.float32,
        )
        joined = jnp.concatenate(
            [
                grad_keys.reshape(seq_count, pos_count, D),
                grad_values.reshape(seq_count, pos_count, D),
            ],
            axis=-1,
        )
        return (grad_queries, joined)

    def pass_back(grad_values):
        return from_behind(grad_values.astype(jnp.bfloat16), "blk", 1).astype(grad_values.dtype)

    zero_kv = jnp.zeros((seq_count, pos_count, 2 * D), jnp.float32)
    zero_query = jnp.zeros((seq_count, pos_count, HEADS, HEAD_DIM), jnp.float32)

    def cycle_step(turn_index, cycle_state):
        kv_block, grad_kv, grad_query = cycle_state
        part_query, part_kv = key_block(kv_block, (cycle_index - turn_index) % cycle_size)
        kv_block = from_behind(kv_block, "blk", 1)
        return (kv_block, pass_back(grad_kv + part_kv), grad_query + part_query)

    kv_block, grad_kv, grad_query = lax.fori_loop(
        0, cycle_size - 1, cycle_step, (kv_local, zero_kv, zero_query)
    )
    part_query, part_kv = key_block(kv_block, (cycle_index + 1) % cycle_size)
    grad_kv = pass_back(grad_kv + part_kv)
    grad_query = grad_query + part_query
    grad_qkv = jnp.concatenate(
        [grad_query.reshape(seq_count, pos_count, D), grad_kv], axis=-1
    ).astype(jnp.bfloat16)
    grad_w_qkv = outer_sum(attn_low, grad_qkv)
    grad_in_norm, grad_gain_attn, grad_bias_attn, grad_scale_attn, grad_shift_attn = attn_pull(
        project_back(grad_qkv, w_qkv)
    )
    input_grad = residual_grad + grad_in_norm
    grad_input = input_grad.astype(jnp.bfloat16)
    grad_w_embed = outer_sum(normed_low, grad_input)
    grad_modulation = jnp.concatenate(
        [grad_scale_attn, grad_shift_attn, grad_scale_mlp, grad_shift_mlp], axis=1
    )
    grad_w_time = jnp.dot(
        time_low.astype(jnp.float32).T, grad_modulation, precision=lax.Precision.HIGHEST
    )
    (grad_rows,) = norm_pull(project_back(grad_input, w_embed))
    flat_ids = token_ids.reshape(-1)
    flat_grads = grad_rows.reshape(-1, EMB)
    row_count = VOCAB // lax.axis_size(("dp", "blk"))
    own_start = lax.axis_index(("dp", "blk")) * row_count
    piece_ids = lax.all_gather(flat_ids, ("dp", "blk"), axis=0, tiled=True)
    piece_grads = lax.all_gather(
        flat_grads.astype(jnp.bfloat16), ("dp", "blk"), axis=0, tiled=True
    ).astype(jnp.float32)
    grad_table = scatter_rows(
        jnp.zeros((row_count, EMB), jnp.float32), piece_ids - own_start, piece_grads
    )
    group_count = lax.axis_size("dp")
    gradients = (
        grad_w_embed,
        grad_w_time,
        grad_gain_attn,
        grad_bias_attn,
        grad_gain_mlp,
        grad_bias_mlp,
        grad_w_qkv,
        grad_w_out,
        grad_w_up,
        grad_w_down,
    )
    grouped = tuple((group_columns(g, group_count) for g in gradients))
    in_group = (
        lax.psum_scatter(
            grouped[0].astype(jnp.bfloat16), "blk", scatter_dimension=2, tiled=True
        ).astype(jnp.float32),
        lax.psum_scatter(
            grouped[1].astype(jnp.bfloat16), "blk", scatter_dimension=2, tiled=True
        ).astype(jnp.float32),
        lax.psum_scatter(
            grouped[2].astype(jnp.bfloat16), "blk", scatter_dimension=2, tiled=True
        ).astype(jnp.float32),
        lax.psum_scatter(
            grouped[3].astype(jnp.bfloat16), "blk", scatter_dimension=2, tiled=True
        ).astype(jnp.float32),
        lax.psum_scatter(
            grouped[4].astype(jnp.bfloat16), "blk", scatter_dimension=2, tiled=True
        ).astype(jnp.float32),
        lax.psum_scatter(
            grouped[5].astype(jnp.bfloat16), "blk", scatter_dimension=2, tiled=True
        ).astype(jnp.float32),
        lax.psum_scatter(
            grouped[6].astype(jnp.bfloat16), "blk", scatter_dimension=2, tiled=True
        ).astype(jnp.float32),
        lax.psum_scatter(
            grouped[7].astype(jnp.bfloat16), "blk", scatter_dimension=2, tiled=True
        ).astype(jnp.float32),
        lax.psum_scatter(
            grouped[8].astype(jnp.bfloat16), "blk", scatter_dimension=2, tiled=True
        ).astype(jnp.float32),
        lax.psum_scatter(
            grouped[9].astype(jnp.bfloat16), "blk", scatter_dimension=2, tiled=True
        ).astype(jnp.float32),
    )
    across = (
        lax.psum_scatter(
            in_group[0].astype(jnp.bfloat16), "dp", scatter_dimension=1, tiled=True
        ).astype(jnp.float32),
        lax.psum_scatter(
            in_group[1].astype(jnp.bfloat16), "dp", scatter_dimension=1, tiled=True
        ).astype(jnp.float32),
        lax.psum_scatter(
            in_group[2].astype(jnp.bfloat16), "dp", scatter_dimension=1, tiled=True
        ).astype(jnp.float32),
        lax.psum_scatter(
            in_group[3].astype(jnp.bfloat16), "dp", scatter_dimension=1, tiled=True
        ).astype(jnp.float32),
        lax.psum_scatter(
            in_group[4].astype(jnp.bfloat16), "dp", scatter_dimension=1, tiled=True
        ).astype(jnp.float32),
        lax.psum_scatter(
            in_group[5].astype(jnp.bfloat16), "dp", scatter_dimension=1, tiled=True
        ).astype(jnp.float32),
        lax.psum_scatter(
            in_group[6].astype(jnp.bfloat16), "dp", scatter_dimension=1, tiled=True
        ).astype(jnp.float32),
        lax.psum_scatter(
            in_group[7].astype(jnp.bfloat16), "dp", scatter_dimension=1, tiled=True
        ).astype(jnp.float32),
        lax.psum_scatter(
            in_group[8].astype(jnp.bfloat16), "dp", scatter_dimension=1, tiled=True
        ).astype(jnp.float32),
        lax.psum_scatter(
            in_group[9].astype(jnp.bfloat16), "dp", scatter_dimension=1, tiled=True
        ).astype(jnp.float32),
    )
    summed = tuple(
        (
            a.reshape(g.shape[:-1] + (a.shape[-1],)) if g.ndim == 2 else a.reshape(a.shape[-1])
            for a, g in zip(across, gradients)
        )
    )
    return (
        layer_out,
        grad_input,
        grad_table,
        summed[0],
        summed[1],
        summed[2],
        summed[3],
        summed[4],
        summed[5],
        summed[6],
        summed[7],
        summed[8],
        summed[9],
    )


BF16 = jnp.bfloat16
F32 = jnp.float32
LOG2_E = 1.4426950408889634
VMEM_BYTES = 58 * 1024 * 1024
META_ROWS = 4
SLOT_ROWS = 72
EXACT_BASE = 256
TOKEN_TILE = 256
ANY_SPEC = pl.BlockSpec(memory_space=pl.ANY)


def dot_nn(left, right):
    return lax.dot_general(left, right, (((1,), (0,)), ((), ())), preferred_element_type=F32)


def dot_nt(left, right):
    return lax.dot_general(left, right, (((1,), (1,)), ((), ())), preferred_element_type=F32)


def dot_tn(left, right):
    return lax.dot_general(left, right, (((0,), (0,)), ((), ())), preferred_element_type=F32)


def head_operands(queries, keys, head, length):
    lane = lax.broadcasted_iota(jnp.int32, queries.shape, 1)
    row = lax.broadcasted_iota(jnp.int32, queries.shape, 0)
    mine = (lane // HEAD_DIM) == head
    spare = lane == (1 - head) * HEAD_DIM
    zero = jnp.zeros_like(queries)
    fill = jnp.where(row >= length, jnp.full_like(queries, NEG_FILL), zero)
    one_query = jnp.where(mine, queries, jnp.where(spare, jnp.ones_like(queries), zero))
    one_key = jnp.where(mine, keys, jnp.where(spare, fill, zero))
    return mine, one_query, one_key


def attend_kernel(length_ref, q_ref, k_ref, v_ref, out_ref, lse_ref):
    length = length_ref[0]
    factor = LOG2_E * HEAD_DIM**-0.5
    rows = []
    for head in range(2):
        mine, one_query, one_key = head_operands(q_ref[...], k_ref[...], head, length)
        value_one = jnp.where(mine, v_ref[...], jnp.ones_like(v_ref[...]))
        scores = dot_nt(one_key, one_query)
        top = jnp.max(scores, axis=0, keepdims=True)
        weights = jnp.exp2(scores * factor - top * factor).astype(BF16)
        mixed = dot_tn(value_one, weights)
        other = (1 - head) * HEAD_DIM
        total = mixed[other : other + 1]
        lse_ref[0, head : head + 1, :] = top * factor + jnp.log2(total)
        rows.append(mixed[head * HEAD_DIM : (head + 1) * HEAD_DIM] * (1.0 / total))
    out_ref[...] = jnp.transpose(jnp.concatenate(rows, axis=0), (1, 0)).astype(BF16)


def attend_back_kernel(
    length_ref, q_ref, k_ref, v_ref, out_ref, grad_ref, lse_ref, dq_ref, dk_ref, dv_ref, *, chunk
):
    length = length_ref[0]
    positions = q_ref.shape[0]
    factor = LOG2_E * HEAD_DIM**-0.5
    scale = HEAD_DIM**-0.5
    grad = grad_ref[...]
    product = grad.astype(F32) * out_ref[...].astype(F32)
    high = product.astype(BF16)
    low = (product - high.astype(F32)).astype(BF16)
    head_of_lane = lax.broadcasted_iota(jnp.int32, (16, 2 * HEAD_DIM), 1) // HEAD_DIM
    picker = jnp.where(
        head_of_lane == lax.broadcasted_iota(jnp.int32, (16, 2 * HEAD_DIM), 0), 1.0, 0.0
    ).astype(BF16)
    delta = dot_nt(picker, high) + dot_nt(picker, low)
    query_rows = []
    key_parts = ([], [])
    value_parts = ([], [])
    for head in range(2):
        mine, one_query, one_key = head_operands(q_ref[...], k_ref[...], head, length)
        one_value = jnp.where(mine, v_ref[...], jnp.zeros_like(v_ref[...]))
        lse = lse_ref[0, head : head + 1, :]
        row_delta = delta[head : head + 1, :]
        query_grad = jnp.zeros((2 * HEAD_DIM, positions), F32)
        for start in range(0, positions, chunk):
            span = slice(start, start + chunk)
            weights = jnp.exp2(dot_nt(one_key[span], one_query) * factor - lse)
            weight_grad = dot_nt(one_value[span], grad)
            score_grad = (weights * (weight_grad - row_delta)).astype(BF16)
            value_parts[head].append(dot_nn(weights.astype(BF16), grad))
            key_parts[head].append(dot_nn(score_grad, q_ref[...]))
            query_grad = query_grad + dot_tn(k_ref[span, :], score_grad)
        query_rows.append(query_grad[head * HEAD_DIM : (head + 1) * HEAD_DIM])
    first = lax.broadcasted_iota(jnp.int32, (chunk, 2 * HEAD_DIM), 1) < HEAD_DIM
    for part, start in enumerate(range(0, positions, chunk)):
        span = slice(start, start + chunk)
        dk_ref[span, :] = (jnp.where(first, key_parts[0][part], key_parts[1][part]) * scale).astype(BF16)
        dv_ref[span, :] = jnp.where(first, value_parts[0][part], value_parts[1][part]).astype(BF16)
    dq_ref[...] = jnp.transpose(jnp.concatenate(query_rows, axis=0) * scale, (1, 0)).astype(BF16)


def gelu_with_slope(values):
    root = math.sqrt(2.0 / math.pi)
    square = values * values
    bend = jnp.tanh(root * values * (1.0 + 0.044715 * square))
    half = 0.5 * (1.0 + bend)
    slope = half + 0.5 * values * (1.0 - bend * bend) * (root * (1.0 + 3.0 * 0.044715 * square))
    return values * half, slope


def swap_core(value):
    return lax.ppermute(value, "blk", [(0, 1), (1, 0)])


def join_halves(core, own, other):
    first = jnp.where(core == 0, own, other)
    second = jnp.where(core == 0, other, own)
    return jnp.concatenate([first, second], axis=0)


def to_whole(core, local):
    own = lax.dynamic_index_in_dim(local, core, 0, keepdims=False)
    away = lax.dynamic_index_in_dim(local, 1 - core, 0, keepdims=False)
    return join_halves(core, own, swap_core(away))


def to_split(core, whole):
    half = whole.shape[0] // 2
    halves = whole.reshape((2, half) + whole.shape[1:])
    own = lax.dynamic_index_in_dim(halves, core, 0, keepdims=False)
    away = swap_core(lax.dynamic_index_in_dim(halves, 1 - core, 0, keepdims=False))
    return jnp.stack([jnp.where(core == 0, own, away), jnp.where(core == 0, away, own)])


COST_SHARE = 0.3


def kernel_cost(microseconds):
    flops = int(COST_SHARE * microseconds * 1e9)
    return pl.CostEstimate(flops=flops, bytes_accessed=1024, transcendentals=0)


def run_kernel(
    body, grid, scalars, inputs, in_specs, out_specs, out_shape, microseconds, name, scratch=(), carried=()
):
    scalar_count, input_count, output_count = len(scalars), len(inputs), len(out_shape)
    carried_count = len(carried)
    first_carried = scalar_count + input_count

    def kernel(*refs):
        rest = refs[first_carried + carried_count :]
        body(*refs[:first_carried], *rest[:output_count], *rest[output_count + carried_count :])

    results = pl.pallas_call(
        kernel,
        grid_spec=pltpu.PrefetchScalarGridSpec(
            num_scalar_prefetch=scalar_count,
            grid=grid,
            in_specs=list(in_specs) + [ANY_SPEC] * carried_count,
            out_specs=list(out_specs) + [ANY_SPEC] * carried_count,
            scratch_shapes=list(scratch),
        ),
        out_shape=list(out_shape) + [jax.ShapeDtypeStruct(c.shape, c.dtype) for c in carried],
        input_output_aliases={first_carried + i: output_count + i for i in range(carried_count)},
        compiler_params=pltpu.CompilerParams(vmem_limit_bytes=VMEM_BYTES),
        cost_estimate=kernel_cost(microseconds),
        name=name,
    )(*scalars, *inputs, *carried)
    return results[:output_count], results[output_count:]


def behind(*arrays):
    def kernel(*refs):
        pass

    return pl.pallas_call(
        kernel,
        in_specs=[ANY_SPEC] * len(arrays),
        out_specs=[ANY_SPEC] * len(arrays),
        out_shape=[jax.ShapeDtypeStruct(a.shape, a.dtype) for a in arrays],
        input_output_aliases={i: i for i in range(len(arrays))},
        compiler_params=pltpu.CompilerParams(vmem_limit_bytes=VMEM_BYTES),
        cost_estimate=kernel_cost(1),
        name="behind",
    )(*arrays)


def shaped(dtype, *shape):
    return jax.ShapeDtypeStruct(shape, dtype)


def row_spec(tile, columns):
    return pl.BlockSpec((tile, columns), lambda i, *scalars: (i, 0))


def fixed_spec(*shape):
    return pl.BlockSpec(shape, lambda *grid: (0,) * len(shape))


def attend(length, qkv):
    positions = qkv.shape[0]
    pairs = HEADS // 2

    def spec(group):
        return pl.BlockSpec((positions, 2 * HEAD_DIM), lambda pair, length: (0, group * pairs + pair))

    results, _ = run_kernel(
        attend_kernel,
        (pairs,),
        [length],
        [qkv, qkv, qkv],
        [spec(0), spec(1), spec(2)],
        [spec(0), pl.BlockSpec((1, 2, positions), lambda pair, length: (pair, 0, 0))],
        [shaped(BF16, positions, D), shaped(F32, pairs, 2, positions)],
        30,
        "attend",
    )
    return results


def attend_back(length, qkv, attended, grad_att, lse, part, parts, grads, carried):
    positions = qkv.shape[0]
    pairs = HEADS // 2
    count = pairs // parts
    shift = part * count

    def spec(group):
        return pl.BlockSpec(
            (positions, 2 * HEAD_DIM), lambda pair, length: (0, group * pairs + shift + pair)
        )

    lse_spec = pl.BlockSpec((1, 2, positions), lambda pair, length: (shift + pair, 0, 0))
    inputs = [qkv, qkv, qkv, attended, grad_att, lse]
    held = len(grads)
    kept = len(carried)

    def kernel(*refs):
        attend_back_kernel(*refs[:7], *refs[7 + held + kept : 10 + held + kept], chunk=min(512, positions))

    aliases = {7 + i: i for i in range(held)}
    aliases.update({7 + held + i: 3 + i for i in range(kept)})
    results = pl.pallas_call(
        kernel,
        grid_spec=pltpu.PrefetchScalarGridSpec(
            num_scalar_prefetch=1,
            grid=(count,),
            in_specs=[spec(0), spec(1), spec(2), spec(0), spec(0), lse_spec] + [ANY_SPEC] * (held + kept),
            out_specs=[spec(0)] * 3 + [ANY_SPEC] * kept,
        ),
        out_shape=[shaped(BF16, positions, D)] * 3 + [jax.ShapeDtypeStruct(c.shape, c.dtype) for c in carried],
        input_output_aliases=aliases,
        compiler_params=pltpu.CompilerParams(vmem_limit_bytes=VMEM_BYTES),
        cost_estimate=kernel_cost(46 / parts),
        name="attend_back",
    )(length, *inputs, *grads, *carried)
    return results[:3], results[3:]


def norm_rows(features):
    center = features - jnp.mean(features, axis=-1, keepdims=True)
    rstd = lax.rsqrt(jnp.mean(center * center, axis=-1, keepdims=True) + 1e-05)
    return center * rstd, rstd


def norm_rows_back(grad_norm, xhat, rstd, gain_row):
    scaled = grad_norm * gain_row
    mean_scaled = jnp.mean(scaled, axis=-1, keepdims=True)
    mean_cross = jnp.mean(scaled * xhat, axis=-1, keepdims=True)
    return rstd * (scaled - mean_scaled - xhat * mean_cross)


def add_column_sums(sums_ref, grad_norm, xhat):
    sums_ref[0:1, :] += jnp.sum(grad_norm * xhat, axis=0, keepdims=True)
    sums_ref[1:2, :] += jnp.sum(grad_norm, axis=0, keepdims=True)


def valid_column(length, tile):
    row = lax.broadcasted_iota(jnp.int32, (tile, 1), 0) + pl.program_id(0) * tile
    return row < length


def share_out(core, value, keep_ref, away_ref):
    rows = keep_ref.shape[-2]
    if len(keep_ref.shape) == 4:
        outer, inner = keep_ref.shape[:2]
        value = value.astype(BF16).reshape(outer, inner, 2, rows, value.shape[1])
        first, second = value[:, :, 0], value[:, :, 1]
        keep_ref[...] = jnp.where(core == 0, first, second)
        away_ref[...] = jnp.where(core == 0, second, first)
        return
    groups = keep_ref.shape[0]
    value = value.astype(BF16).reshape(groups, 2, rows, value.shape[1])
    first, second = value[:, 0], value[:, 1]
    keep_ref[...] = jnp.where(core == 0, first, second)
    away_ref[...] = jnp.where(core == 0, second, first)


def embed_kernel(emb_ref, we_ref, gain_ref, shift_ref, wqkv_ref, low_ref, in_ref, attn_ref, qkv_ref):
    rows = emb_ref[...].astype(F32)
    normed = rows * lax.rsqrt(jnp.mean(rows * rows, axis=-1, keepdims=True) + 1e-06)
    low = normed.astype(BF16)
    low_ref[...] = low
    inputs = dot_nn(low, we_ref[...])
    in_ref[...] = inputs
    xhat, _ = norm_rows(inputs)
    attn = (xhat * gain_ref[...] + shift_ref[...]).astype(BF16)
    attn_ref[...] = attn
    qkv_ref[...] = dot_nn(attn, wqkv_ref[...]).astype(BF16)


def embed_and_project(emb, w_embed, gain_row, shift_row, w_qkv):
    count = emb.shape[0]
    tile = TOKEN_TILE
    results, _ = run_kernel(
        embed_kernel,
        (count // tile,),
        [],
        [emb, w_embed, gain_row, shift_row, w_qkv],
        [row_spec(tile, EMB), fixed_spec(EMB, D), fixed_spec(1, D), fixed_spec(1, D), fixed_spec(D, 3 * D)],
        [row_spec(tile, EMB), row_spec(tile, D), row_spec(tile, D), row_spec(tile, 3 * D)],
        [shaped(BF16, count, EMB), shaped(F32, count, D), shaped(BF16, count, D), shaped(BF16, count, 3 * D)],
        12,
        "embed_and_project",
    )
    return results


def residual_kernel(length_ref, att_ref, in_ref, wo_ref, gain_ref, shift_ref, cot_ref, res_ref, mlp_ref, fin_ref):
    residual = in_ref[...] + dot_nn(att_ref[...], wo_ref[...])
    res_ref[...] = residual
    xhat, _ = norm_rows(residual)
    mlp_ref[...] = (xhat * gain_ref[...] + shift_ref[...]).astype(BF16)
    cot = cot_ref[...]
    fin_ref[...] = jnp.where(valid_column(length_ref[0], cot.shape[0]), cot, jnp.zeros_like(cot))


def attention_residual(length, attended, inputs, w_out, gain_row, shift_row, cot):
    count = attended.shape[0]
    row = row_spec(TOKEN_TILE, D)
    results, _ = run_kernel(
        residual_kernel,
        (count // TOKEN_TILE,),
        [length],
        [attended, inputs, w_out, gain_row, shift_row, cot],
        [row, row, fixed_spec(D, D), fixed_spec(1, D), fixed_spec(1, D), row],
        [row, row, row],
        [shaped(F32, count, D), shaped(BF16, count, D), shaped(BF16, count, D)],
        8,
        "attention_residual",
    )
    return results


def feed_forward_kernel(
    core_ref, mlp_ref, fin_ref, wu_ref, wd_ref, down_in_ref, grad_in_ref,
    gwd_keep_ref, gwd_away_ref, gwu_keep_ref, gwu_away_ref, down_ref, grad_ref,
    fin_t_ref, hid_ref, pre_ref, *, first
):
    core = core_ref[0]
    count = mlp_ref.shape[0]

    @pl.when(pl.program_id(0) == 0)
    def _():
        fin_t_ref[...] = jnp.transpose(fin_ref[...], (1, 0))
        if first:
            down_ref[...] = jnp.zeros_like(down_ref)
            grad_ref[...] = jnp.zeros_like(grad_ref)
        else:
            down_ref[...] = down_in_ref[...]
            grad_ref[...] = grad_in_ref[...]

    for start in range(0, count, TOKEN_TILE):
        span = slice(start, start + TOKEN_TILE)
        hidden, slope = gelu_with_slope(dot_nn(mlp_ref[span, :], wu_ref[...]))
        hid_ref[span, :] = hidden.astype(BF16)
        pre_ref[span, :] = (dot_nt(fin_ref[span, :], wd_ref[...]) * slope).astype(BF16)
    share_out(core, dot_nn(fin_t_ref[...], hid_ref[...]), gwd_keep_ref, gwd_away_ref)
    share_out(core, dot_tn(pre_ref[...], mlp_ref[...]), gwu_keep_ref, gwu_away_ref)
    for start in range(0, count, TOKEN_TILE):
        span = slice(start, start + TOKEN_TILE)
        down_ref[span, :] += dot_nn(hid_ref[span, :], wd_ref[...])
        grad_ref[span, :] += dot_nt(pre_ref[span, :], wu_ref[...])


def feed_forward(core, groups, part, parts, mlp_low, final_low, w_up, w_down, down, grad, carried, tile=512):
    count = mlp_low.shape[0]
    width = w_up.shape[1] // parts
    steps = width // tile
    shift = part * steps
    first = down is None
    if first:
        down = grad = jnp.zeros((8, 128), F32)
    down_rows = D // (2 * groups)
    up_rows = w_up.shape[1] // (2 * groups)
    down_share = (groups // 4, 4, down_rows)
    down_spec = pl.BlockSpec((*down_share, tile), lambda j, core: (0, 0, 0, j))
    up_spec = pl.BlockSpec((tile // (2 * up_rows), up_rows, D), lambda j, core: (j, 0, 0))
    whole = fixed_spec(count, D)
    return run_kernel(
        functools.partial(feed_forward_kernel, first=first),
        (steps,),
        [core],
        [mlp_low, final_low, w_up, w_down, down, grad],
        [
            whole,
            whole,
            pl.BlockSpec((D, tile), lambda j, core: (0, shift + j)),
            pl.BlockSpec((tile, D), lambda j, core: (shift + j, 0)),
            fixed_spec(*down.shape),
            fixed_spec(*down.shape),
        ],
        [down_spec, down_spec, up_spec, up_spec, whole, whole],
        [shaped(BF16, *down_share, width)] * 2
        + [shaped(BF16, groups // parts, up_rows, D)] * 2
        + [shaped(F32, count, D)] * 2,
        36,
        "feed_forward",
        scratch=[pltpu.VMEM((D, count), BF16), pltpu.VMEM((count, tile), BF16), pltpu.VMEM((count, tile), BF16)],
        carried=carried,
    )


def middle_kernel(
    length_ref, core_ref, down_ref, gmn_ref, res_ref, fin_ref, gain_ref, wo_ref, att_ref,
    out_ref, low_ref, gatt_ref, gwo_keep_ref, gwo_away_ref, sums_ref, acc_ref
):
    step = pl.program_id(0)

    @pl.when(step == 0)
    def _():
        sums_ref[...] = jnp.zeros_like(sums_ref)
        acc_ref[...] = jnp.zeros_like(acc_ref)

    residual = res_ref[...]
    keep = valid_column(length_ref[0], residual.shape[0])
    out_ref[...] = jnp.where(keep, residual + down_ref[...], 0.0).astype(BF16)
    xhat, rstd = norm_rows(residual)
    grad = gmn_ref[...]
    add_column_sums(sums_ref, grad, xhat)
    low = (fin_ref[...].astype(F32) + norm_rows_back(grad, xhat, rstd, gain_ref[...])).astype(BF16)
    low_ref[...] = low
    gatt_ref[...] = dot_nt(low, wo_ref[...]).astype(BF16)
    acc_ref[...] += dot_tn(low, att_ref[...])

    @pl.when(step == pl.num_programs(0) - 1)
    def _():
        share_out(core_ref[0], acc_ref[...], gwo_keep_ref, gwo_away_ref)


def feed_forward_to_attention(
    length, core, groups, down, grad_mlp_norm, residual, final_low, gain_row, w_out, attended, carried
):
    count = residual.shape[0]
    row = row_spec(TOKEN_TILE, D)
    share = (groups // 4, 4, D // (2 * groups), D)
    return run_kernel(
        middle_kernel,
        (count // TOKEN_TILE,),
        [length, core],
        [down, grad_mlp_norm, residual, final_low, gain_row, w_out, attended],
        [row, row, row, row, fixed_spec(1, D), fixed_spec(D, D), row],
        [row, row, row, fixed_spec(*share), fixed_spec(*share), fixed_spec(8, D)],
        [shaped(BF16, count, D)] * 3 + [shaped(BF16, *share)] * 2 + [shaped(F32, 8, D)],
        15,
        "feed_forward_to_attention",
        scratch=[pltpu.VMEM((D, D), F32)],
        carried=carried,
    )


def outer_kernel(core_ref, dq_ref, dk_ref, dv_ref, right_ref, keep_ref, away_ref, all_ref):
    right = right_ref[...]
    for group, ref in enumerate((dq_ref, dk_ref, dv_ref)):
        for start in range(0, D, TOKEN_TILE):
            rows = slice(group * D + start, group * D + start + TOKEN_TILE)
            all_ref[rows, :] = dot_tn(ref[:, start : start + TOKEN_TILE], right).astype(BF16)
    share_out(core_ref[0], all_ref[...], keep_ref, away_ref)


def outer_qkv(core, groups, grads, right, half, carried):
    count = right.shape[0]
    columns = right.shape[1] // 2
    share = (groups, 3 * D // (2 * groups), columns)
    return run_kernel(
        outer_kernel,
        (1,),
        [core],
        [*grads, right],
        [fixed_spec(count, D)] * 3 + [pl.BlockSpec((count, columns), lambda i, core: (0, half))],
        [fixed_spec(*share)] * 2,
        [shaped(BF16, *share)] * 2,
        8,
        "outer_qkv",
        scratch=[pltpu.VMEM((3 * D, columns), BF16)],
        carried=carried,
    )


def input_kernel(
    core_ref, dq_ref, dk_ref, dv_ref, wqkv_ref, in_ref, low_ref, gain_ref, we_ref, emb_ref, nl_ref,
    grad_ref, rows_ref, gwe_keep_ref, gwe_away_ref, sums_ref, acc_ref
):
    step = pl.program_id(0)

    @pl.when(step == 0)
    def _():
        sums_ref[...] = jnp.zeros_like(sums_ref)
        acc_ref[...] = jnp.zeros_like(acc_ref)

    grad = (
        dot_nt(dq_ref[...], wqkv_ref[:, :D])
        + dot_nt(dk_ref[...], wqkv_ref[:, D : 2 * D])
        + dot_nt(dv_ref[...], wqkv_ref[:, 2 * D :])
    )
    xhat, rstd = norm_rows(in_ref[...])
    add_column_sums(sums_ref, grad, xhat)
    low = (low_ref[...].astype(F32) + norm_rows_back(grad, xhat, rstd, gain_ref[...])).astype(BF16)
    grad_ref[...] = low
    acc_ref[...] += dot_tn(low, nl_ref[...])
    back = dot_nt(low, we_ref[...])
    emb = emb_ref[...].astype(F32)
    emb_rstd = lax.rsqrt(jnp.mean(emb * emb, axis=-1, keepdims=True) + 1e-06)
    normed = emb * emb_rstd
    rows_ref[...] = (emb_rstd * (back - normed * jnp.mean(normed * back, axis=-1, keepdims=True))).astype(BF16)

    @pl.when(step == pl.num_programs(0) - 1)
    def _():
        share_out(core_ref[0], acc_ref[...], gwe_keep_ref, gwe_away_ref)


def input_gradient(core, groups, grads, w_qkv, inputs, residual_low, gain_row, w_embed, emb, normed_low, carried):
    count = inputs.shape[0]
    tile = TOKEN_TILE
    share = (2 * groups, D // (4 * groups), EMB)
    row, narrow = row_spec(tile, D), row_spec(tile, EMB)
    return run_kernel(
        input_kernel,
        (count // tile,),
        [core],
        [*grads, w_qkv, inputs, residual_low, gain_row, w_embed, emb, normed_low],
        [row, row, row, fixed_spec(D, 3 * D), row, row, fixed_spec(1, D), fixed_spec(EMB, D), narrow, narrow],
        [row, narrow, fixed_spec(*share), fixed_spec(*share), fixed_spec(8, D)],
        [shaped(BF16, count, D), shaped(BF16, count, EMB)] + [shaped(BF16, *share)] * 2 + [shaped(F32, 8, D)],
        16,
        "input_gradient",
        scratch=[pltpu.VMEM((D, EMB), F32)],
        carried=carried,
    )


def exchange(value, bit, dp_bits, pattern=1):
    return lax.ppermute(value, "dp", [(i, i ^ (pattern << bit)) for i in range(1 << dp_bits)])


class Halving:
    def __init__(self, labels, dp_bits):
        self.labels = list(labels)
        self.dp_bits = dp_bits
        self.keep = self.arrived = None

    def over_cores(self, keep, away):
        shape = (2,) * len(self.labels) + keep.shape[1:]
        self.keep, self.arrived = keep.reshape(shape), swap_core(away).reshape(shape)

    def total(self):
        return self.arrived.astype(F32) + self.keep.astype(F32)

    def halves(self, bit_label):
        place = self.labels.index(bit_label)
        bit = (lax.axis_index("dp") >> bit_label) & 1
        self.labels.pop(place)

        def half(which):
            parts = (self.arrived, self.keep)
            first, second = (lax.dynamic_index_in_dim(p, which, place, keepdims=False) for p in parts)
            return (first.astype(F32) + second.astype(F32)).astype(BF16)

        return half(bit), half(1 - bit)

    def send(self, bit_label, keep, away):
        self.keep, self.arrived = keep, exchange(away, bit_label, self.dp_bits)

    def step(self, bit_label):
        self.send(bit_label, *self.halves(bit_label))


def whole_sequence_shards(
    token_ids,
    seq_lengths,
    diffusion_time,
    embed_table,
    w_embed,
    w_time,
    gain_attn,
    bias_attn,
    gain_mlp,
    bias_mlp,
    w_qkv,
    w_out,
    w_up,
    w_down,
    cotangent,
):
    core = lax.axis_index("blk")
    cores = core.reshape(1).astype(jnp.int32)
    groups = lax.axis_size("dp")
    devices = 2 * groups
    dp_bits = groups.bit_length() - 1
    everywhere = ("dp", "blk")
    labels = list(reversed(range(dp_bits)))
    planes = [[4 * high + low for low in range(4)] for high in range(groups // 4)]
    lines = [[4 * high + low for high in range(groups // 4)] for low in range(4)]
    ids = to_whole(core, token_ids)
    cot = to_whole(core, cotangent)
    positions = ids.shape[0]
    length = lax.dynamic_index_in_dim(seq_lengths, core, 0, keepdims=True)
    time = lax.dynamic_index_in_dim(diffusion_time, core, 0, keepdims=True)
    emb = embed_table[ids]

    valid = jnp.arange(positions, dtype=jnp.int32) < length[0]
    row_count = VOCAB // devices
    owner = jnp.where(valid, ids // row_count, -1)
    offset = ids % row_count
    slots = SLOT_ROWS - META_ROWS
    member = owner[:, None] == jnp.arange(devices, dtype=jnp.int32)[None, :]
    earlier = jnp.arange(positions)[:, None] > jnp.arange(positions)[None, :]
    before = dot_nn(earlier.astype(BF16), member.astype(BF16))
    rank = jnp.sum(jnp.where(member, before, 0.0), axis=1).astype(jnp.int32)
    most = jnp.max(jnp.sum(member.astype(jnp.int32), axis=0))
    offset_digits = jnp.stack(
        [(offset // EXACT_BASE).astype(BF16), (offset % EXACT_BASE).astype(BF16), jnp.ones(positions, BF16)],
        axis=1,
    )

    def dispatch(turn):
        slot = rank - turn * slots
        inside = (owner >= 0) & (slot >= 0) & (slot < slots)
        target = jnp.where(inside, owner * SLOT_ROWS + META_ROWS + slot, -1)
        place = jnp.arange(devices * SLOT_ROWS, dtype=jnp.int32)[:, None] == target[None, :]
        digits = dot_nn(place.astype(BF16), offset_digits).reshape(devices, SLOT_ROWS, 3)
        head = jnp.transpose(digits, (0, 2, 1)).reshape(devices, 1, 3 * SLOT_ROWS)
        peak = jnp.stack([most // EXACT_BASE, most % EXACT_BASE]).astype(F32)
        peak = jnp.broadcast_to(peak, (devices, 1, 2))
        gap = jnp.zeros((devices, 1, EMB - 3 * SLOT_ROWS - 2), F32)
        return target, jnp.concatenate([head, peak, gap], axis=2)

    meta_target = jnp.arange(devices * META_ROWS, dtype=jnp.int32)
    meta_target = meta_target // META_ROWS * SLOT_ROWS + meta_target % META_ROWS

    def packed(target, meta, grads):
        meta = meta.astype(BF16).reshape(devices * META_ROWS, EMB)
        target = jnp.concatenate([target, meta_target])
        place = jnp.arange(devices * SLOT_ROWS, dtype=jnp.int32)[:, None] == target[None, :]
        rows = dot_nn(place.astype(BF16), jnp.concatenate([grads, meta]))
        return rows.astype(BF16).reshape(devices, SLOT_ROWS, EMB)

    def deliver(rows):
        return lax.all_to_all(rows, everywhere, 0, 0, tiled=True)

    def collect(rows):
        head = rows[:, 0].astype(F32)
        high, low, used = (head[:, i * SLOT_ROWS : (i + 1) * SLOT_ROWS] for i in range(3))
        row = jnp.where(used > 0.5, high * EXACT_BASE + low, -1.0).astype(jnp.int32)
        hit = jnp.arange(row_count, dtype=jnp.int32)[:, None] == row.reshape(1, -1)
        return dot_nn(hit.astype(BF16), rows.reshape(-1, EMB))

    first_target, first_head = dispatch(0)

    def over_cores(keep, arrived):
        return (keep.astype(F32) + arrived.astype(F32)).astype(BF16)

    def scattered(value, index_groups):
        return lax.psum_scatter(value, "dp", scatter_dimension=0, axis_index_groups=index_groups, tiled=True)[0]

    time_low = time_features(time, TIME_WIDTH).astype(BF16)
    modulation = dot_nn(time_low, w_time)
    scale_attn, shift_attn, scale_mlp, shift_mlp = jnp.split(modulation, 4, axis=1)
    gain_row_attn = gain_attn + scale_attn
    gain_row_mlp = gain_mlp + scale_mlp
    normed_low, inputs, attn_low, qkv = embed_and_project(
        emb, w_embed, gain_row_attn, bias_attn + shift_attn, w_qkv
    )
    attended, lse = attend(length, qkv)
    residual, mlp_low, final_low = attention_residual(
        length, attended, inputs, w_out, gain_row_mlp, bias_mlp + shift_mlp, cot
    )

    top = dp_bits - 1
    hidden_width = w_up.shape[1]
    feed = functools.partial(feed_forward, cores, groups)
    (keep_d, away_d, keep_u, away_u, down, grad), _ = feed(
        0, 2, mlp_low, final_low, w_up, w_down, None, None, []
    )
    up_0, up_1 = Halving(labels[1:], dp_bits), Halving(labels[1:], dp_bits)
    qkv_a, qkv_b = Halving(labels, dp_bits), Halving(labels, dp_bits)
    up_0.over_cores(keep_u, away_u)
    arrived_d = swap_core(away_d)
    (next_keep, next_away, keep_u, away_u, down, grad), (up_0.keep, keep_d) = feed(
        1, 2, mlp_low, final_low, w_up, w_down, down, grad, [up_0.keep, keep_d]
    )
    keep, away, down_0, next_keep, next_away, keep_u, away_u = behind(
        *up_0.halves(0), over_cores(keep_d, arrived_d), next_keep, next_away, keep_u, away_u
    )
    up_0.send(0, keep, away)
    up_1.over_cores(keep_u, away_u)
    arrived_d = swap_core(next_away)
    down_0 = scattered(down_0, lines)
    (layer_out, residual_low, grad_att, keep_o, away_o, sums_mlp), kept = feed_forward_to_attention(
        length, cores, groups, down, grad, residual, final_low, gain_row_mlp, w_out, attended,
        [up_0.keep, up_1.keep, next_keep],
    )
    up_0.keep, up_1.keep, keep_d = kept
    keep_0, away_0, keep_1, away_1, down_1, keep_o, away_o = behind(
        *up_0.halves(1), *up_1.halves(0), over_cores(keep_d, arrived_d), keep_o, away_o
    )
    up_0.send(1, keep_0, away_0)
    up_1.send(0, keep_1, away_1)
    down_1 = scattered(down_1, lines)
    arrived_o = swap_core(away_o)
    back = functools.partial(attend_back, length, qkv, attended, grad_att, lse)
    grads, (up_0.keep, up_1.keep, keep_o, down_0) = back(0, 2, [], [up_0.keep, up_1.keep, keep_o, down_0])
    keep_0, away_0, keep_1, away_1, out_sum = behind(
        *up_0.halves(2), *up_1.halves(1), over_cores(keep_o, arrived_o)
    )
    up_0.send(2, keep_0, away_0)
    up_1.send(1, keep_1, away_1)
    out_sum = scattered(out_sum, lines)
    layer_out = to_split(core, layer_out)
    grads, (up_0.keep, up_1.keep) = back(1, 2, grads, [up_0.keep, up_1.keep])
    for bit in range(3, top):
        up_0.step(bit)
    keep_1, away_1 = behind(*up_1.halves(2))
    up_1.send(2, keep_1, away_1)
    for bit in range(3, top):
        up_1.step(bit)
    (keep_a, away_a), (up_0.keep, up_1.keep, down_1) = outer_qkv(
        cores, groups, grads, attn_low, 0, [up_0.keep, up_1.keep, down_1]
    )
    zero_first, one_first = up_0.total().astype(BF16), up_1.total().astype(BF16)
    top_bit = (lax.axis_index("dp") >> top) & 1
    up_keep, up_away, keep_a, away_a = behind(
        jnp.where(top_bit == 0, zero_first, one_first),
        jnp.where(top_bit == 0, one_first, zero_first),
        keep_a,
        away_a,
    )
    up_away = exchange(up_away, top, dp_bits)
    qkv_a.over_cores(keep_a, away_a)
    orders = [list(range(dp_bits)), [1, 0] + list(range(2, dp_bits))]
    (keep_b, away_b), (qkv_a.keep, up_keep) = outer_qkv(
        cores, groups, grads, attn_low, 1, [qkv_a.keep, up_keep]
    )
    in_plane = jnp.concatenate([down_0, down_1, out_sum], axis=2)
    keep_a, away_a, keep_b, away_b, in_plane = behind(*qkv_a.halves(orders[0][0]), keep_b, away_b, in_plane)
    own_sum = scattered(in_plane, planes)
    qkv_a.send(orders[0][0], keep_a, away_a)
    qkv_b.over_cores(keep_b, away_b)
    grad_w_up = (up_away.astype(F32) + up_keep.astype(F32)).T
    qkv_b.send(orders[1][0], *behind(*qkv_b.halves(orders[1][0])))
    (grad_input, grad_rows, keep_e, away_e, sums_attn), (qkv_a.keep, qkv_b.keep) = input_gradient(
        cores, groups, grads, w_qkv, inputs, residual_low, gain_row_attn, w_embed, emb, normed_low,
        [qkv_a.keep, qkv_b.keep],
    )

    grad_modulation = jnp.concatenate([sums_attn[0], sums_attn[1], sums_mlp[0], sums_mlp[1]])
    gain_columns = jnp.transpose(grad_modulation.reshape(4, devices, -1), (1, 0, 2)).reshape(devices, -1)
    mod_rows = jnp.concatenate([grad_modulation.reshape(devices, -1), gain_columns], axis=1)
    mod_high = mod_rows.astype(BF16).astype(F32)
    mod_low = mod_rows - mod_high
    time_rows = jnp.broadcast_to(time_low.astype(F32), (devices, TIME_WIDTH))
    first_meta = jnp.concatenate(
        [first_head, jnp.stack([mod_high, mod_low, time_rows], axis=1)], axis=1
    )
    embed_rows = over_cores(keep_e, swap_core(away_e))
    payload = jnp.concatenate([packed(first_target, first_meta, grad_rows), embed_rows], axis=1)
    payload, keep_a, away_a, keep_b, away_b = behind(
        payload, *qkv_a.halves(orders[0][1]), *qkv_b.halves(orders[1][1])
    )
    arrived = deliver(payload)
    qkv_a.send(orders[0][1], keep_a, away_a)
    qkv_b.send(orders[1][1], keep_b, away_b)
    grad_w_qkv = jnp.concatenate([qkv_a.total(), qkv_b.total()], axis=-1).astype(BF16)
    grad_w_qkv = grad_w_qkv.reshape(groups // 4, -1, D)
    plane = lax.axis_index("dp") >> 2
    parts = [lax.dynamic_index_in_dim(grad_w_qkv, plane, 0, keepdims=False)]
    for step in range(1, groups // 4):
        away = lax.dynamic_index_in_dim(grad_w_qkv, plane ^ step, 0, keepdims=False)
        parts.append(exchange(away, 2, dp_bits, step))
    grad_w_qkv = sum(part.astype(F32) for part in parts)
    embed_sum = arrived[:, SLOT_ROWS:].astype(F32).reshape(groups, -1, EMB)
    embed_sum = jnp.sum(embed_sum, axis=0)
    arrived = arrived[:, :SLOT_ROWS]
    grad_input = to_split(core, grad_input)
    grad_table = collect(arrived)
    sums = arrived[:, 1].astype(F32) + arrived[:, 2].astype(F32)
    time_width = sums.shape[1] // 2
    grad_w_time = lax.dot_general(
        arrived[:, 3].astype(F32),
        sums[:, :time_width],
        (((0,), (0,)), ((), ())),
        precision=lax.Precision.HIGHEST,
    )
    gain_sums = jnp.sum(sums[:, time_width:], axis=0).reshape(4, -1)
    peaks = arrived[:, 0, 3 * SLOT_ROWS : 3 * SLOT_ROWS + 2].astype(F32)
    peak = jnp.max(peaks[:, 0] * EXACT_BASE + peaks[:, 1]).astype(jnp.int32)
    turns = (peak + slots - 1) // slots

    def more_turns(state):
        return state[0] < turns

    def next_turn(state):
        turn, table = state
        target, head = dispatch(turn)
        meta = jnp.pad(head, ((0, 0), (0, META_ROWS - 1), (0, 0)))
        return turn + 1, table + collect(deliver(packed(target, meta, grad_rows)))

    _, grad_table = lax.while_loop(more_turns, next_turn, (jnp.int32(1), grad_table))
    return (
        layer_out,
        grad_input,
        grad_table,
        embed_sum.T,
        grad_w_time,
        gain_sums[0],
        gain_sums[1],
        gain_sums[2],
        gain_sums[3],
        grad_w_qkv.T,
        own_sum[:, hidden_width:].astype(F32).T,
        grad_w_up,
        own_sum[:, :hidden_width].astype(F32).T,
    )


def shards(*arguments):
    seq_count, pos_count = arguments[0].shape
    groups = lax.axis_size("dp")
    whole = seq_count == 2 and lax.axis_size("blk") == 2
    whole = whole and groups >= 4 and groups & (groups - 1) == 0 and pos_count % 256 == 0
    return whole_sequence_shards(*arguments) if whole else split_position_shards(*arguments)


def solution(mesh):
    return jax.shard_map(
        shards,
        mesh=mesh,
        in_specs=(
            P("dp", "blk"),
            P("dp"),
            P("dp"),
            P(),
            P(),
            P(),
            P(),
            P(),
            P(),
            P(),
            P(),
            P(),
            P(),
            P(),
            P("dp", "blk", None),
        ),
        out_specs=(
            P("dp", "blk", None),
            P("dp", "blk", None),
            P(("dp", "blk"), None),
            P(None, ("dp", "blk")),
            P(None, ("dp", "blk")),
            P(("dp", "blk")),
            P(("dp", "blk")),
            P(("dp", "blk")),
            P(("dp", "blk")),
            P(None, ("dp", "blk")),
            P(None, ("dp", "blk")),
            P(None, ("dp", "blk")),
            P(None, ("dp", "blk")),
        ),
        check_vma=False,
    )
```

```python
import functools
import math

import jax
import jax.numpy as jnp
from jax import lax
from jax.experimental import pallas as pl
from jax.experimental.pallas import tpu as pltpu
from jax.sharding import PartitionSpec as P

D = 1024
HEADS = 16
HEAD_DIM = 64
EMB = 256
VOCAB = 32000
TIME_WIDTH = 256


NEG_FILL = -1000000000.0


def from_behind(value, axis, steps):
    count = lax.axis_size(axis)
    pairs = [(source, (source + steps) % count) for source in range(count)]
    return lax.ppermute(value, axis, pairs)


def time_features(diffusion_time, feature_width):
    half_width = feature_width // 2
    frequency = jnp.exp(-math.log(1000.0) * jnp.arange(half_width, dtype=jnp.float32) / half_width)
    angles = diffusion_time.astype(jnp.float32)[:, None] * frequency[None, :]
    return jnp.concatenate([jnp.sin(angles), jnp.cos(angles)], axis=1)


def modulated_norm(features, gain_vec, bias_vec, scale_rows, shift_rows):
    center = features - jnp.mean(features, axis=-1, keepdims=True)
    spread = jnp.mean(center * center, axis=-1, keepdims=True)
    return center * lax.rsqrt(spread + 1e-05) * (gain_vec + scale_rows[:, None, :]) + (
        bias_vec + shift_rows[:, None, :]
    )


def normalize_rows(row_values):
    return row_values * lax.rsqrt(jnp.mean(row_values * row_values, axis=-1, keepdims=True) + 1e-06)


def project(left_side, right_side):
    return lax.dot_general(
        left_side,
        right_side,
        (((left_side.ndim - 1,), (0,)), ((), ())),
        preferred_element_type=jnp.float32,
    )


def project_back(left_side, right_side):
    return lax.dot_general(
        left_side,
        right_side,
        (((left_side.ndim - 1,), (1,)), ((), ())),
        preferred_element_type=jnp.float32,
    )


def outer_sum(left_side, right_side):
    return lax.dot_general(
        left_side, right_side, (((0, 1), (0, 1)), ((), ())), preferred_element_type=jnp.float32
    )


def scatter_rows(running_total, offsets, grad_values):
    row_span = running_total.shape[0]
    inside = (offsets >= 0) & (offsets < row_span)
    return running_total.at[jnp.where(inside, offsets, row_span)].add(grad_values, mode="drop")


def group_columns(matrix, group_count):
    if matrix.ndim == 1:
        return matrix.reshape(1, group_count, matrix.shape[0] // group_count)
    return matrix.reshape(matrix.shape[0], group_count, matrix.shape[1] // group_count)


def split_position_shards(
    token_ids,
    seq_lengths,
    diffusion_time,
    embed_table,
    w_embed,
    w_time,
    gain_attn,
    bias_attn,
    gain_mlp,
    bias_mlp,
    w_qkv,
    w_out,
    w_up,
    w_down,
    cotangent,
):
    seq_count, pos_count = token_ids.shape
    scale_factor = HEAD_DIM ** (-0.5)
    cycle_size = lax.axis_size("blk")
    cycle_index = lax.axis_index("blk")
    positions = cycle_index * pos_count + jnp.arange(pos_count, dtype=jnp.int32)
    valid_rows = (positions[None, :] < seq_lengths[:, None]).astype(jnp.float32)[:, :, None]
    emb_rows = embed_table[token_ids].astype(jnp.float32)
    normed, norm_pull = jax.vjp(normalize_rows, emb_rows)
    normed_low = normed.astype(jnp.bfloat16)
    inputs = project(normed_low, w_embed)
    time_low = time_features(diffusion_time, TIME_WIDTH).astype(jnp.bfloat16)
    modulation = jnp.dot(time_low, w_time, preferred_element_type=jnp.float32)
    scale_attn, shift_attn, scale_mlp, shift_mlp = jnp.split(modulation, 4, axis=1)
    normed_attn, attn_pull = jax.vjp(
        modulated_norm, inputs, gain_attn, bias_attn, scale_attn, shift_attn
    )
    attn_low = normed_attn.astype(jnp.bfloat16)
    qkv_low = project(attn_low, w_qkv).astype(jnp.bfloat16)
    queries = qkv_low[:, :, :D].reshape(seq_count, pos_count, HEADS, HEAD_DIM)
    kv_local = qkv_low[:, :, D:]

    def masked_scores(key_heads, key_start):
        key_count = key_heads.shape[1]
        key_pos = key_start + jnp.arange(key_count, dtype=jnp.int32)
        key_keep = (key_pos[None, :] < seq_lengths[:, None])[:, None, None, :]
        scores = (
            jnp.einsum("sqhd,skhd->shqk", queries, key_heads, preferred_element_type=jnp.float32)
            * scale_factor
        )
        return jnp.where(key_keep, scores, NEG_FILL)

    key_piece = lax.all_gather(kv_local, "blk", axis=1, tiled=True)
    run_max = jnp.full((seq_count, HEADS, pos_count), -1e30, jnp.float32)
    key_count = key_piece.shape[1]
    key_heads = key_piece[:, :, :D].reshape(seq_count, key_count, HEADS, HEAD_DIM)
    value_heads = key_piece[:, :, D:].reshape(seq_count, key_count, HEADS, HEAD_DIM)
    scores = masked_scores(key_heads, jnp.int32(0))
    new_max = jnp.maximum(run_max, jnp.max(scores, axis=-1))
    softmax_weights = jnp.exp(scores - new_max[..., None])
    run_sum = jnp.sum(softmax_weights, axis=-1)
    contrib = jnp.einsum(
        "shqk,skhd->sqhd",
        softmax_weights.astype(jnp.bfloat16),
        value_heads,
        preferred_element_type=jnp.float32,
    )
    run_acc = contrib
    run_max, run_sum, run_acc = (new_max, run_sum, run_acc)
    log_total = run_max + jnp.log(run_sum)
    attended = run_acc / jnp.transpose(run_sum, (0, 2, 1))[..., None]
    attended_low = attended.reshape(seq_count, pos_count, D).astype(jnp.bfloat16)
    residual = inputs + project(attended_low, w_out)
    normed_mlp, mlp_pull = jax.vjp(
        modulated_norm, residual, gain_mlp, bias_mlp, scale_mlp, shift_mlp
    )
    mlp_low = normed_mlp.astype(jnp.bfloat16)
    pre_act = project(mlp_low, w_up)
    activated, gelu_pull = jax.vjp(jax.nn.gelu, pre_act)
    hidden_low = activated.astype(jnp.bfloat16)
    final_sum = (residual + project(hidden_low, w_down)) * valid_rows
    layer_out = final_sum.astype(jnp.bfloat16)
    grad_final = cotangent.astype(jnp.float32) * valid_rows
    final_low = grad_final.astype(jnp.bfloat16)
    grad_w_down = outer_sum(hidden_low, final_low)
    (grad_pre,) = gelu_pull(project_back(final_low, w_down))
    pre_low = grad_pre.astype(jnp.bfloat16)
    grad_w_up = outer_sum(mlp_low, pre_low)
    grad_res_norm, grad_gain_mlp, grad_bias_mlp, grad_scale_mlp, grad_shift_mlp = mlp_pull(
        project_back(pre_low, w_up)
    )
    residual_grad = grad_final + grad_res_norm
    residual_low = residual_grad.astype(jnp.bfloat16)
    grad_w_out = outer_sum(attended_low, residual_low)
    grad_att = (
        project_back(residual_low, w_out)
        .astype(jnp.bfloat16)
        .reshape(seq_count, pos_count, HEADS, HEAD_DIM)
    )
    row_delta = jnp.transpose(jnp.sum(grad_att * attended, axis=-1), (0, 2, 1))

    def key_block(kv_block, owner_index):
        key_heads = kv_block[:, :, :D].reshape(seq_count, pos_count, HEADS, HEAD_DIM)
        value_heads = kv_block[:, :, D:].reshape(seq_count, pos_count, HEADS, HEAD_DIM)
        scores = masked_scores(key_heads, owner_index * pos_count)
        softmax_weights = jnp.exp(scores - log_total[..., None])
        grad_weights = jnp.einsum(
            "sqhd,skhd->shqk", grad_att, value_heads, preferred_element_type=jnp.float32
        )
        grad_scores = (
            softmax_weights * (grad_weights - row_delta[..., None]) * scale_factor
        ).astype(jnp.bfloat16)
        grad_queries = jnp.einsum(
            "shqk,skhd->sqhd", grad_scores, key_heads, preferred_element_type=jnp.float32
        )
        grad_keys = jnp.einsum(
            "shqk,sqhd->skhd", grad_scores, queries, preferred_element_type=jnp.float32
        )
        grad_values = jnp.einsum(
            "shqk,sqhd->skhd",
            softmax_weights.astype(jnp.bfloat16),
            grad_att,
            preferred_element_type=jnp.float32,
        )
        joined = jnp.concatenate(
            [
                grad_keys.reshape(seq_count, pos_count, D),
                grad_values.reshape(seq_count, pos_count, D),
            ],
            axis=-1,
        )
        return (grad_queries, joined)

    def pass_back(grad_values):
        return from_behind(grad_values.astype(jnp.bfloat16), "blk", 1).astype(grad_values.dtype)

    zero_kv = jnp.zeros((seq_count, pos_count, 2 * D), jnp.float32)
    zero_query = jnp.zeros((seq_count, pos_count, HEADS, HEAD_DIM), jnp.float32)

    def cycle_step(turn_index, cycle_state):
        kv_block, grad_kv, grad_query = cycle_state
        part_query, part_kv = key_block(kv_block, (cycle_index - turn_index) % cycle_size)
        kv_block = from_behind(kv_block, "blk", 1)
        return (kv_block, pass_back(grad_kv + part_kv), grad_query + part_query)

    kv_block, grad_kv, grad_query = lax.fori_loop(
        0, cycle_size - 1, cycle_step, (kv_local, zero_kv, zero_query)
    )
    part_query, part_kv = key_block(kv_block, (cycle_index + 1) % cycle_size)
    grad_kv = pass_back(grad_kv + part_kv)
    grad_query = grad_query + part_query
    grad_qkv = jnp.concatenate(
        [grad_query.reshape(seq_count, pos_count, D), grad_kv], axis=-1
    ).astype(jnp.bfloat16)
    grad_w_qkv = outer_sum(attn_low, grad_qkv)
    grad_in_norm, grad_gain_attn, grad_bias_attn, grad_scale_attn, grad_shift_attn = attn_pull(
        project_back(grad_qkv, w_qkv)
    )
    input_grad = residual_grad + grad_in_norm
    grad_input = input_grad.astype(jnp.bfloat16)
    grad_w_embed = outer_sum(normed_low, grad_input)
    grad_modulation = jnp.concatenate(
        [grad_scale_attn, grad_shift_attn, grad_scale_mlp, grad_shift_mlp], axis=1
    )
    grad_w_time = jnp.dot(
        time_low.astype(jnp.float32).T, grad_modulation, precision=lax.Precision.HIGHEST
    )
    (grad_rows,) = norm_pull(project_back(grad_input, w_embed))
    flat_ids = token_ids.reshape(-1)
    flat_grads = grad_rows.reshape(-1, EMB)
    row_count = VOCAB // lax.axis_size(("dp", "blk"))
    own_start = lax.axis_index(("dp", "blk")) * row_count
    piece_ids = lax.all_gather(flat_ids, ("dp", "blk"), axis=0, tiled=True)
    piece_grads = lax.all_gather(
        flat_grads.astype(jnp.bfloat16), ("dp", "blk"), axis=0, tiled=True
    ).astype(jnp.float32)
    grad_table = scatter_rows(
        jnp.zeros((row_count, EMB), jnp.float32), piece_ids - own_start, piece_grads
    )
    group_count = lax.axis_size("dp")
    gradients = (
        grad_w_embed,
        grad_w_time,
        grad_gain_attn,
        grad_bias_attn,
        grad_gain_mlp,
        grad_bias_mlp,
        grad_w_qkv,
        grad_w_out,
        grad_w_up,
        grad_w_down,
    )
    grouped = tuple((group_columns(g, group_count) for g in gradients))
    in_group = (
        lax.psum_scatter(
            grouped[0].astype(jnp.bfloat16), "blk", scatter_dimension=2, tiled=True
        ).astype(jnp.float32),
        lax.psum_scatter(
            grouped[1].astype(jnp.bfloat16), "blk", scatter_dimension=2, tiled=True
        ).astype(jnp.float32),
        lax.psum_scatter(
            grouped[2].astype(jnp.bfloat16), "blk", scatter_dimension=2, tiled=True
        ).astype(jnp.float32),
        lax.psum_scatter(
            grouped[3].astype(jnp.bfloat16), "blk", scatter_dimension=2, tiled=True
        ).astype(jnp.float32),
        lax.psum_scatter(
            grouped[4].astype(jnp.bfloat16), "blk", scatter_dimension=2, tiled=True
        ).astype(jnp.float32),
        lax.psum_scatter(
            grouped[5].astype(jnp.bfloat16), "blk", scatter_dimension=2, tiled=True
        ).astype(jnp.float32),
        lax.psum_scatter(
            grouped[6].astype(jnp.bfloat16), "blk", scatter_dimension=2, tiled=True
        ).astype(jnp.float32),
        lax.psum_scatter(
            grouped[7].astype(jnp.bfloat16), "blk", scatter_dimension=2, tiled=True
        ).astype(jnp.float32),
        lax.psum_scatter(
            grouped[8].astype(jnp.bfloat16), "blk", scatter_dimension=2, tiled=True
        ).astype(jnp.float32),
        lax.psum_scatter(
            grouped[9].astype(jnp.bfloat16), "blk", scatter_dimension=2, tiled=True
        ).astype(jnp.float32),
    )
    across = (
        lax.psum_scatter(
            in_group[0].astype(jnp.bfloat16), "dp", scatter_dimension=1, tiled=True
        ).astype(jnp.float32),
        lax.psum_scatter(
            in_group[1].astype(jnp.bfloat16), "dp", scatter_dimension=1, tiled=True
        ).astype(jnp.float32),
        lax.psum_scatter(
            in_group[2].astype(jnp.bfloat16), "dp", scatter_dimension=1, tiled=True
        ).astype(jnp.float32),
        lax.psum_scatter(
            in_group[3].astype(jnp.bfloat16), "dp", scatter_dimension=1, tiled=True
        ).astype(jnp.float32),
        lax.psum_scatter(
            in_group[4].astype(jnp.bfloat16), "dp", scatter_dimension=1, tiled=True
        ).astype(jnp.float32),
        lax.psum_scatter(
            in_group[5].astype(jnp.bfloat16), "dp", scatter_dimension=1, tiled=True
        ).astype(jnp.float32),
        lax.psum_scatter(
            in_group[6].astype(jnp.bfloat16), "dp", scatter_dimension=1, tiled=True
        ).astype(jnp.float32),
        lax.psum_scatter(
            in_group[7].astype(jnp.bfloat16), "dp", scatter_dimension=1, tiled=True
        ).astype(jnp.float32),
        lax.psum_scatter(
            in_group[8].astype(jnp.bfloat16), "dp", scatter_dimension=1, tiled=True
        ).astype(jnp.float32),
        lax.psum_scatter(
            in_group[9].astype(jnp.bfloat16), "dp", scatter_dimension=1, tiled=True
        ).astype(jnp.float32),
    )
    summed = tuple(
        (
            a.reshape(g.shape[:-1] + (a.shape[-1],)) if g.ndim == 2 else a.reshape(a.shape[-1])
            for a, g in zip(across, gradients)
        )
    )
    return (
        layer_out,
        grad_input,
        grad_table,
        summed[0],
        summed[1],
        summed[2],
        summed[3],
        summed[4],
        summed[5],
        summed[6],
        summed[7],
        summed[8],
        summed[9],
    )


BF16 = jnp.bfloat16
F32 = jnp.float32
LOG2_E = 1.4426950408889634
VMEM_BYTES = 58 * 1024 * 1024
META_ROWS = 4
SLOT_ROWS = 64
EXACT_BASE = 256
TOKEN_TILE = 256
ANY_SPEC = pl.BlockSpec(memory_space=pl.ANY)


def dot_nn(left, right):
    return lax.dot_general(left, right, (((1,), (0,)), ((), ())), preferred_element_type=F32)


def dot_nt(left, right):
    return lax.dot_general(left, right, (((1,), (1,)), ((), ())), preferred_element_type=F32)


def dot_tn(left, right):
    return lax.dot_general(left, right, (((0,), (0,)), ((), ())), preferred_element_type=F32)


def head_operands(queries, keys, head, length):
    lane = lax.broadcasted_iota(jnp.int32, queries.shape, 1)
    row = lax.broadcasted_iota(jnp.int32, queries.shape, 0)
    mine = (lane // HEAD_DIM) == head
    spare = lane == (1 - head) * HEAD_DIM
    zero = jnp.zeros_like(queries)
    fill = jnp.where(row >= length, jnp.full_like(queries, NEG_FILL), zero)
    one_query = jnp.where(mine, queries, jnp.where(spare, jnp.ones_like(queries), zero))
    one_key = jnp.where(mine, keys, jnp.where(spare, fill, zero))
    return mine, one_query, one_key


def attend_kernel(length_ref, q_ref, k_ref, v_ref, out_ref, lse_ref):
    length = length_ref[0]
    factor = LOG2_E * HEAD_DIM**-0.5
    rows = []
    for head in range(2):
        mine, one_query, one_key = head_operands(q_ref[...], k_ref[...], head, length)
        value_one = jnp.where(mine, v_ref[...], jnp.ones_like(v_ref[...]))
        scores = dot_nt(one_key, one_query)
        top = jnp.max(scores, axis=0, keepdims=True)
        weights = jnp.exp2(scores * factor - top * factor).astype(BF16)
        mixed = dot_tn(value_one, weights)
        other = (1 - head) * HEAD_DIM
        total = mixed[other : other + 1]
        lse_ref[0, head : head + 1, :] = top * factor + jnp.log2(total)
        rows.append(mixed[head * HEAD_DIM : (head + 1) * HEAD_DIM] * (1.0 / total))
    out_ref[...] = jnp.transpose(jnp.concatenate(rows, axis=0), (1, 0)).astype(BF16)


def attend_back_kernel(
    length_ref, q_ref, k_ref, v_ref, out_ref, grad_ref, lse_ref, dq_ref, dk_ref, dv_ref, *, chunk
):
    length = length_ref[0]
    positions = q_ref.shape[0]
    factor = LOG2_E * HEAD_DIM**-0.5
    scale = HEAD_DIM**-0.5
    grad = grad_ref[...]
    product = grad.astype(F32) * out_ref[...].astype(F32)
    high = product.astype(BF16)
    low = (product - high.astype(F32)).astype(BF16)
    head_of_lane = lax.broadcasted_iota(jnp.int32, (16, 2 * HEAD_DIM), 1) // HEAD_DIM
    picker = jnp.where(
        head_of_lane == lax.broadcasted_iota(jnp.int32, (16, 2 * HEAD_DIM), 0), 1.0, 0.0
    ).astype(BF16)
    delta = dot_nt(picker, high) + dot_nt(picker, low)
    query_rows = []
    key_parts = ([], [])
    value_parts = ([], [])
    for head in range(2):
        mine, one_query, one_key = head_operands(q_ref[...], k_ref[...], head, length)
        one_value = jnp.where(mine, v_ref[...], jnp.zeros_like(v_ref[...]))
        lse = lse_ref[0, head : head + 1, :]
        row_delta = delta[head : head + 1, :]
        query_grad = jnp.zeros((2 * HEAD_DIM, positions), F32)
        for start in range(0, positions, chunk):
            span = slice(start, start + chunk)
            weights = jnp.exp2(dot_nt(one_key[span], one_query) * factor - lse)
            weight_grad = dot_nt(one_value[span], grad)
            score_grad = (weights * (weight_grad - row_delta)).astype(BF16)
            value_parts[head].append(dot_nn(weights.astype(BF16), grad))
            key_parts[head].append(dot_nn(score_grad, q_ref[...]))
            query_grad = query_grad + dot_tn(k_ref[span, :], score_grad)
        query_rows.append(query_grad[head * HEAD_DIM : (head + 1) * HEAD_DIM])
    first = lax.broadcasted_iota(jnp.int32, (chunk, 2 * HEAD_DIM), 1) < HEAD_DIM
    for part, start in enumerate(range(0, positions, chunk)):
        span = slice(start, start + chunk)
        dk_ref[span, :] = (jnp.where(first, key_parts[0][part], key_parts[1][part]) * scale).astype(BF16)
        dv_ref[span, :] = jnp.where(first, value_parts[0][part], value_parts[1][part]).astype(BF16)
    dq_ref[...] = jnp.transpose(jnp.concatenate(query_rows, axis=0) * scale, (1, 0)).astype(BF16)


def gelu_with_slope(values):
    root = math.sqrt(2.0 / math.pi)
    square = values * values
    share = 0.5 + 0.5 * jnp.tanh(values * (root + root * 0.044715 * square))
    result = values * share
    slope = share + (result - result * share) * (2.0 * root + 6.0 * root * 0.044715 * square)
    return result, slope


def swap_core(value):
    return lax.ppermute(value, "blk", [(0, 1), (1, 0)])


def join_halves(core, own, other):
    first = jnp.where(core == 0, own, other)
    second = jnp.where(core == 0, other, own)
    return jnp.concatenate([first, second], axis=0)


def to_whole(core, local):
    own = lax.dynamic_index_in_dim(local, core, 0, keepdims=False)
    away = lax.dynamic_index_in_dim(local, 1 - core, 0, keepdims=False)
    return join_halves(core, own, swap_core(away))


def fill_other(core, value, arrived):
    return lax.dynamic_update_index_in_dim(value, arrived, 1 - core, 0)


COST_SHARE = 0.3


def kernel_cost(microseconds):
    flops = int(COST_SHARE * microseconds * 1e9)
    return pl.CostEstimate(flops=flops, bytes_accessed=1024, transcendentals=0)


def run_kernel(
    body, grid, scalars, inputs, in_specs, out_specs, out_shape, microseconds, name, scratch=(), carried=()
):
    scalar_count, input_count, output_count = len(scalars), len(inputs), len(out_shape)
    carried_count = len(carried)
    first_carried = scalar_count + input_count

    def kernel(*refs):
        rest = refs[first_carried + carried_count :]
        body(*refs[:first_carried], *rest[:output_count], *rest[output_count + carried_count :])

    results = pl.pallas_call(
        kernel,
        grid_spec=pltpu.PrefetchScalarGridSpec(
            num_scalar_prefetch=scalar_count,
            grid=grid,
            in_specs=list(in_specs) + [ANY_SPEC] * carried_count,
            out_specs=list(out_specs) + [ANY_SPEC] * carried_count,
            scratch_shapes=list(scratch),
        ),
        out_shape=list(out_shape) + [jax.ShapeDtypeStruct(c.shape, c.dtype) for c in carried],
        input_output_aliases={first_carried + i: output_count + i for i in range(carried_count)},
        compiler_params=pltpu.CompilerParams(vmem_limit_bytes=VMEM_BYTES),
        cost_estimate=kernel_cost(microseconds),
        name=name,
    )(*scalars, *inputs, *carried)
    return results[:output_count], results[output_count:]


def behind(*arrays):
    def kernel(*refs):
        pass

    return pl.pallas_call(
        kernel,
        in_specs=[ANY_SPEC] * len(arrays),
        out_specs=[ANY_SPEC] * len(arrays),
        out_shape=[jax.ShapeDtypeStruct(a.shape, a.dtype) for a in arrays],
        input_output_aliases={i: i for i in range(len(arrays))},
        compiler_params=pltpu.CompilerParams(vmem_limit_bytes=VMEM_BYTES),
        cost_estimate=kernel_cost(1),
        name="behind",
    )(*arrays)


FEED_TILE = 512


def shaped(dtype, *shape):
    return jax.ShapeDtypeStruct(shape, dtype)


def row_spec(tile, columns):
    return pl.BlockSpec((tile, columns), lambda i, *scalars: (i, 0))


def fixed_spec(*shape):
    return pl.BlockSpec(shape, lambda *grid: (0,) * len(shape))


def attend(length, qkv):
    positions = qkv.shape[0]
    pairs = HEADS // 2

    def spec(group):
        return pl.BlockSpec((positions, 2 * HEAD_DIM), lambda pair, length: (0, group * pairs + pair))

    results, _ = run_kernel(
        attend_kernel,
        (pairs,),
        [length],
        [qkv, qkv, qkv],
        [spec(0), spec(1), spec(2)],
        [spec(0), pl.BlockSpec((1, 2, positions), lambda pair, length: (pair, 0, 0))],
        [shaped(BF16, positions, D), shaped(F32, pairs, 2, positions)],
        30,
        "attend",
    )
    return results


def attend_back(length, qkv, attended, grad_att, lse, part, parts, grads, carried):
    positions = qkv.shape[0]
    pairs = HEADS // 2
    count = pairs // parts
    shift = part * count

    def spec(group):
        return pl.BlockSpec(
            (positions, 2 * HEAD_DIM), lambda pair, length: (0, group * pairs + shift + pair)
        )

    lse_spec = pl.BlockSpec((1, 2, positions), lambda pair, length: (shift + pair, 0, 0))
    inputs = [qkv, qkv, qkv, attended, grad_att, lse]
    held = len(grads)
    kept = len(carried)

    def kernel(*refs):
        attend_back_kernel(*refs[:7], *refs[7 + held + kept : 10 + held + kept], chunk=min(512, positions))

    aliases = {7 + i: i for i in range(held)}
    aliases.update({7 + held + i: 3 + i for i in range(kept)})
    results = pl.pallas_call(
        kernel,
        grid_spec=pltpu.PrefetchScalarGridSpec(
            num_scalar_prefetch=1,
            grid=(count,),
            in_specs=[spec(0), spec(1), spec(2), spec(0), spec(0), lse_spec] + [ANY_SPEC] * (held + kept),
            out_specs=[spec(0)] * 3 + [ANY_SPEC] * kept,
        ),
        out_shape=[shaped(BF16, positions, D)] * 3 + [jax.ShapeDtypeStruct(c.shape, c.dtype) for c in carried],
        input_output_aliases=aliases,
        compiler_params=pltpu.CompilerParams(vmem_limit_bytes=VMEM_BYTES),
        cost_estimate=kernel_cost(46 / parts),
        name="attend_back",
    )(length, *inputs, *grads, *carried)
    return results[:3], results[3:]


def norm_rows(features):
    center = features - jnp.mean(features, axis=-1, keepdims=True)
    rstd = lax.rsqrt(jnp.mean(center * center, axis=-1, keepdims=True) + 1e-05)
    return center * rstd, rstd


def norm_rows_back(grad_norm, xhat, rstd, gain_row):
    scaled = grad_norm * gain_row
    mean_scaled = jnp.mean(scaled, axis=-1, keepdims=True)
    mean_cross = jnp.mean(scaled * xhat, axis=-1, keepdims=True)
    return rstd * (scaled - mean_scaled - xhat * mean_cross)


def add_column_sums(sums_ref, grad_norm, xhat):
    sums_ref[0:1, :] += jnp.sum(grad_norm * xhat, axis=0, keepdims=True)
    sums_ref[1:2, :] += jnp.sum(grad_norm, axis=0, keepdims=True)


def split_specs(count, tile):
    steps = count // tile // 2

    def early(i):
        return jnp.minimum(i, steps - 1)

    def late(i):
        return jnp.maximum(i - steps, 0)

    def own(i, *scalars):
        core = scalars[-1][0]
        return core, jnp.where(core == 0, early(i), late(i)), 0

    def other(i, *scalars):
        return jnp.where(scalars[-1][0] == 0, late(i), early(i)), 0

    return [pl.BlockSpec((1, tile, D), own), pl.BlockSpec((tile, D), other)]


def store_split(core, own_ref, other_ref, value):
    half = pl.program_id(0) * 2 // pl.num_programs(0)

    @pl.when(half == core)
    def _():
        own_ref[0] = value

    @pl.when(half != core)
    def _():
        other_ref[...] = value


def valid_column(length, tile):
    row = lax.broadcasted_iota(jnp.int32, (tile, 1), 0) + pl.program_id(0) * tile
    return row < length


def share_out(core, value, keep_ref, away_ref):
    rows = keep_ref.shape[-2]
    if len(keep_ref.shape) == 4:
        outer, inner = keep_ref.shape[:2]
        value = value.astype(BF16).reshape(outer, inner, 2, rows, value.shape[1])
        first, second = value[:, :, 0], value[:, :, 1]
        keep_ref[...] = jnp.where(core == 0, first, second)
        away_ref[...] = jnp.where(core == 0, second, first)
        return
    groups = keep_ref.shape[0]
    value = value.astype(BF16).reshape(groups, 2, rows, value.shape[1])
    first, second = value[:, 0], value[:, 1]
    keep_ref[...] = jnp.where(core == 0, first, second)
    away_ref[...] = jnp.where(core == 0, second, first)


def embed_kernel(emb_ref, we_ref, gain_ref, shift_ref, wqkv_ref, low_ref, in_ref, attn_ref, qkv_ref):
    rows = emb_ref[...].astype(F32)
    normed = rows * lax.rsqrt(jnp.mean(rows * rows, axis=-1, keepdims=True) + 1e-06)
    low = normed.astype(BF16)
    low_ref[...] = low
    inputs = dot_nn(low, we_ref[...])
    in_ref[...] = inputs.astype(BF16)
    xhat, _ = norm_rows(inputs)
    attn = (xhat * gain_ref[...] + shift_ref[...]).astype(BF16)
    attn_ref[...] = attn
    qkv_ref[...] = dot_nn(attn, wqkv_ref[...]).astype(BF16)


def embed_and_project(emb, w_embed, gain_row, shift_row, w_qkv):
    count = emb.shape[0]
    tile = TOKEN_TILE
    results, _ = run_kernel(
        embed_kernel,
        (count // tile,),
        [],
        [emb, w_embed, gain_row, shift_row, w_qkv],
        [row_spec(tile, EMB), fixed_spec(EMB, D), fixed_spec(1, D), fixed_spec(1, D), fixed_spec(D, 3 * D)],
        [row_spec(tile, EMB), row_spec(tile, D), row_spec(tile, D), row_spec(tile, 3 * D)],
        [shaped(BF16, count, EMB), shaped(BF16, count, D), shaped(BF16, count, D), shaped(BF16, count, 3 * D)],
        12,
        "embed_and_project",
    )
    return results


def residual_kernel(length_ref, att_ref, in_ref, wo_ref, gain_ref, shift_ref, cot_ref, res_ref, mlp_ref, fin_ref):
    residual = in_ref[...].astype(F32) + dot_nn(att_ref[...], wo_ref[...])
    res_ref[...] = residual.astype(BF16)
    xhat, _ = norm_rows(residual)
    mlp_ref[...] = (xhat * gain_ref[...] + shift_ref[...]).astype(BF16)
    cot = cot_ref[...]
    fin_ref[...] = jnp.where(valid_column(length_ref[0], cot.shape[0]), cot, jnp.zeros_like(cot))


def attention_residual(length, attended, inputs, w_out, gain_row, shift_row, cot):
    count = attended.shape[0]
    row = row_spec(TOKEN_TILE, D)
    results, _ = run_kernel(
        residual_kernel,
        (count // TOKEN_TILE,),
        [length],
        [attended, inputs, w_out, gain_row, shift_row, cot],
        [row, row, fixed_spec(D, D), fixed_spec(1, D), fixed_spec(1, D), row],
        [row, row, row],
        [shaped(BF16, count, D)] * 3,
        8,
        "attention_residual",
    )
    return results


def feed_forward_kernel(
    core_ref, mlp_ref, fin_ref, wu_ref, wd_ref, down_in_ref, grad_in_ref,
    gwd_keep_ref, gwd_away_ref, gwu_keep_ref, gwu_away_ref, down_ref, grad_ref,
    fin_t_ref, hid_ref, pre_ref, *, first
):
    core = core_ref[0]
    count = mlp_ref.shape[0]

    @pl.when(pl.program_id(0) == 0)
    def _():
        fin_t_ref[...] = jnp.transpose(fin_ref[...], (1, 0))
        if first:
            down_ref[...] = jnp.zeros_like(down_ref)
            grad_ref[...] = jnp.zeros_like(grad_ref)
        else:
            down_ref[...] = down_in_ref[...]
            grad_ref[...] = grad_in_ref[...]

    for start in range(0, count, FEED_TILE):
        span = slice(start, start + FEED_TILE)
        hidden, slope = gelu_with_slope(dot_nn(mlp_ref[span, :], wu_ref[...]))
        hid_ref[span, :] = hidden.astype(BF16)
        pre_ref[span, :] = (dot_nt(fin_ref[span, :], wd_ref[...]) * slope).astype(BF16)
    share_out(core, dot_nn(fin_t_ref[...], hid_ref[...]), gwd_keep_ref, gwd_away_ref)
    share_out(core, dot_tn(pre_ref[...], mlp_ref[...]), gwu_keep_ref, gwu_away_ref)
    for start in range(0, count, FEED_TILE):
        span = slice(start, start + FEED_TILE)
        down_ref[span, :] += dot_nn(hid_ref[span, :], wd_ref[...])
        grad_ref[span, :] += dot_nt(pre_ref[span, :], wu_ref[...])


def feed_forward(core, groups, part, parts, mlp_low, final_low, w_up, w_down, down, grad, carried, tile=512):
    count = mlp_low.shape[0]
    width = w_up.shape[1] // parts
    steps = width // tile
    shift = part * steps
    first = down is None
    if first:
        down = grad = jnp.zeros((8, 128), F32)
    down_rows = D // (2 * groups)
    up_rows = w_up.shape[1] // (2 * groups)
    down_share = (groups // 4, 4, down_rows)
    down_spec = pl.BlockSpec((*down_share, tile), lambda j, core: (0, 0, 0, j))
    up_spec = pl.BlockSpec((tile // (2 * up_rows), up_rows, D), lambda j, core: (j, 0, 0))
    whole = fixed_spec(count, D)
    return run_kernel(
        functools.partial(feed_forward_kernel, first=first),
        (steps,),
        [core],
        [mlp_low, final_low, w_up, w_down, down, grad],
        [
            whole,
            whole,
            pl.BlockSpec((D, tile), lambda j, core: (0, shift + j)),
            pl.BlockSpec((tile, D), lambda j, core: (shift + j, 0)),
            fixed_spec(*down.shape),
            fixed_spec(*down.shape),
        ],
        [down_spec, down_spec, up_spec, up_spec, whole, whole],
        [shaped(BF16, *down_share, width)] * 2
        + [shaped(BF16, groups // parts, up_rows, D)] * 2
        + [shaped(F32, count, D)] * 2,
        36,
        "feed_forward",
        scratch=[pltpu.VMEM((D, count), BF16), pltpu.VMEM((count, tile), BF16), pltpu.VMEM((count, tile), BF16)],
        carried=carried,
    )


def middle_kernel(
    length_ref, core_ref, down_ref, gmn_ref, res_ref, fin_ref, gain_ref, wo_ref, att_ref,
    out_ref, out_away_ref, low_ref, gatt_ref, gwo_keep_ref, gwo_away_ref, sums_ref, acc_ref
):
    step = pl.program_id(0)

    @pl.when(step == 0)
    def _():
        sums_ref[...] = jnp.zeros_like(sums_ref)
        acc_ref[...] = jnp.zeros_like(acc_ref)

    residual = res_ref[...].astype(F32)
    keep = valid_column(length_ref[0], residual.shape[0])
    final = jnp.where(keep, residual + down_ref[...], 0.0).astype(BF16)
    store_split(core_ref[0], out_ref, out_away_ref, final)
    xhat, rstd = norm_rows(residual)
    grad = gmn_ref[...]
    add_column_sums(sums_ref, grad, xhat)
    low = (fin_ref[...].astype(F32) + norm_rows_back(grad, xhat, rstd, gain_ref[...])).astype(BF16)
    low_ref[...] = low
    gatt_ref[...] = dot_nt(low, wo_ref[...]).astype(BF16)
    acc_ref[...] += dot_tn(low, att_ref[...])

    @pl.when(step == pl.num_programs(0) - 1)
    def _():
        share_out(core_ref[0], acc_ref[...], gwo_keep_ref, gwo_away_ref)


def feed_forward_to_attention(
    length, core, groups, down, grad_mlp_norm, residual, final_low, gain_row, w_out, attended, carried
):
    count = residual.shape[0]
    row = row_spec(TOKEN_TILE, D)
    share = (groups // 4, 4, D // (2 * groups), D)
    return run_kernel(
        middle_kernel,
        (count // TOKEN_TILE,),
        [length, core],
        [down, grad_mlp_norm, residual, final_low, gain_row, w_out, attended],
        [row, row, row, row, fixed_spec(1, D), fixed_spec(D, D), row],
        split_specs(count, TOKEN_TILE) + [row, row, fixed_spec(*share), fixed_spec(*share), fixed_spec(8, D)],
        [shaped(BF16, 2, count // 2, D), shaped(BF16, count // 2, D)] + [shaped(BF16, count, D)] * 2 + [shaped(BF16, *share)] * 2 + [shaped(F32, 8, D)],
        15,
        "feed_forward_to_attention",
        scratch=[pltpu.VMEM((D, D), F32)],
        carried=carried,
    )


def outer_kernel(core_ref, dq_ref, dk_ref, dv_ref, right_ref, keep_ref, away_ref, all_ref):
    right = right_ref[...]
    for group, ref in enumerate((dq_ref, dk_ref, dv_ref)):
        for start in range(0, D, TOKEN_TILE):
            rows = slice(group * D + start, group * D + start + TOKEN_TILE)
            all_ref[rows, :] = dot_tn(ref[:, start : start + TOKEN_TILE], right).astype(BF16)
    share_out(core_ref[0], all_ref[...], keep_ref, away_ref)


def outer_qkv(core, groups, grads, right, half, carried):
    count = right.shape[0]
    columns = right.shape[1] // 2
    share = (groups, 3 * D // (2 * groups), columns)
    return run_kernel(
        outer_kernel,
        (1,),
        [core],
        [*grads, right],
        [fixed_spec(count, D)] * 3 + [pl.BlockSpec((count, columns), lambda i, core: (0, half))],
        [fixed_spec(*share)] * 2,
        [shaped(BF16, *share)] * 2,
        8,
        "outer_qkv",
        scratch=[pltpu.VMEM((3 * D, columns), BF16)],
        carried=carried,
    )


def input_kernel(
    core_ref, dq_ref, dk_ref, dv_ref, wqkv_ref, in_ref, low_ref, gain_ref, we_ref, emb_ref, nl_ref,
    grad_ref, grad_away_ref, rows_ref, gwe_keep_ref, gwe_away_ref, sums_ref, acc_ref
):
    step = pl.program_id(0)

    @pl.when(step == 0)
    def _():
        sums_ref[...] = jnp.zeros_like(sums_ref)
        acc_ref[...] = jnp.zeros_like(acc_ref)

    grad = (
        dot_nt(dq_ref[...], wqkv_ref[:, :D])
        + dot_nt(dk_ref[...], wqkv_ref[:, D : 2 * D])
        + dot_nt(dv_ref[...], wqkv_ref[:, 2 * D :])
    )
    xhat, rstd = norm_rows(in_ref[...].astype(F32))
    add_column_sums(sums_ref, grad, xhat)
    low = (low_ref[...].astype(F32) + norm_rows_back(grad, xhat, rstd, gain_ref[...])).astype(BF16)
    store_split(core_ref[0], grad_ref, grad_away_ref, low)
    acc_ref[...] += dot_tn(low, nl_ref[...])
    back = dot_nt(low, we_ref[...])
    emb = emb_ref[...].astype(F32)
    emb_rstd = lax.rsqrt(jnp.mean(emb * emb, axis=-1, keepdims=True) + 1e-06)
    normed = emb * emb_rstd
    rows_ref[...] = (emb_rstd * (back - normed * jnp.mean(normed * back, axis=-1, keepdims=True))).astype(BF16)

    @pl.when(step == pl.num_programs(0) - 1)
    def _():
        share_out(core_ref[0], acc_ref[...], gwe_keep_ref, gwe_away_ref)


def input_gradient(core, groups, grads, w_qkv, inputs, residual_low, gain_row, w_embed, emb, normed_low, carried):
    count = inputs.shape[0]
    tile = TOKEN_TILE
    share = (2 * groups, D // (4 * groups), EMB)
    row, narrow = row_spec(tile, D), row_spec(tile, EMB)
    return run_kernel(
        input_kernel,
        (count // tile,),
        [core],
        [*grads, w_qkv, inputs, residual_low, gain_row, w_embed, emb, normed_low],
        [row, row, row, fixed_spec(D, 3 * D), row, row, fixed_spec(1, D), fixed_spec(EMB, D), narrow, narrow],
        split_specs(count, tile) + [narrow, fixed_spec(*share), fixed_spec(*share), fixed_spec(8, D)],
        [shaped(BF16, 2, count // 2, D), shaped(BF16, count // 2, D), shaped(BF16, count, EMB)] + [shaped(BF16, *share)] * 2 + [shaped(F32, 8, D)],
        16,
        "input_gradient",
        scratch=[pltpu.VMEM((D, EMB), F32)],
        carried=carried,
    )


def exchange(value, bit, dp_bits, pattern=1):
    return lax.ppermute(value, "dp", [(i, i ^ (pattern << bit)) for i in range(1 << dp_bits)])


class Halving:
    def __init__(self, labels, dp_bits):
        self.labels = list(labels)
        self.dp_bits = dp_bits
        self.terms = []
        self.fixed = {}

    def over_cores(self, keep, away):
        shape = (2,) * len(self.labels) + keep.shape[1:]
        labels = tuple(self.labels)
        self.terms = [(keep.reshape(shape), labels), (swap_core(away).reshape(shape), labels)]

    @property
    def keep(self):
        return self.terms[0][0]

    @keep.setter
    def keep(self, value):
        self.terms[0] = (value, self.terms[0][1])

    def part(self, fixed):
        total = 0.0
        for value, labels in self.terms:
            spans = [label not in fixed for label in labels]
            starts = [0 if span else fixed[label] for span, label in zip(spans, labels)] + [0, 0]
            sizes = [2 if span else 1 for span in spans] + list(value.shape[-2:])
            piece = lax.dynamic_slice(value, starts, sizes)
            total = total + piece.reshape((2,) * sum(spans) + value.shape[-2:]).astype(F32)
        return total

    def total(self):
        return self.part(self.fixed)

    def away(self, bit_label):
        bit = (lax.axis_index("dp") >> bit_label) & 1
        return self.part({**self.fixed, bit_label: 1 - bit}).astype(BF16)

    def send(self, bit_label, away):
        self.fixed[bit_label] = (lax.axis_index("dp") >> bit_label) & 1
        labels = tuple(label for label in self.labels if label not in self.fixed)
        self.terms.append((exchange(away, bit_label, self.dp_bits), labels))


def between_planes(value, dp_bits):
    plane = lax.axis_index("dp") >> 2
    parts = [lax.dynamic_index_in_dim(value, plane, 0, keepdims=False)]
    for step in range(1, value.shape[0]):
        away = lax.dynamic_index_in_dim(value, plane ^ step, 0, keepdims=False)
        parts.append(exchange(away, 2, dp_bits, step))
    return parts


def whole_sequence_shards(
    token_ids,
    seq_lengths,
    diffusion_time,
    embed_table,
    w_embed,
    w_time,
    gain_attn,
    bias_attn,
    gain_mlp,
    bias_mlp,
    w_qkv,
    w_out,
    w_up,
    w_down,
    cotangent,
):
    core = lax.axis_index("blk")
    cores = core.reshape(1).astype(jnp.int32)
    groups = lax.axis_size("dp")
    devices = 2 * groups
    dp_bits = groups.bit_length() - 1
    everywhere = ("dp", "blk")
    labels = list(reversed(range(dp_bits)))
    planes = [[4 * high + low for low in range(4)] for high in range(groups // 4)]
    lines = [[4 * high + low for high in range(groups // 4)] for low in range(4)]
    ids = to_whole(core, token_ids)
    cot = to_whole(core, cotangent)
    positions = ids.shape[0]
    length = lax.dynamic_index_in_dim(seq_lengths, core, 0, keepdims=True)
    time = lax.dynamic_index_in_dim(diffusion_time, core, 0, keepdims=True)
    emb = embed_table[ids]

    valid = jnp.arange(positions, dtype=jnp.int32) < length[0]
    row_count = VOCAB // devices
    owner = jnp.where(valid, ids // row_count, -1)
    offset = ids % row_count
    slots = SLOT_ROWS - META_ROWS
    member = owner[:, None] == jnp.arange(devices, dtype=jnp.int32)[None, :]
    earlier = jnp.arange(positions)[:, None] > jnp.arange(positions)[None, :]
    before = dot_nn(earlier.astype(BF16), member.astype(BF16))
    rank = jnp.sum(jnp.where(member, before, 0.0), axis=1).astype(jnp.int32)
    most = jnp.max(jnp.sum(member.astype(jnp.int32), axis=0))
    offset_digits = jnp.stack(
        [(offset // EXACT_BASE).astype(BF16), (offset % EXACT_BASE).astype(BF16), jnp.ones(positions, BF16)],
        axis=1,
    )

    def dispatch(turn):
        slot = rank - turn * slots
        inside = (owner >= 0) & (slot >= 0) & (slot < slots)
        target = jnp.where(inside, owner * SLOT_ROWS + META_ROWS + slot, -1)
        place = jnp.arange(devices * SLOT_ROWS, dtype=jnp.int32)[:, None] == target[None, :]
        digits = dot_nn(place.astype(BF16), offset_digits).reshape(devices, SLOT_ROWS, 3)
        head = jnp.transpose(digits, (0, 2, 1)).reshape(devices, 1, 3 * SLOT_ROWS)
        peak = jnp.stack([most // EXACT_BASE, most % EXACT_BASE]).astype(F32)
        peak = jnp.broadcast_to(peak, (devices, 1, 2))
        gap = jnp.zeros((devices, 1, EMB - 3 * SLOT_ROWS - 2), F32)
        return target, jnp.concatenate([head, peak, gap], axis=2)

    meta_target = jnp.arange(devices * META_ROWS, dtype=jnp.int32)
    meta_target = meta_target // META_ROWS * SLOT_ROWS + meta_target % META_ROWS

    def packed(target, meta, grads):
        meta = meta.astype(BF16).reshape(devices * META_ROWS, EMB)
        target = jnp.concatenate([target, meta_target])
        place = jnp.arange(devices * SLOT_ROWS, dtype=jnp.int32)[:, None] == target[None, :]
        rows = dot_nn(place.astype(BF16), jnp.concatenate([grads, meta]))
        return rows.astype(BF16).reshape(devices, SLOT_ROWS, EMB)

    def deliver(rows):
        return lax.all_to_all(rows, everywhere, 0, 0, tiled=True)

    def collect(rows):
        head = rows[:, 0].astype(F32)
        high, low, used = (head[:, i * SLOT_ROWS : (i + 1) * SLOT_ROWS] for i in range(3))
        row = jnp.where(used > 0.5, high * EXACT_BASE + low, -1.0).astype(jnp.int32)
        row = jnp.pad(row, ((0, 0), (0, rows.shape[1] - SLOT_ROWS)), constant_values=-1)
        hit = jnp.arange(row_count, dtype=jnp.int32)[:, None] == row.reshape(1, -1)
        return dot_nn(hit.astype(BF16), rows.reshape(-1, EMB))

    first_target, first_head = dispatch(0)

    def over_cores(keep, arrived):
        return (keep.astype(F32) + arrived.astype(F32)).astype(BF16)

    def scattered(value, index_groups):
        return lax.psum_scatter(value, "dp", scatter_dimension=0, axis_index_groups=index_groups, tiled=True)[0]

    time_low = time_features(time, TIME_WIDTH).astype(BF16)
    modulation = dot_nn(time_low, w_time)
    scale_attn, shift_attn, scale_mlp, shift_mlp = jnp.split(modulation, 4, axis=1)
    gain_row_attn = gain_attn + scale_attn
    gain_row_mlp = gain_mlp + scale_mlp
    normed_low, inputs, attn_low, qkv = embed_and_project(
        emb, w_embed, gain_row_attn, bias_attn + shift_attn, w_qkv
    )
    attended, lse = attend(length, qkv)
    residual, mlp_low, final_low = attention_residual(
        length, attended, inputs, w_out, gain_row_mlp, bias_mlp + shift_mlp, cot
    )

    hidden_width = w_up.shape[1]
    feed = functools.partial(feed_forward, cores, groups)
    (keep_d, away_d, keep_u, away_u, down, grad), _ = feed(
        0, 2, mlp_low, final_low, w_up, w_down, None, None, []
    )
    up_0, up_1 = Halving(labels[1:], dp_bits), Halving(labels[1:], dp_bits)
    qkv_a, qkv_b = Halving(labels, dp_bits), Halving(labels, dp_bits)
    up_0.over_cores(keep_u, away_u)
    arrived_d = swap_core(away_d)
    (next_keep, next_away, keep_u, away_u, down, grad), (up_0.keep, keep_d) = feed(
        1, 2, mlp_low, final_low, w_up, w_down, down, grad, [up_0.keep, keep_d]
    )
    away, down_0, next_keep, next_away, keep_u, away_u = behind(
        up_0.away(0), over_cores(keep_d, arrived_d), next_keep, next_away, keep_u, away_u
    )
    up_0.send(0, away)
    up_1.over_cores(keep_u, away_u)
    arrived_d = swap_core(next_away)
    down_0 = scattered(down_0, lines)
    (layer_out, layer_away, residual_low, grad_att, keep_o, away_o, sums_mlp), kept = feed_forward_to_attention(
        length, cores, groups, down, grad, residual, final_low, gain_row_mlp, w_out, attended,
        [up_0.keep, up_1.keep, next_keep],
    )
    up_0.keep, up_1.keep, keep_d = kept
    away_0, away_1, down_1, keep_o, away_o = behind(
        up_0.away(1), up_1.away(0), over_cores(keep_d, arrived_d), keep_o, away_o
    )
    up_0.send(1, away_0)
    up_1.send(0, away_1)
    down_1 = scattered(down_1, lines)
    arrived_o = swap_core(away_o)
    back = functools.partial(attend_back, length, qkv, attended, grad_att, lse)
    grads, (up_0.keep, up_1.keep, keep_o, down_0) = back(0, 2, [], [up_0.keep, up_1.keep, keep_o, down_0])
    away_1, out_sum, up_first = behind(
        up_1.away(1), over_cores(keep_o, arrived_o), up_0.total().astype(BF16)
    )
    up_1.send(1, away_1)
    out_sum = scattered(out_sum, lines)
    grads, (up_1.keep, up_first) = back(1, 2, grads, [up_1.keep, up_first])
    up_rows = [up_first, up_1.total().astype(BF16)]
    up_rows = jnp.concatenate([rows.reshape((-1,) + rows.shape[-2:]) for rows in up_rows])
    up_sum = scattered(up_rows, lines)
    (keep_a, away_a), (down_1,) = outer_qkv(cores, groups, grads, attn_low, 0, [down_1])
    keep_a, away_a = behind(keep_a, away_a)
    qkv_a.over_cores(keep_a, away_a)
    orders = [(0, 1), (1, 0)]
    (keep_b, away_b), (qkv_a.keep,) = outer_qkv(cores, groups, grads, attn_low, 1, [qkv_a.keep])
    in_plane = jnp.concatenate([down_0, down_1, out_sum], axis=2)
    away_a, keep_b, away_b, in_plane = behind(qkv_a.away(orders[0][0]), keep_b, away_b, in_plane)
    own_sum = scattered(in_plane, planes)
    qkv_a.send(orders[0][0], away_a)
    qkv_b.over_cores(keep_b, away_b)
    qkv_b.send(orders[1][0], *behind(qkv_b.away(orders[1][0])))
    (grad_input, input_away, grad_rows, keep_e, away_e, sums_attn), kept = input_gradient(
        cores, groups, grads, w_qkv, inputs, residual_low, gain_row_attn, w_embed, emb, normed_low,
        [qkv_a.keep, qkv_b.keep],
    )
    qkv_a.keep, qkv_b.keep = kept

    grad_modulation = jnp.concatenate([sums_attn[0], sums_attn[1], sums_mlp[0], sums_mlp[1]])
    gain_columns = jnp.transpose(grad_modulation.reshape(4, devices, -1), (1, 0, 2)).reshape(devices, -1)
    mod_rows = jnp.concatenate([grad_modulation.reshape(devices, -1), gain_columns], axis=1)
    mod_high = mod_rows.astype(BF16).astype(F32)
    mod_low = mod_rows - mod_high
    time_rows = jnp.broadcast_to(time_low.astype(F32), (devices, TIME_WIDTH))
    first_meta = jnp.concatenate(
        [first_head, jnp.stack([mod_high, mod_low, time_rows], axis=1)], axis=1
    )
    embed_rows = over_cores(keep_e, swap_core(away_e))
    payload = jnp.concatenate([packed(first_target, first_meta, grad_rows), embed_rows], axis=1)
    payload, away_a, away_b, up_sum, layer_away, input_away = behind(
        payload, qkv_a.away(orders[0][1]), qkv_b.away(orders[1][1]), up_sum, layer_away, input_away
    )
    arrived = deliver(payload)
    qkv_a.send(orders[0][1], away_a)
    qkv_b.send(orders[1][1], away_b)
    qkv_rows = jnp.concatenate([qkv_a.total(), qkv_b.total()], axis=-1).astype(BF16)
    qkv_rows = qkv_rows.reshape((-1,) + qkv_rows.shape[-2:])
    layer_out = fill_other(core, layer_out, swap_core(layer_away))
    grad_w_qkv = sum(part.astype(F32) for part in between_planes(qkv_rows, dp_bits))
    embed_sum = arrived[:, SLOT_ROWS:].astype(F32).reshape(groups, -1, EMB)
    embed_sum = jnp.sum(embed_sum, axis=0)
    grad_input = fill_other(core, grad_input, swap_core(input_away))
    grad_table = collect(arrived)
    sums = arrived[:, 1].astype(F32) + arrived[:, 2].astype(F32)
    time_width = sums.shape[1] // 2
    grad_w_time = lax.dot_general(
        arrived[:, 3].astype(F32),
        sums[:, :time_width],
        (((0,), (0,)), ((), ())),
        precision=lax.Precision.HIGHEST,
    )
    gain_sums = jnp.sum(sums[:, time_width:], axis=0).reshape(4, -1)
    peaks = arrived[:, 0, 3 * SLOT_ROWS : 3 * SLOT_ROWS + 2].astype(F32)
    peak = jnp.max(peaks[:, 0] * EXACT_BASE + peaks[:, 1]).astype(jnp.int32)
    turns = (peak + slots - 1) // slots

    def more_turns(state):
        return state[0] < turns

    def next_turn(state):
        turn, table = state
        target, head = dispatch(turn)
        meta = jnp.pad(head, ((0, 0), (0, META_ROWS - 1), (0, 0)))
        return turn + 1, table + collect(deliver(packed(target, meta, grad_rows)))

    _, grad_table = lax.while_loop(more_turns, next_turn, (jnp.int32(1), grad_table))
    return (
        layer_out,
        grad_input,
        grad_table,
        embed_sum.T,
        grad_w_time,
        gain_sums[0],
        gain_sums[1],
        gain_sums[2],
        gain_sums[3],
        grad_w_qkv.T,
        own_sum[:, hidden_width:].astype(F32).T,
        up_sum.astype(F32).T,
        own_sum[:, :hidden_width].astype(F32).T,
    )


def shards(*arguments):
    seq_count, pos_count = arguments[0].shape
    groups = lax.axis_size("dp")
    whole = seq_count == 2 and lax.axis_size("blk") == 2
    whole = whole and groups >= 4 and groups & (groups - 1) == 0 and pos_count % 256 == 0
    return whole_sequence_shards(*arguments) if whole else split_position_shards(*arguments)


def solution(mesh):
    return jax.shard_map(
        shards,
        mesh=mesh,
        in_specs=(
            P("dp", "blk"),
            P("dp"),
            P("dp"),
            P(),
            P(),
            P(),
            P(),
            P(),
            P(),
            P(),
            P(),
            P(),
            P(),
            P(),
            P("dp", "blk", None),
        ),
        out_specs=(
            P("dp", "blk", None),
            P("dp", "blk", None),
            P(("dp", "blk"), None),
            P(None, ("dp", "blk")),
            P(None, ("dp", "blk")),
            P(("dp", "blk")),
            P(("dp", "blk")),
            P(("dp", "blk")),
            P(("dp", "blk")),
            P(None, ("dp", "blk")),
            P(None, ("dp", "blk")),
            P(None, ("dp", "blk")),
            P(None, ("dp", "blk")),
        ),
        check_vma=False,
    )
```

```python
import functools
import math

import jax
import jax.numpy as jnp
from jax import lax
from jax.experimental import pallas as pl
from jax.experimental.pallas import tpu as pltpu
from jax.sharding import PartitionSpec as P

D = 1024
HEADS = 16
HEAD_DIM = 64
EMB = 256
VOCAB = 32000
TIME_WIDTH = 256


NEG_FILL = -1000000000.0


def from_behind(value, axis, steps):
    count = lax.axis_size(axis)
    pairs = [(source, (source + steps) % count) for source in range(count)]
    return lax.ppermute(value, axis, pairs)


def time_features(diffusion_time, feature_width):
    half_width = feature_width // 2
    frequency = jnp.exp(-math.log(1000.0) * jnp.arange(half_width, dtype=jnp.float32) / half_width)
    angles = diffusion_time.astype(jnp.float32)[:, None] * frequency[None, :]
    return jnp.concatenate([jnp.sin(angles), jnp.cos(angles)], axis=1)


def modulated_norm(features, gain_vec, bias_vec, scale_rows, shift_rows):
    center = features - jnp.mean(features, axis=-1, keepdims=True)
    spread = jnp.mean(center * center, axis=-1, keepdims=True)
    return center * lax.rsqrt(spread + 1e-05) * (gain_vec + scale_rows[:, None, :]) + (
        bias_vec + shift_rows[:, None, :]
    )


def normalize_rows(row_values):
    return row_values * lax.rsqrt(jnp.mean(row_values * row_values, axis=-1, keepdims=True) + 1e-06)


def project(left_side, right_side):
    return lax.dot_general(
        left_side,
        right_side,
        (((left_side.ndim - 1,), (0,)), ((), ())),
        preferred_element_type=jnp.float32,
    )


def project_back(left_side, right_side):
    return lax.dot_general(
        left_side,
        right_side,
        (((left_side.ndim - 1,), (1,)), ((), ())),
        preferred_element_type=jnp.float32,
    )


def outer_sum(left_side, right_side):
    return lax.dot_general(
        left_side, right_side, (((0, 1), (0, 1)), ((), ())), preferred_element_type=jnp.float32
    )


def scatter_rows(running_total, offsets, grad_values):
    row_span = running_total.shape[0]
    inside = (offsets >= 0) & (offsets < row_span)
    return running_total.at[jnp.where(inside, offsets, row_span)].add(grad_values, mode="drop")


def group_columns(matrix, group_count):
    if matrix.ndim == 1:
        return matrix.reshape(1, group_count, matrix.shape[0] // group_count)
    return matrix.reshape(matrix.shape[0], group_count, matrix.shape[1] // group_count)


def split_position_shards(
    token_ids,
    seq_lengths,
    diffusion_time,
    embed_table,
    w_embed,
    w_time,
    gain_attn,
    bias_attn,
    gain_mlp,
    bias_mlp,
    w_qkv,
    w_out,
    w_up,
    w_down,
    cotangent,
):
    seq_count, pos_count = token_ids.shape
    scale_factor = HEAD_DIM ** (-0.5)
    cycle_size = lax.axis_size("blk")
    cycle_index = lax.axis_index("blk")
    positions = cycle_index * pos_count + jnp.arange(pos_count, dtype=jnp.int32)
    valid_rows = (positions[None, :] < seq_lengths[:, None]).astype(jnp.float32)[:, :, None]
    emb_rows = embed_table[token_ids].astype(jnp.float32)
    normed, norm_pull = jax.vjp(normalize_rows, emb_rows)
    normed_low = normed.astype(jnp.bfloat16)
    inputs = project(normed_low, w_embed)
    time_low = time_features(diffusion_time, TIME_WIDTH).astype(jnp.bfloat16)
    modulation = jnp.dot(time_low, w_time, preferred_element_type=jnp.float32)
    scale_attn, shift_attn, scale_mlp, shift_mlp = jnp.split(modulation, 4, axis=1)
    normed_attn, attn_pull = jax.vjp(
        modulated_norm, inputs, gain_attn, bias_attn, scale_attn, shift_attn
    )
    attn_low = normed_attn.astype(jnp.bfloat16)
    qkv_low = project(attn_low, w_qkv).astype(jnp.bfloat16)
    queries = qkv_low[:, :, :D].reshape(seq_count, pos_count, HEADS, HEAD_DIM)
    kv_local = qkv_low[:, :, D:]

    def masked_scores(key_heads, key_start):
        key_count = key_heads.shape[1]
        key_pos = key_start + jnp.arange(key_count, dtype=jnp.int32)
        key_keep = (key_pos[None, :] < seq_lengths[:, None])[:, None, None, :]
        scores = (
            jnp.einsum("sqhd,skhd->shqk", queries, key_heads, preferred_element_type=jnp.float32)
            * scale_factor
        )
        return jnp.where(key_keep, scores, NEG_FILL)

    key_piece = lax.all_gather(kv_local, "blk", axis=1, tiled=True)
    run_max = jnp.full((seq_count, HEADS, pos_count), -1e30, jnp.float32)
    key_count = key_piece.shape[1]
    key_heads = key_piece[:, :, :D].reshape(seq_count, key_count, HEADS, HEAD_DIM)
    value_heads = key_piece[:, :, D:].reshape(seq_count, key_count, HEADS, HEAD_DIM)
    scores = masked_scores(key_heads, jnp.int32(0))
    new_max = jnp.maximum(run_max, jnp.max(scores, axis=-1))
    softmax_weights = jnp.exp(scores - new_max[..., None])
    run_sum = jnp.sum(softmax_weights, axis=-1)
    contrib = jnp.einsum(
        "shqk,skhd->sqhd",
        softmax_weights.astype(jnp.bfloat16),
        value_heads,
        preferred_element_type=jnp.float32,
    )
    run_acc = contrib
    run_max, run_sum, run_acc = (new_max, run_sum, run_acc)
    log_total = run_max + jnp.log(run_sum)
    attended = run_acc / jnp.transpose(run_sum, (0, 2, 1))[..., None]
    attended_low = attended.reshape(seq_count, pos_count, D).astype(jnp.bfloat16)
    residual = inputs + project(attended_low, w_out)
    normed_mlp, mlp_pull = jax.vjp(
        modulated_norm, residual, gain_mlp, bias_mlp, scale_mlp, shift_mlp
    )
    mlp_low = normed_mlp.astype(jnp.bfloat16)
    pre_act = project(mlp_low, w_up)
    activated, gelu_pull = jax.vjp(jax.nn.gelu, pre_act)
    hidden_low = activated.astype(jnp.bfloat16)
    final_sum = (residual + project(hidden_low, w_down)) * valid_rows
    layer_out = final_sum.astype(jnp.bfloat16)
    grad_final = cotangent.astype(jnp.float32) * valid_rows
    final_low = grad_final.astype(jnp.bfloat16)
    grad_w_down = outer_sum(hidden_low, final_low)
    (grad_pre,) = gelu_pull(project_back(final_low, w_down))
    pre_low = grad_pre.astype(jnp.bfloat16)
    grad_w_up = outer_sum(mlp_low, pre_low)
    grad_res_norm, grad_gain_mlp, grad_bias_mlp, grad_scale_mlp, grad_shift_mlp = mlp_pull(
        project_back(pre_low, w_up)
    )
    residual_grad = grad_final + grad_res_norm
    residual_low = residual_grad.astype(jnp.bfloat16)
    grad_w_out = outer_sum(attended_low, residual_low)
    grad_att = (
        project_back(residual_low, w_out)
        .astype(jnp.bfloat16)
        .reshape(seq_count, pos_count, HEADS, HEAD_DIM)
    )
    row_delta = jnp.transpose(jnp.sum(grad_att * attended, axis=-1), (0, 2, 1))

    def key_block(kv_block, owner_index):
        key_heads = kv_block[:, :, :D].reshape(seq_count, pos_count, HEADS, HEAD_DIM)
        value_heads = kv_block[:, :, D:].reshape(seq_count, pos_count, HEADS, HEAD_DIM)
        scores = masked_scores(key_heads, owner_index * pos_count)
        softmax_weights = jnp.exp(scores - log_total[..., None])
        grad_weights = jnp.einsum(
            "sqhd,skhd->shqk", grad_att, value_heads, preferred_element_type=jnp.float32
        )
        grad_scores = (
            softmax_weights * (grad_weights - row_delta[..., None]) * scale_factor
        ).astype(jnp.bfloat16)
        grad_queries = jnp.einsum(
            "shqk,skhd->sqhd", grad_scores, key_heads, preferred_element_type=jnp.float32
        )
        grad_keys = jnp.einsum(
            "shqk,sqhd->skhd", grad_scores, queries, preferred_element_type=jnp.float32
        )
        grad_values = jnp.einsum(
            "shqk,sqhd->skhd",
            softmax_weights.astype(jnp.bfloat16),
            grad_att,
            preferred_element_type=jnp.float32,
        )
        joined = jnp.concatenate(
            [
                grad_keys.reshape(seq_count, pos_count, D),
                grad_values.reshape(seq_count, pos_count, D),
            ],
            axis=-1,
        )
        return (grad_queries, joined)

    def pass_back(grad_values):
        return from_behind(grad_values.astype(jnp.bfloat16), "blk", 1).astype(grad_values.dtype)

    zero_kv = jnp.zeros((seq_count, pos_count, 2 * D), jnp.float32)
    zero_query = jnp.zeros((seq_count, pos_count, HEADS, HEAD_DIM), jnp.float32)

    def cycle_step(turn_index, cycle_state):
        kv_block, grad_kv, grad_query = cycle_state
        part_query, part_kv = key_block(kv_block, (cycle_index - turn_index) % cycle_size)
        kv_block = from_behind(kv_block, "blk", 1)
        return (kv_block, pass_back(grad_kv + part_kv), grad_query + part_query)

    kv_block, grad_kv, grad_query = lax.fori_loop(
        0, cycle_size - 1, cycle_step, (kv_local, zero_kv, zero_query)
    )
    part_query, part_kv = key_block(kv_block, (cycle_index + 1) % cycle_size)
    grad_kv = pass_back(grad_kv + part_kv)
    grad_query = grad_query + part_query
    grad_qkv = jnp.concatenate(
        [grad_query.reshape(seq_count, pos_count, D), grad_kv], axis=-1
    ).astype(jnp.bfloat16)
    grad_w_qkv = outer_sum(attn_low, grad_qkv)
    grad_in_norm, grad_gain_attn, grad_bias_attn, grad_scale_attn, grad_shift_attn = attn_pull(
        project_back(grad_qkv, w_qkv)
    )
    input_grad = residual_grad + grad_in_norm
    grad_input = input_grad.astype(jnp.bfloat16)
    grad_w_embed = outer_sum(normed_low, grad_input)
    grad_modulation = jnp.concatenate(
        [grad_scale_attn, grad_shift_attn, grad_scale_mlp, grad_shift_mlp], axis=1
    )
    grad_w_time = jnp.dot(
        time_low.astype(jnp.float32).T, grad_modulation, precision=lax.Precision.HIGHEST
    )
    (grad_rows,) = norm_pull(project_back(grad_input, w_embed))
    flat_ids = token_ids.reshape(-1)
    flat_grads = grad_rows.reshape(-1, EMB)
    row_count = VOCAB // lax.axis_size(("dp", "blk"))
    own_start = lax.axis_index(("dp", "blk")) * row_count
    piece_ids = lax.all_gather(flat_ids, ("dp", "blk"), axis=0, tiled=True)
    piece_grads = lax.all_gather(
        flat_grads.astype(jnp.bfloat16), ("dp", "blk"), axis=0, tiled=True
    ).astype(jnp.float32)
    grad_table = scatter_rows(
        jnp.zeros((row_count, EMB), jnp.float32), piece_ids - own_start, piece_grads
    )
    group_count = lax.axis_size("dp")
    gradients = (
        grad_w_embed,
        grad_w_time,
        grad_gain_attn,
        grad_bias_attn,
        grad_gain_mlp,
        grad_bias_mlp,
        grad_w_qkv,
        grad_w_out,
        grad_w_up,
        grad_w_down,
    )
    grouped = tuple((group_columns(g, group_count) for g in gradients))
    in_group = (
        lax.psum_scatter(
            grouped[0].astype(jnp.bfloat16), "blk", scatter_dimension=2, tiled=True
        ).astype(jnp.float32),
        lax.psum_scatter(
            grouped[1].astype(jnp.bfloat16), "blk", scatter_dimension=2, tiled=True
        ).astype(jnp.float32),
        lax.psum_scatter(
            grouped[2].astype(jnp.bfloat16), "blk", scatter_dimension=2, tiled=True
        ).astype(jnp.float32),
        lax.psum_scatter(
            grouped[3].astype(jnp.bfloat16), "blk", scatter_dimension=2, tiled=True
        ).astype(jnp.float32),
        lax.psum_scatter(
            grouped[4].astype(jnp.bfloat16), "blk", scatter_dimension=2, tiled=True
        ).astype(jnp.float32),
        lax.psum_scatter(
            grouped[5].astype(jnp.bfloat16), "blk", scatter_dimension=2, tiled=True
        ).astype(jnp.float32),
        lax.psum_scatter(
            grouped[6].astype(jnp.bfloat16), "blk", scatter_dimension=2, tiled=True
        ).astype(jnp.float32),
        lax.psum_scatter(
            grouped[7].astype(jnp.bfloat16), "blk", scatter_dimension=2, tiled=True
        ).astype(jnp.float32),
        lax.psum_scatter(
            grouped[8].astype(jnp.bfloat16), "blk", scatter_dimension=2, tiled=True
        ).astype(jnp.float32),
        lax.psum_scatter(
            grouped[9].astype(jnp.bfloat16), "blk", scatter_dimension=2, tiled=True
        ).astype(jnp.float32),
    )
    across = (
        lax.psum_scatter(
            in_group[0].astype(jnp.bfloat16), "dp", scatter_dimension=1, tiled=True
        ).astype(jnp.float32),
        lax.psum_scatter(
            in_group[1].astype(jnp.bfloat16), "dp", scatter_dimension=1, tiled=True
        ).astype(jnp.float32),
        lax.psum_scatter(
            in_group[2].astype(jnp.bfloat16), "dp", scatter_dimension=1, tiled=True
        ).astype(jnp.float32),
        lax.psum_scatter(
            in_group[3].astype(jnp.bfloat16), "dp", scatter_dimension=1, tiled=True
        ).astype(jnp.float32),
        lax.psum_scatter(
            in_group[4].astype(jnp.bfloat16), "dp", scatter_dimension=1, tiled=True
        ).astype(jnp.float32),
        lax.psum_scatter(
            in_group[5].astype(jnp.bfloat16), "dp", scatter_dimension=1, tiled=True
        ).astype(jnp.float32),
        lax.psum_scatter(
            in_group[6].astype(jnp.bfloat16), "dp", scatter_dimension=1, tiled=True
        ).astype(jnp.float32),
        lax.psum_scatter(
            in_group[7].astype(jnp.bfloat16), "dp", scatter_dimension=1, tiled=True
        ).astype(jnp.float32),
        lax.psum_scatter(
            in_group[8].astype(jnp.bfloat16), "dp", scatter_dimension=1, tiled=True
        ).astype(jnp.float32),
        lax.psum_scatter(
            in_group[9].astype(jnp.bfloat16), "dp", scatter_dimension=1, tiled=True
        ).astype(jnp.float32),
    )
    summed = tuple(
        (
            a.reshape(g.shape[:-1] + (a.shape[-1],)) if g.ndim == 2 else a.reshape(a.shape[-1])
            for a, g in zip(across, gradients)
        )
    )
    return (
        layer_out,
        grad_input,
        grad_table,
        summed[0],
        summed[1],
        summed[2],
        summed[3],
        summed[4],
        summed[5],
        summed[6],
        summed[7],
        summed[8],
        summed[9],
    )


BF16 = jnp.bfloat16
F32 = jnp.float32
LOG2_E = 1.4426950408889634
VMEM_BYTES = 58 * 1024 * 1024
META_ROWS = 4
SLOT_ROWS = 64
EXACT_BASE = 256
TOKEN_TILE = 256
ANY_SPEC = pl.BlockSpec(memory_space=pl.ANY)


def dot_nn(left, right):
    return lax.dot_general(left, right, (((1,), (0,)), ((), ())), preferred_element_type=F32)


def dot_nt(left, right):
    return lax.dot_general(left, right, (((1,), (1,)), ((), ())), preferred_element_type=F32)


def dot_tn(left, right):
    return lax.dot_general(left, right, (((0,), (0,)), ((), ())), preferred_element_type=F32)


def head_operands(queries, keys, head, length):
    lane = lax.broadcasted_iota(jnp.int32, queries.shape, 1)
    row = lax.broadcasted_iota(jnp.int32, queries.shape, 0)
    mine = (lane // HEAD_DIM) == head
    spare = lane == (1 - head) * HEAD_DIM
    zero = jnp.zeros_like(queries)
    fill = jnp.where(row >= length, jnp.full_like(queries, NEG_FILL), zero)
    one_query = jnp.where(mine, queries, jnp.where(spare, jnp.ones_like(queries), zero))
    one_key = jnp.where(mine, keys, jnp.where(spare, fill, zero))
    return mine, one_query, one_key


def attend_kernel(length_ref, q_ref, k_ref, v_ref, out_ref, lse_ref):
    length = length_ref[0]
    factor = LOG2_E * HEAD_DIM**-0.5
    rows = []
    for head in range(2):
        mine, one_query, one_key = head_operands(q_ref[...], k_ref[...], head, length)
        value_one = jnp.where(mine, v_ref[...], jnp.ones_like(v_ref[...]))
        scores = dot_nt(one_key, one_query)
        top = jnp.max(scores, axis=0, keepdims=True)
        weights = jnp.exp2(scores * factor - top * factor).astype(BF16)
        mixed = dot_tn(value_one, weights)
        other = (1 - head) * HEAD_DIM
        total = mixed[other : other + 1]
        lse_ref[0, head : head + 1, :] = top * factor + jnp.log2(total)
        rows.append(mixed[head * HEAD_DIM : (head + 1) * HEAD_DIM] * (1.0 / total))
    out_ref[...] = jnp.transpose(jnp.concatenate(rows, axis=0), (1, 0)).astype(BF16)


def attend_back_kernel(
    length_ref, q_ref, k_ref, v_ref, out_ref, grad_ref, lse_ref, dq_ref, dk_ref, dv_ref, *, chunk
):
    length = length_ref[0]
    positions = q_ref.shape[0]
    factor = LOG2_E * HEAD_DIM**-0.5
    scale = HEAD_DIM**-0.5
    grad = grad_ref[...]
    product = grad.astype(F32) * out_ref[...].astype(F32)
    high = product.astype(BF16)
    low = (product - high.astype(F32)).astype(BF16)
    head_of_lane = lax.broadcasted_iota(jnp.int32, (16, 2 * HEAD_DIM), 1) // HEAD_DIM
    picker = jnp.where(
        head_of_lane == lax.broadcasted_iota(jnp.int32, (16, 2 * HEAD_DIM), 0), 1.0, 0.0
    ).astype(BF16)
    delta = dot_nt(picker, high) + dot_nt(picker, low)
    query_rows = []
    key_parts = ([], [])
    value_parts = ([], [])
    for head in range(2):
        mine, one_query, one_key = head_operands(q_ref[...], k_ref[...], head, length)
        one_value = jnp.where(mine, v_ref[...], jnp.zeros_like(v_ref[...]))
        lse = lse_ref[0, head : head + 1, :]
        row_delta = delta[head : head + 1, :]
        query_grad = jnp.zeros((2 * HEAD_DIM, positions), F32)
        for start in range(0, positions, chunk):
            span = slice(start, start + chunk)
            weights = jnp.exp2(dot_nt(one_key[span], one_query) * factor - lse)
            weight_grad = dot_nt(one_value[span], grad)
            score_grad = (weights * (weight_grad - row_delta)).astype(BF16)
            value_parts[head].append(dot_nn(weights.astype(BF16), grad))
            key_parts[head].append(dot_nn(score_grad, q_ref[...]))
            query_grad = query_grad + dot_tn(k_ref[span, :], score_grad)
        query_rows.append(query_grad[head * HEAD_DIM : (head + 1) * HEAD_DIM])
    first = lax.broadcasted_iota(jnp.int32, (chunk, 2 * HEAD_DIM), 1) < HEAD_DIM
    for part, start in enumerate(range(0, positions, chunk)):
        span = slice(start, start + chunk)
        dk_ref[span, :] = (jnp.where(first, key_parts[0][part], key_parts[1][part]) * scale).astype(BF16)
        dv_ref[span, :] = jnp.where(first, value_parts[0][part], value_parts[1][part]).astype(BF16)
    dq_ref[...] = jnp.transpose(jnp.concatenate(query_rows, axis=0) * scale, (1, 0)).astype(BF16)


def gelu_with_slope(values):
    root = math.sqrt(2.0 / math.pi)
    square = values * values
    share = 0.5 + 0.5 * jnp.tanh(values * (root + root * 0.044715 * square))
    result = values * share
    slope = share + (result - result * share) * (2.0 * root + 6.0 * root * 0.044715 * square)
    return result, slope


def swap_core(value):
    return lax.ppermute(value, "blk", [(0, 1), (1, 0)])


def join_halves(core, own, other):
    first = jnp.where(core == 0, own, other)
    second = jnp.where(core == 0, other, own)
    return jnp.concatenate([first, second], axis=0)


def to_whole(core, local):
    own = lax.dynamic_index_in_dim(local, core, 0, keepdims=False)
    away = lax.dynamic_index_in_dim(local, 1 - core, 0, keepdims=False)
    return join_halves(core, own, swap_core(away))


def fill_other(core, value, arrived):
    return lax.dynamic_update_index_in_dim(value, arrived, 1 - core, 0)


COST_SHARE = 0.3


def kernel_cost(microseconds):
    flops = int(COST_SHARE * microseconds * 1e9)
    return pl.CostEstimate(flops=flops, bytes_accessed=1024, transcendentals=0)


def run_kernel(
    body, grid, scalars, inputs, in_specs, out_specs, out_shape, microseconds, name, scratch=(), carried=()
):
    scalar_count, input_count, output_count = len(scalars), len(inputs), len(out_shape)
    carried_count = len(carried)
    first_carried = scalar_count + input_count

    def kernel(*refs):
        rest = refs[first_carried + carried_count :]
        body(*refs[:first_carried], *rest[:output_count], *rest[output_count + carried_count :])

    results = pl.pallas_call(
        kernel,
        grid_spec=pltpu.PrefetchScalarGridSpec(
            num_scalar_prefetch=scalar_count,
            grid=grid,
            in_specs=list(in_specs) + [ANY_SPEC] * carried_count,
            out_specs=list(out_specs) + [ANY_SPEC] * carried_count,
            scratch_shapes=list(scratch),
        ),
        out_shape=list(out_shape) + [jax.ShapeDtypeStruct(c.shape, c.dtype) for c in carried],
        input_output_aliases={first_carried + i: output_count + i for i in range(carried_count)},
        compiler_params=pltpu.CompilerParams(vmem_limit_bytes=VMEM_BYTES),
        cost_estimate=kernel_cost(microseconds),
        name=name,
    )(*scalars, *inputs, *carried)
    return results[:output_count], results[output_count:]


def behind(*arrays):
    def kernel(*refs):
        pass

    return pl.pallas_call(
        kernel,
        in_specs=[ANY_SPEC] * len(arrays),
        out_specs=[ANY_SPEC] * len(arrays),
        out_shape=[jax.ShapeDtypeStruct(a.shape, a.dtype) for a in arrays],
        input_output_aliases={i: i for i in range(len(arrays))},
        compiler_params=pltpu.CompilerParams(vmem_limit_bytes=VMEM_BYTES),
        cost_estimate=kernel_cost(1),
        name="behind",
    )(*arrays)


FEED_TILE = 512


def shaped(dtype, *shape):
    return jax.ShapeDtypeStruct(shape, dtype)


def row_spec(tile, columns):
    return pl.BlockSpec((tile, columns), lambda i, *scalars: (i, 0))


def fixed_spec(*shape):
    return pl.BlockSpec(shape, lambda *grid: (0,) * len(shape))


def attend(length, qkv):
    positions = qkv.shape[0]
    pairs = HEADS // 2

    def spec(group):
        return pl.BlockSpec((positions, 2 * HEAD_DIM), lambda pair, length: (0, group * pairs + pair))

    results, _ = run_kernel(
        attend_kernel,
        (pairs,),
        [length],
        [qkv, qkv, qkv],
        [spec(0), spec(1), spec(2)],
        [spec(0), pl.BlockSpec((1, 2, positions), lambda pair, length: (pair, 0, 0))],
        [shaped(BF16, positions, D), shaped(F32, pairs, 2, positions)],
        30,
        "attend",
    )
    return results


def attend_back(length, qkv, attended, grad_att, lse, part, parts, grads, carried):
    positions = qkv.shape[0]
    pairs = HEADS // 2
    count = pairs // parts
    shift = part * count

    def spec(group):
        return pl.BlockSpec(
            (positions, 2 * HEAD_DIM), lambda pair, length: (0, group * pairs + shift + pair)
        )

    lse_spec = pl.BlockSpec((1, 2, positions), lambda pair, length: (shift + pair, 0, 0))
    inputs = [qkv, qkv, qkv, attended, grad_att, lse]
    held = len(grads)
    kept = len(carried)

    def kernel(*refs):
        attend_back_kernel(*refs[:7], *refs[7 + held + kept : 10 + held + kept], chunk=min(512, positions))

    aliases = {7 + i: i for i in range(held)}
    aliases.update({7 + held + i: 3 + i for i in range(kept)})
    results = pl.pallas_call(
        kernel,
        grid_spec=pltpu.PrefetchScalarGridSpec(
            num_scalar_prefetch=1,
            grid=(count,),
            in_specs=[spec(0), spec(1), spec(2), spec(0), spec(0), lse_spec] + [ANY_SPEC] * (held + kept),
            out_specs=[spec(0)] * 3 + [ANY_SPEC] * kept,
        ),
        out_shape=[shaped(BF16, positions, D)] * 3 + [jax.ShapeDtypeStruct(c.shape, c.dtype) for c in carried],
        input_output_aliases=aliases,
        compiler_params=pltpu.CompilerParams(vmem_limit_bytes=VMEM_BYTES),
        cost_estimate=kernel_cost(46 / parts),
        name="attend_back",
    )(length, *inputs, *grads, *carried)
    return results[:3], results[3:]


def norm_rows(features):
    center = features - jnp.mean(features, axis=-1, keepdims=True)
    rstd = lax.rsqrt(jnp.mean(center * center, axis=-1, keepdims=True) + 1e-05)
    return center * rstd, rstd


def norm_rows_back(grad_norm, xhat, rstd, gain_row):
    scaled = grad_norm * gain_row
    mean_scaled = jnp.mean(scaled, axis=-1, keepdims=True)
    mean_cross = jnp.mean(scaled * xhat, axis=-1, keepdims=True)
    return rstd * (scaled - mean_scaled - xhat * mean_cross)


def add_column_sums(sums_ref, grad_norm, xhat):
    sums_ref[0:1, :] += jnp.sum(grad_norm * xhat, axis=0, keepdims=True)
    sums_ref[1:2, :] += jnp.sum(grad_norm, axis=0, keepdims=True)


def split_specs(count, tile):
    steps = count // tile // 2

    def early(i):
        return jnp.minimum(i, steps - 1)

    def late(i):
        return jnp.maximum(i - steps, 0)

    def own(i, *scalars):
        core = scalars[-1][0]
        return core, jnp.where(core == 0, early(i), late(i)), 0

    def other(i, *scalars):
        return jnp.where(scalars[-1][0] == 0, late(i), early(i)), 0

    return [pl.BlockSpec((1, tile, D), own), pl.BlockSpec((tile, D), other)]


def store_split(core, own_ref, other_ref, value):
    half = pl.program_id(0) * 2 // pl.num_programs(0)

    @pl.when(half == core)
    def _():
        own_ref[0] = value

    @pl.when(half != core)
    def _():
        other_ref[...] = value


def valid_column(length, tile):
    row = lax.broadcasted_iota(jnp.int32, (tile, 1), 0) + pl.program_id(0) * tile
    return row < length


def share_out(core, value, keep_ref, away_ref):
    rows = keep_ref.shape[-2]
    if len(keep_ref.shape) == 4:
        outer, inner = keep_ref.shape[:2]
        value = value.astype(BF16).reshape(outer, inner, 2, rows, value.shape[1])
        first, second = value[:, :, 0], value[:, :, 1]
        keep_ref[...] = jnp.where(core == 0, first, second)
        away_ref[...] = jnp.where(core == 0, second, first)
        return
    groups = keep_ref.shape[0]
    value = value.astype(BF16).reshape(groups, 2, rows, value.shape[1])
    first, second = value[:, 0], value[:, 1]
    keep_ref[...] = jnp.where(core == 0, first, second)
    away_ref[...] = jnp.where(core == 0, second, first)


def embed_kernel(emb_ref, we_ref, gain_ref, shift_ref, wqkv_ref, low_ref, in_ref, attn_ref, qkv_ref):
    rows = emb_ref[...].astype(F32)
    normed = rows * lax.rsqrt(jnp.mean(rows * rows, axis=-1, keepdims=True) + 1e-06)
    low = normed.astype(BF16)
    low_ref[...] = low
    inputs = dot_nn(low, we_ref[...])
    in_ref[...] = inputs.astype(BF16)
    xhat, _ = norm_rows(inputs)
    attn = (xhat * gain_ref[...] + shift_ref[...]).astype(BF16)
    attn_ref[...] = attn
    qkv_ref[...] = dot_nn(attn, wqkv_ref[...]).astype(BF16)


def embed_and_project(emb, w_embed, gain_row, shift_row, w_qkv):
    count = emb.shape[0]
    tile = TOKEN_TILE
    results, _ = run_kernel(
        embed_kernel,
        (count // tile,),
        [],
        [emb, w_embed, gain_row, shift_row, w_qkv],
        [row_spec(tile, EMB), fixed_spec(EMB, D), fixed_spec(1, D), fixed_spec(1, D), fixed_spec(D, 3 * D)],
        [row_spec(tile, EMB), row_spec(tile, D), row_spec(tile, D), row_spec(tile, 3 * D)],
        [shaped(BF16, count, EMB), shaped(BF16, count, D), shaped(BF16, count, D), shaped(BF16, count, 3 * D)],
        12,
        "embed_and_project",
    )
    return results


def residual_kernel(
    length_ref, core_ref, att_ref, in_ref, wo_ref, gain_ref, shift_ref, cot_ref, cot_other_ref,
    res_ref, mlp_ref, fin_ref
):
    residual = in_ref[...].astype(F32) + dot_nn(att_ref[...], wo_ref[...])
    res_ref[...] = residual.astype(BF16)
    xhat, _ = norm_rows(residual)
    mlp_ref[...] = (xhat * gain_ref[...] + shift_ref[...]).astype(BF16)
    half = pl.program_id(0) * 2 // pl.num_programs(0)
    cot = jnp.where(half == core_ref[0], cot_ref[0], cot_other_ref[...])
    fin_ref[...] = jnp.where(valid_column(length_ref[0], cot.shape[0]), cot, jnp.zeros_like(cot))


def attention_residual(length, core, attended, inputs, w_out, gain_row, shift_row, cot, cot_other):
    count = attended.shape[0]
    row = row_spec(TOKEN_TILE, D)
    results, _ = run_kernel(
        residual_kernel,
        (count // TOKEN_TILE,),
        [length, core],
        [attended, inputs, w_out, gain_row, shift_row, cot, cot_other],
        [row, row, fixed_spec(D, D), fixed_spec(1, D), fixed_spec(1, D)] + split_specs(count, TOKEN_TILE),
        [row, row, row],
        [shaped(BF16, count, D)] * 3,
        8,
        "attention_residual",
    )
    return results


def feed_forward_kernel(
    core_ref, mlp_ref, fin_ref, wu_ref, wd_ref, down_in_ref, grad_in_ref,
    gwd_keep_ref, gwd_away_ref, gwu_keep_ref, gwu_away_ref, down_ref, grad_ref,
    fin_t_ref, hid_ref, pre_ref, *, first
):
    core = core_ref[0]
    count = mlp_ref.shape[0]

    @pl.when(pl.program_id(0) == 0)
    def _():
        fin_t_ref[...] = jnp.transpose(fin_ref[...], (1, 0))
        if first:
            down_ref[...] = jnp.zeros_like(down_ref)
            grad_ref[...] = jnp.zeros_like(grad_ref)
        else:
            down_ref[...] = down_in_ref[...]
            grad_ref[...] = grad_in_ref[...]

    for start in range(0, count, FEED_TILE):
        span = slice(start, start + FEED_TILE)
        hidden, slope = gelu_with_slope(dot_nn(mlp_ref[span, :], wu_ref[...]))
        hid_ref[span, :] = hidden.astype(BF16)
        pre_ref[span, :] = (dot_nt(fin_ref[span, :], wd_ref[...]) * slope).astype(BF16)
    share_out(core, dot_nn(fin_t_ref[...], hid_ref[...]), gwd_keep_ref, gwd_away_ref)
    share_out(core, dot_tn(pre_ref[...], mlp_ref[...]), gwu_keep_ref, gwu_away_ref)
    for start in range(0, count, FEED_TILE):
        span = slice(start, start + FEED_TILE)
        down_ref[span, :] += dot_nn(hid_ref[span, :], wd_ref[...])
        grad_ref[span, :] += dot_nt(pre_ref[span, :], wu_ref[...])


def feed_forward(core, groups, part, parts, mlp_low, final_low, w_up, w_down, down, grad, carried, tile=512):
    count = mlp_low.shape[0]
    width = w_up.shape[1] // parts
    steps = width // tile
    shift = part * steps
    first = down is None
    if first:
        down = grad = jnp.zeros((8, 128), F32)
    down_rows = D // (2 * groups)
    up_rows = w_up.shape[1] // (2 * groups)
    down_share = (groups // 4, 4, down_rows)
    down_spec = pl.BlockSpec((*down_share, tile), lambda j, core: (0, 0, 0, j))
    up_spec = pl.BlockSpec((tile // (2 * up_rows), up_rows, D), lambda j, core: (j, 0, 0))
    whole = fixed_spec(count, D)
    return run_kernel(
        functools.partial(feed_forward_kernel, first=first),
        (steps,),
        [core],
        [mlp_low, final_low, w_up, w_down, down, grad],
        [
            whole,
            whole,
            pl.BlockSpec((D, tile), lambda j, core: (0, shift + j)),
            pl.BlockSpec((tile, D), lambda j, core: (shift + j, 0)),
            fixed_spec(*down.shape),
            fixed_spec(*down.shape),
        ],
        [down_spec, down_spec, up_spec, up_spec, whole, whole],
        [shaped(BF16, *down_share, width)] * 2
        + [shaped(BF16, groups // parts, up_rows, D)] * 2
        + [shaped(F32, count, D)] * 2,
        36,
        "feed_forward",
        scratch=[pltpu.VMEM((D, count), BF16), pltpu.VMEM((count, tile), BF16), pltpu.VMEM((count, tile), BF16)],
        carried=carried,
    )


def middle_kernel(
    length_ref, core_ref, down_ref, gmn_ref, res_ref, fin_ref, gain_ref, wo_ref, att_ref,
    out_ref, out_away_ref, low_ref, gatt_ref, gwo_keep_ref, gwo_away_ref, sums_ref, acc_ref
):
    step = pl.program_id(0)

    @pl.when(step == 0)
    def _():
        sums_ref[...] = jnp.zeros_like(sums_ref)
        acc_ref[...] = jnp.zeros_like(acc_ref)

    residual = res_ref[...].astype(F32)
    keep = valid_column(length_ref[0], residual.shape[0])
    final = jnp.where(keep, residual + down_ref[...], 0.0).astype(BF16)
    store_split(core_ref[0], out_ref, out_away_ref, final)
    xhat, rstd = norm_rows(residual)
    grad = gmn_ref[...]
    add_column_sums(sums_ref, grad, xhat)
    low = (fin_ref[...].astype(F32) + norm_rows_back(grad, xhat, rstd, gain_ref[...])).astype(BF16)
    low_ref[...] = low
    gatt_ref[...] = dot_nt(low, wo_ref[...]).astype(BF16)
    acc_ref[...] += dot_tn(low, att_ref[...])

    @pl.when(step == pl.num_programs(0) - 1)
    def _():
        share_out(core_ref[0], acc_ref[...], gwo_keep_ref, gwo_away_ref)


def feed_forward_to_attention(
    length, core, groups, down, grad_mlp_norm, residual, final_low, gain_row, w_out, attended, carried
):
    count = residual.shape[0]
    row = row_spec(TOKEN_TILE, D)
    share = (groups // 4, 4, D // (2 * groups), D)
    return run_kernel(
        middle_kernel,
        (count // TOKEN_TILE,),
        [length, core],
        [down, grad_mlp_norm, residual, final_low, gain_row, w_out, attended],
        [row, row, row, row, fixed_spec(1, D), fixed_spec(D, D), row],
        split_specs(count, TOKEN_TILE) + [row, row, fixed_spec(*share), fixed_spec(*share), fixed_spec(8, D)],
        [shaped(BF16, 2, count // 2, D), shaped(BF16, count // 2, D)] + [shaped(BF16, count, D)] * 2 + [shaped(BF16, *share)] * 2 + [shaped(F32, 8, D)],
        15,
        "feed_forward_to_attention",
        scratch=[pltpu.VMEM((D, D), F32)],
        carried=carried,
    )


def outer_kernel(core_ref, dq_ref, dk_ref, dv_ref, right_ref, keep_ref, away_ref, all_ref):
    right = right_ref[...]
    for group, ref in enumerate((dq_ref, dk_ref, dv_ref)):
        for start in range(0, D, TOKEN_TILE):
            rows = slice(group * D + start, group * D + start + TOKEN_TILE)
            all_ref[rows, :] = dot_tn(ref[:, start : start + TOKEN_TILE], right).astype(BF16)
    share_out(core_ref[0], all_ref[...], keep_ref, away_ref)


def outer_qkv(core, groups, grads, right, half, carried):
    count = right.shape[0]
    columns = right.shape[1] // 2
    share = (groups, 3 * D // (2 * groups), columns)
    return run_kernel(
        outer_kernel,
        (1,),
        [core],
        [*grads, right],
        [fixed_spec(count, D)] * 3 + [pl.BlockSpec((count, columns), lambda i, core: (0, half))],
        [fixed_spec(*share)] * 2,
        [shaped(BF16, *share)] * 2,
        8,
        "outer_qkv",
        scratch=[pltpu.VMEM((3 * D, columns), BF16)],
        carried=carried,
    )


def input_kernel(
    core_ref, dq_ref, dk_ref, dv_ref, wqkv_ref, in_ref, low_ref, gain_ref, we_ref, emb_ref, nl_ref,
    grad_ref, grad_away_ref, rows_ref, gwe_keep_ref, gwe_away_ref, sums_ref, acc_ref
):
    step = pl.program_id(0)

    @pl.when(step == 0)
    def _():
        sums_ref[...] = jnp.zeros_like(sums_ref)
        acc_ref[...] = jnp.zeros_like(acc_ref)

    grad = (
        dot_nt(dq_ref[...], wqkv_ref[:, :D])
        + dot_nt(dk_ref[...], wqkv_ref[:, D : 2 * D])
        + dot_nt(dv_ref[...], wqkv_ref[:, 2 * D :])
    )
    xhat, rstd = norm_rows(in_ref[...].astype(F32))
    add_column_sums(sums_ref, grad, xhat)
    low = (low_ref[...].astype(F32) + norm_rows_back(grad, xhat, rstd, gain_ref[...])).astype(BF16)
    store_split(core_ref[0], grad_ref, grad_away_ref, low)
    acc_ref[...] += dot_tn(low, nl_ref[...])
    back = dot_nt(low, we_ref[...])
    emb = emb_ref[...].astype(F32)
    emb_rstd = lax.rsqrt(jnp.mean(emb * emb, axis=-1, keepdims=True) + 1e-06)
    normed = emb * emb_rstd
    rows_ref[...] = (emb_rstd * (back - normed * jnp.mean(normed * back, axis=-1, keepdims=True))).astype(BF16)

    @pl.when(step == pl.num_programs(0) - 1)
    def _():
        share_out(core_ref[0], acc_ref[...], gwe_keep_ref, gwe_away_ref)


def input_gradient(core, groups, grads, w_qkv, inputs, residual_low, gain_row, w_embed, emb, normed_low, carried):
    count = inputs.shape[0]
    tile = TOKEN_TILE
    share = (2 * groups, D // (4 * groups), EMB)
    row, narrow = row_spec(tile, D), row_spec(tile, EMB)
    return run_kernel(
        input_kernel,
        (count // tile,),
        [core],
        [*grads, w_qkv, inputs, residual_low, gain_row, w_embed, emb, normed_low],
        [row, row, row, fixed_spec(D, 3 * D), row, row, fixed_spec(1, D), fixed_spec(EMB, D), narrow, narrow],
        split_specs(count, tile) + [narrow, fixed_spec(*share), fixed_spec(*share), fixed_spec(8, D)],
        [shaped(BF16, 2, count // 2, D), shaped(BF16, count // 2, D), shaped(BF16, count, EMB)] + [shaped(BF16, *share)] * 2 + [shaped(F32, 8, D)],
        16,
        "input_gradient",
        scratch=[pltpu.VMEM((D, EMB), F32)],
        carried=carried,
    )


def exchange(value, bit, dp_bits, pattern=1):
    return lax.ppermute(value, "dp", [(i, i ^ (pattern << bit)) for i in range(1 << dp_bits)])


class Halving:
    def __init__(self, labels, dp_bits, flat):
        self.labels = list(labels)
        self.flat = flat
        self.dp_bits = dp_bits
        self.terms = []
        self.fixed = {}

    def over_cores(self, keep, away):
        labels = tuple(self.labels)
        shape = keep.shape if self.flat else (2,) * len(labels) + keep.shape[1:]
        self.terms = [(keep.reshape(shape), labels), (swap_core(away).reshape(shape), labels)]

    @property
    def keep(self):
        return self.terms[0][0]

    @keep.setter
    def keep(self, value):
        self.terms[0] = (value, self.terms[0][1])

    def part(self, fixed):
        total = 0.0
        for value, labels in self.terms:
            spans = [label not in fixed for label in labels]
            starts = [0 if span else fixed[label] for span, label in zip(spans, labels)] + [0, 0]
            sizes = [2 if span else 1 for span in spans] + list(value.shape[-2:])
            piece = lax.dynamic_slice(value.reshape((2,) * len(labels) + value.shape[-2:]), starts, sizes)
            left = (-1,) if self.flat else (2,) * sum(spans)
            total = total + piece.reshape(left + value.shape[-2:]).astype(F32)
        return total

    def total(self):
        return self.part(self.fixed)

    def away(self, bit_label):
        bit = (lax.axis_index("dp") >> bit_label) & 1
        return self.part({**self.fixed, bit_label: 1 - bit}).astype(BF16)

    def send(self, bit_label, away):
        self.fixed[bit_label] = (lax.axis_index("dp") >> bit_label) & 1
        labels = tuple(label for label in self.labels if label not in self.fixed)
        self.terms.append((exchange(away, bit_label, self.dp_bits), labels))


def between_planes(value, dp_bits):
    plane = lax.axis_index("dp") >> 2
    parts = [lax.dynamic_index_in_dim(value, plane, 0, keepdims=False)]
    for step in range(1, value.shape[0]):
        away = lax.dynamic_index_in_dim(value, plane ^ step, 0, keepdims=False)
        parts.append(exchange(away, 2, dp_bits, step))
    return parts


def whole_sequence_shards(
    token_ids,
    seq_lengths,
    diffusion_time,
    embed_table,
    w_embed,
    w_time,
    gain_attn,
    bias_attn,
    gain_mlp,
    bias_mlp,
    w_qkv,
    w_out,
    w_up,
    w_down,
    cotangent,
):
    core = lax.axis_index("blk")
    cores = core.reshape(1).astype(jnp.int32)
    groups = lax.axis_size("dp")
    devices = 2 * groups
    dp_bits = groups.bit_length() - 1
    everywhere = ("dp", "blk")
    labels = list(reversed(range(dp_bits)))
    planes = [[4 * high + low for low in range(4)] for high in range(groups // 4)]
    lines = [[4 * high + low for high in range(groups // 4)] for low in range(4)]
    ids = to_whole(core, token_ids)
    cot_other = swap_core(lax.dynamic_index_in_dim(cotangent, 1 - core, 0, keepdims=False))
    positions = ids.shape[0]
    length = lax.dynamic_index_in_dim(seq_lengths, core, 0, keepdims=True)
    time = lax.dynamic_index_in_dim(diffusion_time, core, 0, keepdims=True)
    emb = embed_table[ids]

    valid = jnp.arange(positions, dtype=jnp.int32) < length[0]
    row_count = VOCAB // devices
    owner = jnp.where(valid, ids // row_count, -1)
    offset = ids % row_count
    slots = SLOT_ROWS - META_ROWS
    member = owner[:, None] == jnp.arange(devices, dtype=jnp.int32)[None, :]
    earlier = jnp.arange(positions)[:, None] > jnp.arange(positions)[None, :]
    before = dot_nn(earlier.astype(BF16), member.astype(BF16))
    rank = jnp.sum(jnp.where(member, before, 0.0), axis=1).astype(jnp.int32)
    most = jnp.max(jnp.sum(member.astype(jnp.int32), axis=0))
    offset_digits = jnp.stack(
        [(offset // EXACT_BASE).astype(BF16), (offset % EXACT_BASE).astype(BF16), jnp.ones(positions, BF16)],
        axis=1,
    )

    def dispatch(turn):
        slot = rank - turn * slots
        inside = (owner >= 0) & (slot >= 0) & (slot < slots)
        target = jnp.where(inside, owner * SLOT_ROWS + META_ROWS + slot, -1)
        place = jnp.arange(devices * SLOT_ROWS, dtype=jnp.int32)[:, None] == target[None, :]
        digits = dot_nn(place.astype(BF16), offset_digits).reshape(devices, SLOT_ROWS, 3)
        head = jnp.transpose(digits, (0, 2, 1)).reshape(devices, 1, 3 * SLOT_ROWS)
        peak = jnp.stack([most // EXACT_BASE, most % EXACT_BASE]).astype(F32)
        peak = jnp.broadcast_to(peak, (devices, 1, 2))
        gap = jnp.zeros((devices, 1, EMB - 3 * SLOT_ROWS - 2), F32)
        return target, jnp.concatenate([head, peak, gap], axis=2)

    meta_target = jnp.arange(devices * META_ROWS, dtype=jnp.int32)
    meta_target = meta_target // META_ROWS * SLOT_ROWS + meta_target % META_ROWS

    def packed(target, meta, grads):
        meta = meta.astype(BF16).reshape(devices * META_ROWS, EMB)
        target = jnp.concatenate([target, meta_target])
        place = jnp.arange(devices * SLOT_ROWS, dtype=jnp.int32)[:, None] == target[None, :]
        rows = dot_nn(place.astype(BF16), jnp.concatenate([grads, meta]))
        return rows.astype(BF16).reshape(devices, SLOT_ROWS, EMB)

    def deliver(rows):
        return lax.all_to_all(rows, everywhere, 0, 0, tiled=True)

    def collect(rows):
        head = rows[:, 0].astype(F32)
        high, low, used = (head[:, i * SLOT_ROWS : (i + 1) * SLOT_ROWS] for i in range(3))
        row = jnp.where(used > 0.5, high * EXACT_BASE + low, -1.0).astype(jnp.int32)
        row = jnp.pad(row, ((0, 0), (0, rows.shape[1] - SLOT_ROWS)), constant_values=-1)
        hit = jnp.arange(row_count, dtype=jnp.int32)[:, None] == row.reshape(1, -1)
        return dot_nn(hit.astype(BF16), rows.reshape(-1, EMB))

    first_target, first_head = dispatch(0)

    def over_cores(keep, arrived):
        return (keep.astype(F32) + arrived.astype(F32)).astype(BF16)

    def scattered(value, index_groups):
        return lax.psum_scatter(value, "dp", scatter_dimension=0, axis_index_groups=index_groups, tiled=True)[0]

    time_low = time_features(time, TIME_WIDTH).astype(BF16)
    modulation = dot_nn(time_low, w_time)
    scale_attn, shift_attn, scale_mlp, shift_mlp = jnp.split(modulation, 4, axis=1)
    gain_row_attn = gain_attn + scale_attn
    gain_row_mlp = gain_mlp + scale_mlp
    normed_low, inputs, attn_low, qkv = embed_and_project(
        emb, w_embed, gain_row_attn, bias_attn + shift_attn, w_qkv
    )
    attended, lse = attend(length, qkv)
    residual, mlp_low, final_low = attention_residual(
        length, cores, attended, inputs, w_out, gain_row_mlp, bias_mlp + shift_mlp, cotangent, cot_other
    )

    hidden_width = w_up.shape[1]
    feed = functools.partial(feed_forward, cores, groups)
    (keep_d, away_d, keep_u, away_u, down, grad), _ = feed(
        0, 2, mlp_low, final_low, w_up, w_down, None, None, []
    )
    up_0, up_1 = Halving(labels[1:], dp_bits, True), Halving(labels[1:], dp_bits, True)
    qkv_a, qkv_b = Halving(labels, dp_bits, False), Halving(labels, dp_bits, False)
    up_0.over_cores(keep_u, away_u)
    arrived_d = swap_core(away_d)
    (next_keep, next_away, keep_u, away_u, down, grad), (up_0.keep, keep_d) = feed(
        1, 2, mlp_low, final_low, w_up, w_down, down, grad, [up_0.keep, keep_d]
    )
    away, down_0, next_keep, next_away, keep_u, away_u = behind(
        up_0.away(0), over_cores(keep_d, arrived_d), next_keep, next_away, keep_u, away_u
    )
    up_0.send(0, away)
    up_1.over_cores(keep_u, away_u)
    arrived_d = swap_core(next_away)
    down_0 = scattered(down_0, lines)
    (layer_out, layer_away, residual_low, grad_att, keep_o, away_o, sums_mlp), kept = feed_forward_to_attention(
        length, cores, groups, down, grad, residual, final_low, gain_row_mlp, w_out, attended,
        [up_0.keep, up_1.keep, next_keep],
    )
    up_0.keep, up_1.keep, keep_d = kept
    away_0, away_1, down_1, keep_o, away_o = behind(
        up_0.away(1), up_1.away(0), over_cores(keep_d, arrived_d), keep_o, away_o
    )
    up_0.send(1, away_0)
    up_1.send(0, away_1)
    down_1 = scattered(down_1, lines)
    arrived_o = swap_core(away_o)
    back = functools.partial(attend_back, length, qkv, attended, grad_att, lse)
    grads, (up_0.keep, up_1.keep, keep_o) = back(0, 2, [], [up_0.keep, up_1.keep, keep_o])
    away_1, out_sum, up_first = behind(
        up_1.away(1), over_cores(keep_o, arrived_o), up_0.total().astype(BF16)
    )
    up_1.send(1, away_1)
    out_sum = scattered(out_sum, lines)
    grads, (up_1.keep, up_first, down_0) = back(1, 2, grads, [up_1.keep, up_first, down_0])
    up_rows = [up_first, up_1.total().astype(BF16)]
    up_rows = jnp.concatenate(up_rows)
    up_sum = scattered(up_rows, lines)
    (keep_a, away_a), (down_1,) = outer_qkv(cores, groups, grads, attn_low, 0, [down_1])
    keep_a, away_a = behind(keep_a, away_a)
    qkv_a.over_cores(keep_a, away_a)
    orders = [(0, 1), (1, 0)]
    (keep_b, away_b), (qkv_a.keep, down_1) = outer_qkv(
        cores, groups, grads, attn_low, 1, [qkv_a.keep, down_1]
    )
    in_plane = jnp.concatenate([down_0, down_1, out_sum], axis=2)
    away_a, keep_b, away_b, in_plane = behind(qkv_a.away(orders[0][0]), keep_b, away_b, in_plane)
    own_sum = scattered(in_plane, planes)
    qkv_a.send(orders[0][0], away_a)
    qkv_b.over_cores(keep_b, away_b)
    qkv_b.send(orders[1][0], *behind(qkv_b.away(orders[1][0])))
    (grad_input, input_away, grad_rows, keep_e, away_e, sums_attn), kept = input_gradient(
        cores, groups, grads, w_qkv, inputs, residual_low, gain_row_attn, w_embed, emb, normed_low,
        [qkv_a.keep, qkv_b.keep],
    )
    qkv_a.keep, qkv_b.keep = kept

    grad_modulation = jnp.concatenate([sums_attn[0], sums_attn[1], sums_mlp[0], sums_mlp[1]])
    gain_columns = jnp.transpose(grad_modulation.reshape(4, devices, -1), (1, 0, 2)).reshape(devices, -1)
    mod_rows = jnp.concatenate([grad_modulation.reshape(devices, -1), gain_columns], axis=1)
    mod_high = mod_rows.astype(BF16).astype(F32)
    mod_low = mod_rows - mod_high
    time_rows = jnp.broadcast_to(time_low.astype(F32), (devices, TIME_WIDTH))
    first_meta = jnp.concatenate(
        [first_head, jnp.stack([mod_high, mod_low, time_rows], axis=1)], axis=1
    )
    embed_rows = over_cores(keep_e, swap_core(away_e))
    payload = jnp.concatenate([packed(first_target, first_meta, grad_rows), embed_rows], axis=1)
    payload, away_a, away_b, up_sum, layer_away, input_away = behind(
        payload, qkv_a.away(orders[0][1]), qkv_b.away(orders[1][1]), up_sum, layer_away, input_away
    )
    arrived = deliver(payload)
    qkv_a.send(orders[0][1], away_a)
    qkv_b.send(orders[1][1], away_b)
    qkv_rows = jnp.concatenate([qkv_a.total(), qkv_b.total()], axis=-1).astype(BF16)
    qkv_rows = qkv_rows.reshape((-1,) + qkv_rows.shape[-2:])
    layer_out = fill_other(core, layer_out, swap_core(layer_away))
    grad_w_qkv = sum(part.astype(F32) for part in between_planes(qkv_rows, dp_bits))
    embed_sum = arrived[:, SLOT_ROWS:].astype(F32).reshape(groups, -1, EMB)
    embed_sum = jnp.sum(embed_sum, axis=0)
    grad_input = fill_other(core, grad_input, swap_core(input_away))
    grad_table = collect(arrived)
    sums = arrived[:, 1].astype(F32) + arrived[:, 2].astype(F32)
    time_width = sums.shape[1] // 2
    grad_w_time = lax.dot_general(
        arrived[:, 3].astype(F32),
        sums[:, :time_width],
        (((0,), (0,)), ((), ())),
        precision=lax.Precision.HIGHEST,
    )
    gain_sums = jnp.sum(sums[:, time_width:], axis=0).reshape(4, -1)
    peaks = arrived[:, 0, 3 * SLOT_ROWS : 3 * SLOT_ROWS + 2].astype(F32)
    peak = jnp.max(peaks[:, 0] * EXACT_BASE + peaks[:, 1]).astype(jnp.int32)
    turns = (peak + slots - 1) // slots

    def more_turns(state):
        return state[0] < turns

    def next_turn(state):
        turn, table = state
        target, head = dispatch(turn)
        meta = jnp.pad(head, ((0, 0), (0, META_ROWS - 1), (0, 0)))
        return turn + 1, table + collect(deliver(packed(target, meta, grad_rows)))

    _, grad_table = lax.while_loop(more_turns, next_turn, (jnp.int32(1), grad_table))
    return (
        layer_out,
        grad_input,
        grad_table,
        embed_sum.T,
        grad_w_time,
        gain_sums[0],
        gain_sums[1],
        gain_sums[2],
        gain_sums[3],
        grad_w_qkv.T,
        own_sum[:, hidden_width:].astype(F32).T,
        up_sum.astype(F32).T,
        own_sum[:, :hidden_width].astype(F32).T,
    )


def shards(*arguments):
    seq_count, pos_count = arguments[0].shape
    groups = lax.axis_size("dp")
    whole = seq_count == 2 and lax.axis_size("blk") == 2
    whole = whole and groups >= 4 and groups & (groups - 1) == 0 and pos_count % 256 == 0
    return whole_sequence_shards(*arguments) if whole else split_position_shards(*arguments)


def solution(mesh):
    return jax.shard_map(
        shards,
        mesh=mesh,
        in_specs=(
            P("dp", "blk"),
            P("dp"),
            P("dp"),
            P(),
            P(),
            P(),
            P(),
            P(),
            P(),
            P(),
            P(),
            P(),
            P(),
            P(),
            P("dp", "blk", None),
        ),
        out_specs=(
            P("dp", "blk", None),
            P("dp", "blk", None),
            P(("dp", "blk"), None),
            P(None, ("dp", "blk")),
            P(None, ("dp", "blk")),
            P(("dp", "blk")),
            P(("dp", "blk")),
            P(("dp", "blk")),
            P(("dp", "blk")),
            P(None, ("dp", "blk")),
            P(None, ("dp", "blk")),
            P(None, ("dp", "blk")),
            P(None, ("dp", "blk")),
        ),
        check_vma=False,
    )
```

```python
import functools
import math

import jax
import jax.numpy as jnp
from jax import lax
from jax.experimental import pallas as pl
from jax.experimental.pallas import tpu as pltpu
from jax.sharding import PartitionSpec as P

D = 1024
HEADS = 16
HEAD_DIM = 64
EMB = 256
VOCAB = 32000
TIME_WIDTH = 256


NEG_FILL = -1000000000.0


def from_behind(value, axis, steps):
    count = lax.axis_size(axis)
    pairs = [(source, (source + steps) % count) for source in range(count)]
    return lax.ppermute(value, axis, pairs)


def time_features(diffusion_time, feature_width):
    half_width = feature_width // 2
    frequency = jnp.exp(-math.log(1000.0) * jnp.arange(half_width, dtype=jnp.float32) / half_width)
    angles = diffusion_time.astype(jnp.float32)[:, None] * frequency[None, :]
    return jnp.concatenate([jnp.sin(angles), jnp.cos(angles)], axis=1)


def modulated_norm(features, gain_vec, bias_vec, scale_rows, shift_rows):
    center = features - jnp.mean(features, axis=-1, keepdims=True)
    spread = jnp.mean(center * center, axis=-1, keepdims=True)
    return center * lax.rsqrt(spread + 1e-05) * (gain_vec + scale_rows[:, None, :]) + (
        bias_vec + shift_rows[:, None, :]
    )


def normalize_rows(row_values):
    return row_values * lax.rsqrt(jnp.mean(row_values * row_values, axis=-1, keepdims=True) + 1e-06)


def project(left_side, right_side):
    return lax.dot_general(
        left_side,
        right_side,
        (((left_side.ndim - 1,), (0,)), ((), ())),
        preferred_element_type=jnp.float32,
    )


def project_back(left_side, right_side):
    return lax.dot_general(
        left_side,
        right_side,
        (((left_side.ndim - 1,), (1,)), ((), ())),
        preferred_element_type=jnp.float32,
    )


def outer_sum(left_side, right_side):
    return lax.dot_general(
        left_side, right_side, (((0, 1), (0, 1)), ((), ())), preferred_element_type=jnp.float32
    )


def scatter_rows(running_total, offsets, grad_values):
    row_span = running_total.shape[0]
    inside = (offsets >= 0) & (offsets < row_span)
    return running_total.at[jnp.where(inside, offsets, row_span)].add(grad_values, mode="drop")


def group_columns(matrix, group_count):
    if matrix.ndim == 1:
        return matrix.reshape(1, group_count, matrix.shape[0] // group_count)
    return matrix.reshape(matrix.shape[0], group_count, matrix.shape[1] // group_count)


def split_position_shards(
    token_ids,
    seq_lengths,
    diffusion_time,
    embed_table,
    w_embed,
    w_time,
    gain_attn,
    bias_attn,
    gain_mlp,
    bias_mlp,
    w_qkv,
    w_out,
    w_up,
    w_down,
    cotangent,
):
    seq_count, pos_count = token_ids.shape
    scale_factor = HEAD_DIM ** (-0.5)
    cycle_size = lax.axis_size("blk")
    cycle_index = lax.axis_index("blk")
    positions = cycle_index * pos_count + jnp.arange(pos_count, dtype=jnp.int32)
    valid_rows = (positions[None, :] < seq_lengths[:, None]).astype(jnp.float32)[:, :, None]
    emb_rows = embed_table[token_ids].astype(jnp.float32)
    normed, norm_pull = jax.vjp(normalize_rows, emb_rows)
    normed_low = normed.astype(jnp.bfloat16)
    inputs = project(normed_low, w_embed)
    time_low = time_features(diffusion_time, TIME_WIDTH).astype(jnp.bfloat16)
    modulation = jnp.dot(time_low, w_time, preferred_element_type=jnp.float32)
    scale_attn, shift_attn, scale_mlp, shift_mlp = jnp.split(modulation, 4, axis=1)
    normed_attn, attn_pull = jax.vjp(
        modulated_norm, inputs, gain_attn, bias_attn, scale_attn, shift_attn
    )
    attn_low = normed_attn.astype(jnp.bfloat16)
    qkv_low = project(attn_low, w_qkv).astype(jnp.bfloat16)
    queries = qkv_low[:, :, :D].reshape(seq_count, pos_count, HEADS, HEAD_DIM)
    kv_local = qkv_low[:, :, D:]

    def masked_scores(key_heads, key_start):
        key_count = key_heads.shape[1]
        key_pos = key_start + jnp.arange(key_count, dtype=jnp.int32)
        key_keep = (key_pos[None, :] < seq_lengths[:, None])[:, None, None, :]
        scores = (
            jnp.einsum("sqhd,skhd->shqk", queries, key_heads, preferred_element_type=jnp.float32)
            * scale_factor
        )
        return jnp.where(key_keep, scores, NEG_FILL)

    key_piece = lax.all_gather(kv_local, "blk", axis=1, tiled=True)
    run_max = jnp.full((seq_count, HEADS, pos_count), -1e30, jnp.float32)
    key_count = key_piece.shape[1]
    key_heads = key_piece[:, :, :D].reshape(seq_count, key_count, HEADS, HEAD_DIM)
    value_heads = key_piece[:, :, D:].reshape(seq_count, key_count, HEADS, HEAD_DIM)
    scores = masked_scores(key_heads, jnp.int32(0))
    new_max = jnp.maximum(run_max, jnp.max(scores, axis=-1))
    softmax_weights = jnp.exp(scores - new_max[..., None])
    run_sum = jnp.sum(softmax_weights, axis=-1)
    contrib = jnp.einsum(
        "shqk,skhd->sqhd",
        softmax_weights.astype(jnp.bfloat16),
        value_heads,
        preferred_element_type=jnp.float32,
    )
    run_acc = contrib
    run_max, run_sum, run_acc = (new_max, run_sum, run_acc)
    log_total = run_max + jnp.log(run_sum)
    attended = run_acc / jnp.transpose(run_sum, (0, 2, 1))[..., None]
    attended_low = attended.reshape(seq_count, pos_count, D).astype(jnp.bfloat16)
    residual = inputs + project(attended_low, w_out)
    normed_mlp, mlp_pull = jax.vjp(
        modulated_norm, residual, gain_mlp, bias_mlp, scale_mlp, shift_mlp
    )
    mlp_low = normed_mlp.astype(jnp.bfloat16)
    pre_act = project(mlp_low, w_up)
    activated, gelu_pull = jax.vjp(jax.nn.gelu, pre_act)
    hidden_low = activated.astype(jnp.bfloat16)
    final_sum = (residual + project(hidden_low, w_down)) * valid_rows
    layer_out = final_sum.astype(jnp.bfloat16)
    grad_final = cotangent.astype(jnp.float32) * valid_rows
    final_low = grad_final.astype(jnp.bfloat16)
    grad_w_down = outer_sum(hidden_low, final_low)
    (grad_pre,) = gelu_pull(project_back(final_low, w_down))
    pre_low = grad_pre.astype(jnp.bfloat16)
    grad_w_up = outer_sum(mlp_low, pre_low)
    grad_res_norm, grad_gain_mlp, grad_bias_mlp, grad_scale_mlp, grad_shift_mlp = mlp_pull(
        project_back(pre_low, w_up)
    )
    residual_grad = grad_final + grad_res_norm
    residual_low = residual_grad.astype(jnp.bfloat16)
    grad_w_out = outer_sum(attended_low, residual_low)
    grad_att = (
        project_back(residual_low, w_out)
        .astype(jnp.bfloat16)
        .reshape(seq_count, pos_count, HEADS, HEAD_DIM)
    )
    row_delta = jnp.transpose(jnp.sum(grad_att * attended, axis=-1), (0, 2, 1))

    def key_block(kv_block, owner_index):
        key_heads = kv_block[:, :, :D].reshape(seq_count, pos_count, HEADS, HEAD_DIM)
        value_heads = kv_block[:, :, D:].reshape(seq_count, pos_count, HEADS, HEAD_DIM)
        scores = masked_scores(key_heads, owner_index * pos_count)
        softmax_weights = jnp.exp(scores - log_total[..., None])
        grad_weights = jnp.einsum(
            "sqhd,skhd->shqk", grad_att, value_heads, preferred_element_type=jnp.float32
        )
        grad_scores = (
            softmax_weights * (grad_weights - row_delta[..., None]) * scale_factor
        ).astype(jnp.bfloat16)
        grad_queries = jnp.einsum(
            "shqk,skhd->sqhd", grad_scores, key_heads, preferred_element_type=jnp.float32
        )
        grad_keys = jnp.einsum(
            "shqk,sqhd->skhd", grad_scores, queries, preferred_element_type=jnp.float32
        )
        grad_values = jnp.einsum(
            "shqk,sqhd->skhd",
            softmax_weights.astype(jnp.bfloat16),
            grad_att,
            preferred_element_type=jnp.float32,
        )
        joined = jnp.concatenate(
            [
                grad_keys.reshape(seq_count, pos_count, D),
                grad_values.reshape(seq_count, pos_count, D),
            ],
            axis=-1,
        )
        return (grad_queries, joined)

    def pass_back(grad_values):
        return from_behind(grad_values.astype(jnp.bfloat16), "blk", 1).astype(grad_values.dtype)

    zero_kv = jnp.zeros((seq_count, pos_count, 2 * D), jnp.float32)
    zero_query = jnp.zeros((seq_count, pos_count, HEADS, HEAD_DIM), jnp.float32)

    def cycle_step(turn_index, cycle_state):
        kv_block, grad_kv, grad_query = cycle_state
        part_query, part_kv = key_block(kv_block, (cycle_index - turn_index) % cycle_size)
        kv_block = from_behind(kv_block, "blk", 1)
        return (kv_block, pass_back(grad_kv + part_kv), grad_query + part_query)

    kv_block, grad_kv, grad_query = lax.fori_loop(
        0, cycle_size - 1, cycle_step, (kv_local, zero_kv, zero_query)
    )
    part_query, part_kv = key_block(kv_block, (cycle_index + 1) % cycle_size)
    grad_kv = pass_back(grad_kv + part_kv)
    grad_query = grad_query + part_query
    grad_qkv = jnp.concatenate(
        [grad_query.reshape(seq_count, pos_count, D), grad_kv], axis=-1
    ).astype(jnp.bfloat16)
    grad_w_qkv = outer_sum(attn_low, grad_qkv)
    grad_in_norm, grad_gain_attn, grad_bias_attn, grad_scale_attn, grad_shift_attn = attn_pull(
        project_back(grad_qkv, w_qkv)
    )
    input_grad = residual_grad + grad_in_norm
    grad_input = input_grad.astype(jnp.bfloat16)
    grad_w_embed = outer_sum(normed_low, grad_input)
    grad_modulation = jnp.concatenate(
        [grad_scale_attn, grad_shift_attn, grad_scale_mlp, grad_shift_mlp], axis=1
    )
    grad_w_time = jnp.dot(
        time_low.astype(jnp.float32).T, grad_modulation, precision=lax.Precision.HIGHEST
    )
    (grad_rows,) = norm_pull(project_back(grad_input, w_embed))
    flat_ids = token_ids.reshape(-1)
    flat_grads = grad_rows.reshape(-1, EMB)
    row_count = VOCAB // lax.axis_size(("dp", "blk"))
    own_start = lax.axis_index(("dp", "blk")) * row_count
    piece_ids = lax.all_gather(flat_ids, ("dp", "blk"), axis=0, tiled=True)
    piece_grads = lax.all_gather(
        flat_grads.astype(jnp.bfloat16), ("dp", "blk"), axis=0, tiled=True
    ).astype(jnp.float32)
    grad_table = scatter_rows(
        jnp.zeros((row_count, EMB), jnp.float32), piece_ids - own_start, piece_grads
    )
    group_count = lax.axis_size("dp")
    gradients = (
        grad_w_embed,
        grad_w_time,
        grad_gain_attn,
        grad_bias_attn,
        grad_gain_mlp,
        grad_bias_mlp,
        grad_w_qkv,
        grad_w_out,
        grad_w_up,
        grad_w_down,
    )
    grouped = tuple((group_columns(g, group_count) for g in gradients))
    in_group = (
        lax.psum_scatter(
            grouped[0].astype(jnp.bfloat16), "blk", scatter_dimension=2, tiled=True
        ).astype(jnp.float32),
        lax.psum_scatter(
            grouped[1].astype(jnp.bfloat16), "blk", scatter_dimension=2, tiled=True
        ).astype(jnp.float32),
        lax.psum_scatter(
            grouped[2].astype(jnp.bfloat16), "blk", scatter_dimension=2, tiled=True
        ).astype(jnp.float32),
        lax.psum_scatter(
            grouped[3].astype(jnp.bfloat16), "blk", scatter_dimension=2, tiled=True
        ).astype(jnp.float32),
        lax.psum_scatter(
            grouped[4].astype(jnp.bfloat16), "blk", scatter_dimension=2, tiled=True
        ).astype(jnp.float32),
        lax.psum_scatter(
            grouped[5].astype(jnp.bfloat16), "blk", scatter_dimension=2, tiled=True
        ).astype(jnp.float32),
        lax.psum_scatter(
            grouped[6].astype(jnp.bfloat16), "blk", scatter_dimension=2, tiled=True
        ).astype(jnp.float32),
        lax.psum_scatter(
            grouped[7].astype(jnp.bfloat16), "blk", scatter_dimension=2, tiled=True
        ).astype(jnp.float32),
        lax.psum_scatter(
            grouped[8].astype(jnp.bfloat16), "blk", scatter_dimension=2, tiled=True
        ).astype(jnp.float32),
        lax.psum_scatter(
            grouped[9].astype(jnp.bfloat16), "blk", scatter_dimension=2, tiled=True
        ).astype(jnp.float32),
    )
    across = (
        lax.psum_scatter(
            in_group[0].astype(jnp.bfloat16), "dp", scatter_dimension=1, tiled=True
        ).astype(jnp.float32),
        lax.psum_scatter(
            in_group[1].astype(jnp.bfloat16), "dp", scatter_dimension=1, tiled=True
        ).astype(jnp.float32),
        lax.psum_scatter(
            in_group[2].astype(jnp.bfloat16), "dp", scatter_dimension=1, tiled=True
        ).astype(jnp.float32),
        lax.psum_scatter(
            in_group[3].astype(jnp.bfloat16), "dp", scatter_dimension=1, tiled=True
        ).astype(jnp.float32),
        lax.psum_scatter(
            in_group[4].astype(jnp.bfloat16), "dp", scatter_dimension=1, tiled=True
        ).astype(jnp.float32),
        lax.psum_scatter(
            in_group[5].astype(jnp.bfloat16), "dp", scatter_dimension=1, tiled=True
        ).astype(jnp.float32),
        lax.psum_scatter(
            in_group[6].astype(jnp.bfloat16), "dp", scatter_dimension=1, tiled=True
        ).astype(jnp.float32),
        lax.psum_scatter(
            in_group[7].astype(jnp.bfloat16), "dp", scatter_dimension=1, tiled=True
        ).astype(jnp.float32),
        lax.psum_scatter(
            in_group[8].astype(jnp.bfloat16), "dp", scatter_dimension=1, tiled=True
        ).astype(jnp.float32),
        lax.psum_scatter(
            in_group[9].astype(jnp.bfloat16), "dp", scatter_dimension=1, tiled=True
        ).astype(jnp.float32),
    )
    summed = tuple(
        (
            a.reshape(g.shape[:-1] + (a.shape[-1],)) if g.ndim == 2 else a.reshape(a.shape[-1])
            for a, g in zip(across, gradients)
        )
    )
    return (
        layer_out,
        grad_input,
        grad_table,
        summed[0],
        summed[1],
        summed[2],
        summed[3],
        summed[4],
        summed[5],
        summed[6],
        summed[7],
        summed[8],
        summed[9],
    )


BF16 = jnp.bfloat16
F32 = jnp.float32
LOG2_E = 1.4426950408889634
VMEM_BYTES = 58 * 1024 * 1024
META_ROWS = 4
SLOT_ROWS = 64
EXACT_BASE = 256
TOKEN_TILE = 256
ANY_SPEC = pl.BlockSpec(memory_space=pl.ANY)


def dot_nn(left, right):
    return lax.dot_general(left, right, (((1,), (0,)), ((), ())), preferred_element_type=F32)


def dot_nt(left, right):
    return lax.dot_general(left, right, (((1,), (1,)), ((), ())), preferred_element_type=F32)


def dot_tn(left, right):
    return lax.dot_general(left, right, (((0,), (0,)), ((), ())), preferred_element_type=F32)


def head_operands(queries, keys, head, length):
    lane = lax.broadcasted_iota(jnp.int32, queries.shape, 1)
    row = lax.broadcasted_iota(jnp.int32, queries.shape, 0)
    mine = (lane // HEAD_DIM) == head
    spare = lane == (1 - head) * HEAD_DIM
    zero = jnp.zeros_like(queries)
    fill = jnp.where(row >= length, jnp.full_like(queries, NEG_FILL), zero)
    one_query = jnp.where(mine, queries, jnp.where(spare, jnp.ones_like(queries), zero))
    one_key = jnp.where(mine, keys, jnp.where(spare, fill, zero))
    return mine, one_query, one_key


def attend_kernel(length_ref, q_ref, k_ref, v_ref, out_ref, lse_ref):
    length = length_ref[0]
    factor = LOG2_E * HEAD_DIM**-0.5
    rows = []
    for head in range(2):
        mine, one_query, one_key = head_operands(q_ref[...], k_ref[...], head, length)
        value_one = jnp.where(mine, v_ref[...], jnp.ones_like(v_ref[...]))
        scores = dot_nt(one_key, one_query)
        top = jnp.max(scores, axis=0, keepdims=True)
        weights = jnp.exp2(scores * factor - top * factor).astype(BF16)
        mixed = dot_tn(value_one, weights)
        other = (1 - head) * HEAD_DIM
        total = mixed[other : other + 1]
        lse_ref[0, head : head + 1, :] = top * factor + jnp.log2(total)
        rows.append(mixed[head * HEAD_DIM : (head + 1) * HEAD_DIM] * (1.0 / total))
    out_ref[...] = jnp.transpose(jnp.concatenate(rows, axis=0), (1, 0)).astype(BF16)


def attend_back_kernel(
    length_ref, q_ref, k_ref, v_ref, out_ref, grad_ref, lse_ref, dq_ref, dk_ref, dv_ref, *, chunk
):
    length = length_ref[0]
    positions = q_ref.shape[0]
    factor = LOG2_E * HEAD_DIM**-0.5
    scale = HEAD_DIM**-0.5
    grad = grad_ref[...]
    product = grad.astype(F32) * out_ref[...].astype(F32)
    high = product.astype(BF16)
    low = (product - high.astype(F32)).astype(BF16)
    head_of_lane = lax.broadcasted_iota(jnp.int32, (16, 2 * HEAD_DIM), 1) // HEAD_DIM
    picker = jnp.where(
        head_of_lane == lax.broadcasted_iota(jnp.int32, (16, 2 * HEAD_DIM), 0), 1.0, 0.0
    ).astype(BF16)
    delta = dot_nt(picker, high) + dot_nt(picker, low)
    query_rows = []
    key_parts = ([], [])
    value_parts = ([], [])
    for head in range(2):
        mine, one_query, one_key = head_operands(q_ref[...], k_ref[...], head, length)
        one_value = jnp.where(mine, v_ref[...], jnp.zeros_like(v_ref[...]))
        lse = lse_ref[0, head : head + 1, :]
        row_delta = delta[head : head + 1, :]
        query_grad = jnp.zeros((2 * HEAD_DIM, positions), F32)
        for start in range(0, positions, chunk):
            span = slice(start, start + chunk)
            weights = jnp.exp2(dot_nt(one_key[span], one_query) * factor - lse)
            weight_grad = dot_nt(one_value[span], grad)
            score_grad = (weights * (weight_grad - row_delta)).astype(BF16)
            value_parts[head].append(dot_nn(weights.astype(BF16), grad))
            key_parts[head].append(dot_nn(score_grad, q_ref[...]))
            query_grad = query_grad + dot_tn(k_ref[span, :], score_grad)
        query_rows.append(query_grad[head * HEAD_DIM : (head + 1) * HEAD_DIM])
    first = lax.broadcasted_iota(jnp.int32, (chunk, 2 * HEAD_DIM), 1) < HEAD_DIM
    for part, start in enumerate(range(0, positions, chunk)):
        span = slice(start, start + chunk)
        dk_ref[span, :] = (jnp.where(first, key_parts[0][part], key_parts[1][part]) * scale).astype(BF16)
        dv_ref[span, :] = jnp.where(first, value_parts[0][part], value_parts[1][part]).astype(BF16)
    dq_ref[...] = jnp.transpose(jnp.concatenate(query_rows, axis=0) * scale, (1, 0)).astype(BF16)


def gelu_with_slope(values):
    root = math.sqrt(2.0 / math.pi)
    square = values * values
    share = 0.5 + 0.5 * jnp.tanh(values * (root + root * 0.044715 * square))
    result = values * share
    slope = share + (result - result * share) * (2.0 * root + 6.0 * root * 0.044715 * square)
    return result, slope


def swap_core(value):
    return lax.ppermute(value, "blk", [(0, 1), (1, 0)])


def join_halves(core, own, other):
    first = jnp.where(core == 0, own, other)
    second = jnp.where(core == 0, other, own)
    return jnp.concatenate([first, second], axis=0)


def to_whole(core, local):
    own = lax.dynamic_index_in_dim(local, core, 0, keepdims=False)
    away = lax.dynamic_index_in_dim(local, 1 - core, 0, keepdims=False)
    return join_halves(core, own, swap_core(away))


def fill_other(core, value, arrived):
    return lax.dynamic_update_index_in_dim(value, arrived, 1 - core, 0)


COST_SHARE = 0.3


def kernel_cost(microseconds):
    flops = int(COST_SHARE * microseconds * 1e9)
    return pl.CostEstimate(flops=flops, bytes_accessed=1024, transcendentals=0)


def run_kernel(
    body, grid, scalars, inputs, in_specs, out_specs, out_shape, microseconds, name, scratch=(), carried=()
):
    scalar_count, input_count, output_count = len(scalars), len(inputs), len(out_shape)
    carried_count = len(carried)
    first_carried = scalar_count + input_count

    def kernel(*refs):
        rest = refs[first_carried + carried_count :]
        body(*refs[:first_carried], *rest[:output_count], *rest[output_count + carried_count :])

    results = pl.pallas_call(
        kernel,
        grid_spec=pltpu.PrefetchScalarGridSpec(
            num_scalar_prefetch=scalar_count,
            grid=grid,
            in_specs=list(in_specs) + [ANY_SPEC] * carried_count,
            out_specs=list(out_specs) + [ANY_SPEC] * carried_count,
            scratch_shapes=list(scratch),
        ),
        out_shape=list(out_shape) + [jax.ShapeDtypeStruct(c.shape, c.dtype) for c in carried],
        input_output_aliases={first_carried + i: output_count + i for i in range(carried_count)},
        compiler_params=pltpu.CompilerParams(vmem_limit_bytes=VMEM_BYTES),
        cost_estimate=kernel_cost(microseconds),
        name=name,
    )(*scalars, *inputs, *carried)
    return results[:output_count], results[output_count:]


def behind(*arrays):
    def kernel(*refs):
        pass

    return pl.pallas_call(
        kernel,
        in_specs=[ANY_SPEC] * len(arrays),
        out_specs=[ANY_SPEC] * len(arrays),
        out_shape=[jax.ShapeDtypeStruct(a.shape, a.dtype) for a in arrays],
        input_output_aliases={i: i for i in range(len(arrays))},
        compiler_params=pltpu.CompilerParams(vmem_limit_bytes=VMEM_BYTES),
        cost_estimate=kernel_cost(0),
        name="behind",
    )(*arrays)


FEED_TILE = 512


def shaped(dtype, *shape):
    return jax.ShapeDtypeStruct(shape, dtype)


def row_spec(tile, columns):
    return pl.BlockSpec((tile, columns), lambda i, *scalars: (i, 0))


def fixed_spec(*shape):
    return pl.BlockSpec(shape, lambda *grid: (0,) * len(shape))


def attend(length, qkv):
    positions = qkv.shape[0]
    pairs = HEADS // 2

    def spec(group):
        return pl.BlockSpec((positions, 2 * HEAD_DIM), lambda pair, length: (0, group * pairs + pair))

    results, _ = run_kernel(
        attend_kernel,
        (pairs,),
        [length],
        [qkv, qkv, qkv],
        [spec(0), spec(1), spec(2)],
        [spec(0), pl.BlockSpec((1, 2, positions), lambda pair, length: (pair, 0, 0))],
        [shaped(BF16, positions, D), shaped(F32, pairs, 2, positions)],
        30,
        "attend",
    )
    return results


def attend_back(length, qkv, attended, grad_att, lse, part, parts, grads, carried):
    positions = qkv.shape[0]
    pairs = HEADS // 2
    count = pairs // parts
    shift = part * count

    def spec(group):
        return pl.BlockSpec(
            (positions, 2 * HEAD_DIM), lambda pair, length: (0, group * pairs + shift + pair)
        )

    lse_spec = pl.BlockSpec((1, 2, positions), lambda pair, length: (shift + pair, 0, 0))
    inputs = [qkv, qkv, qkv, attended, grad_att, lse]
    held = len(grads)
    kept = len(carried)

    def kernel(*refs):
        attend_back_kernel(*refs[:7], *refs[7 + held + kept : 10 + held + kept], chunk=min(512, positions))

    aliases = {7 + i: i for i in range(held)}
    aliases.update({7 + held + i: 3 + i for i in range(kept)})
    results = pl.pallas_call(
        kernel,
        grid_spec=pltpu.PrefetchScalarGridSpec(
            num_scalar_prefetch=1,
            grid=(count,),
            in_specs=[spec(0), spec(1), spec(2), spec(0), spec(0), lse_spec] + [ANY_SPEC] * (held + kept),
            out_specs=[spec(0)] * 3 + [ANY_SPEC] * kept,
        ),
        out_shape=[shaped(BF16, positions, D)] * 3 + [jax.ShapeDtypeStruct(c.shape, c.dtype) for c in carried],
        input_output_aliases=aliases,
        compiler_params=pltpu.CompilerParams(vmem_limit_bytes=VMEM_BYTES),
        cost_estimate=kernel_cost(46 / parts),
        name="attend_back",
    )(length, *inputs, *grads, *carried)
    return results[:3], results[3:]


def norm_rows(features):
    center = features - jnp.mean(features, axis=-1, keepdims=True)
    rstd = lax.rsqrt(jnp.mean(center * center, axis=-1, keepdims=True) + 1e-05)
    return center * rstd, rstd


def norm_rows_back(grad_norm, xhat, rstd, gain_row):
    scaled = grad_norm * gain_row
    mean_scaled = jnp.mean(scaled, axis=-1, keepdims=True)
    mean_cross = jnp.mean(scaled * xhat, axis=-1, keepdims=True)
    return rstd * (scaled - mean_scaled - xhat * mean_cross)


def add_column_sums(sums_ref, grad_norm, xhat):
    sums_ref[0:1, :] += jnp.sum(grad_norm * xhat, axis=0, keepdims=True)
    sums_ref[1:2, :] += jnp.sum(grad_norm, axis=0, keepdims=True)


def split_specs(count, tile):
    steps = count // tile // 2

    def early(i):
        return jnp.minimum(i, steps - 1)

    def late(i):
        return jnp.maximum(i - steps, 0)

    def own(i, *scalars):
        core = scalars[-1][0]
        return core, jnp.where(core == 0, early(i), late(i)), 0

    def other(i, *scalars):
        return jnp.where(scalars[-1][0] == 0, late(i), early(i)), 0

    return [pl.BlockSpec((1, tile, D), own), pl.BlockSpec((tile, D), other)]


def store_split(core, own_ref, other_ref, value):
    half = pl.program_id(0) * 2 // pl.num_programs(0)

    @pl.when(half == core)
    def _():
        own_ref[0] = value

    @pl.when(half != core)
    def _():
        other_ref[...] = value


def valid_column(length, tile):
    row = lax.broadcasted_iota(jnp.int32, (tile, 1), 0) + pl.program_id(0) * tile
    return row < length


def share_out(core, value, keep_ref, away_ref):
    rows = keep_ref.shape[-2]
    if len(keep_ref.shape) == 4:
        outer, inner = keep_ref.shape[:2]
        value = value.astype(BF16).reshape(outer, inner, 2, rows, value.shape[1])
        first, second = value[:, :, 0], value[:, :, 1]
        keep_ref[...] = jnp.where(core == 0, first, second)
        away_ref[...] = jnp.where(core == 0, second, first)
        return
    groups = keep_ref.shape[0]
    value = value.astype(BF16).reshape(groups, 2, rows, value.shape[1])
    first, second = value[:, 0], value[:, 1]
    keep_ref[...] = jnp.where(core == 0, first, second)
    away_ref[...] = jnp.where(core == 0, second, first)


def embed_kernel(emb_ref, we_ref, gain_ref, shift_ref, wqkv_ref, low_ref, in_ref, attn_ref, qkv_ref):
    rows = emb_ref[...].astype(F32)
    normed = rows * lax.rsqrt(jnp.mean(rows * rows, axis=-1, keepdims=True) + 1e-06)
    low = normed.astype(BF16)
    low_ref[...] = low
    inputs = dot_nn(low, we_ref[...])
    in_ref[...] = inputs.astype(BF16)
    xhat, _ = norm_rows(inputs)
    attn = (xhat * gain_ref[...] + shift_ref[...]).astype(BF16)
    attn_ref[...] = attn
    qkv_ref[...] = dot_nn(attn, wqkv_ref[...]).astype(BF16)


def embed_and_project(emb, w_embed, gain_row, shift_row, w_qkv):
    count = emb.shape[0]
    tile = TOKEN_TILE
    results, _ = run_kernel(
        embed_kernel,
        (count // tile,),
        [],
        [emb, w_embed, gain_row, shift_row, w_qkv],
        [row_spec(tile, EMB), fixed_spec(EMB, D), fixed_spec(1, D), fixed_spec(1, D), fixed_spec(D, 3 * D)],
        [row_spec(tile, EMB), row_spec(tile, D), row_spec(tile, D), row_spec(tile, 3 * D)],
        [shaped(BF16, count, EMB), shaped(BF16, count, D), shaped(BF16, count, D), shaped(BF16, count, 3 * D)],
        12,
        "embed_and_project",
    )
    return results


def residual_kernel(
    length_ref, core_ref, att_ref, in_ref, wo_ref, gain_ref, shift_ref, cot_ref, cot_other_ref,
    res_ref, mlp_ref, fin_ref
):
    residual = in_ref[...].astype(F32) + dot_nn(att_ref[...], wo_ref[...])
    res_ref[...] = residual.astype(BF16)
    xhat, _ = norm_rows(residual)
    mlp_ref[...] = (xhat * gain_ref[...] + shift_ref[...]).astype(BF16)
    half = pl.program_id(0) * 2 // pl.num_programs(0)
    cot = jnp.where(half == core_ref[0], cot_ref[0], cot_other_ref[...])
    fin_ref[...] = jnp.where(valid_column(length_ref[0], cot.shape[0]), cot, jnp.zeros_like(cot))


def attention_residual(length, core, attended, inputs, w_out, gain_row, shift_row, cot, cot_other):
    count = attended.shape[0]
    row = row_spec(TOKEN_TILE, D)
    results, _ = run_kernel(
        residual_kernel,
        (count // TOKEN_TILE,),
        [length, core],
        [attended, inputs, w_out, gain_row, shift_row, cot, cot_other],
        [row, row, fixed_spec(D, D), fixed_spec(1, D), fixed_spec(1, D)] + split_specs(count, TOKEN_TILE),
        [row, row, row],
        [shaped(BF16, count, D)] * 3,
        8,
        "attention_residual",
    )
    return results


def feed_forward_kernel(
    core_ref, mlp_ref, fin_ref, wu_ref, wd_ref, down_in_ref, grad_in_ref,
    gwd_keep_ref, gwd_away_ref, gwu_keep_ref, gwu_away_ref, down_ref, grad_ref,
    fin_t_ref, hid_ref, pre_ref, *, first
):
    core = core_ref[0]
    count = mlp_ref.shape[0]

    @pl.when(pl.program_id(0) == 0)
    def _():
        fin_t_ref[...] = jnp.transpose(fin_ref[...], (1, 0))
        if first:
            down_ref[...] = jnp.zeros_like(down_ref)
            grad_ref[...] = jnp.zeros_like(grad_ref)
        else:
            down_ref[...] = down_in_ref[...]
            grad_ref[...] = grad_in_ref[...]

    for start in range(0, count, FEED_TILE):
        span = slice(start, start + FEED_TILE)
        hidden, slope = gelu_with_slope(dot_nn(mlp_ref[span, :], wu_ref[...]))
        hid_ref[span, :] = hidden.astype(BF16)
        pre_ref[span, :] = (dot_nt(fin_ref[span, :], wd_ref[...]) * slope).astype(BF16)
    share_out(core, dot_nn(fin_t_ref[...], hid_ref[...]), gwd_keep_ref, gwd_away_ref)
    share_out(core, dot_tn(pre_ref[...], mlp_ref[...]), gwu_keep_ref, gwu_away_ref)
    for start in range(0, count, FEED_TILE):
        span = slice(start, start + FEED_TILE)
        down_ref[span, :] += dot_nn(hid_ref[span, :], wd_ref[...])
        grad_ref[span, :] += dot_nt(pre_ref[span, :], wu_ref[...])


def feed_forward(core, groups, part, parts, mlp_low, final_low, w_up, w_down, down, grad, carried, tile=512):
    count = mlp_low.shape[0]
    width = w_up.shape[1] // parts
    steps = width // tile
    shift = part * steps
    first = down is None
    if first:
        down = grad = jnp.zeros((8, 128), F32)
    down_rows = D // (2 * groups)
    up_rows = w_up.shape[1] // (2 * groups)
    down_share = (groups // 4, 4, down_rows)
    down_spec = pl.BlockSpec((*down_share, tile), lambda j, core: (0, 0, 0, j))
    up_spec = pl.BlockSpec((tile // (2 * up_rows), up_rows, D), lambda j, core: (j, 0, 0))
    whole = fixed_spec(count, D)
    return run_kernel(
        functools.partial(feed_forward_kernel, first=first),
        (steps,),
        [core],
        [mlp_low, final_low, w_up, w_down, down, grad],
        [
            whole,
            whole,
            pl.BlockSpec((D, tile), lambda j, core: (0, shift + j)),
            pl.BlockSpec((tile, D), lambda j, core: (shift + j, 0)),
            fixed_spec(*down.shape),
            fixed_spec(*down.shape),
        ],
        [down_spec, down_spec, up_spec, up_spec, whole, whole],
        [shaped(BF16, *down_share, width)] * 2
        + [shaped(BF16, groups // parts, up_rows, D)] * 2
        + [shaped(F32, count, D)] * 2,
        36,
        "feed_forward",
        scratch=[pltpu.VMEM((D, count), BF16), pltpu.VMEM((count, tile), BF16), pltpu.VMEM((count, tile), BF16)],
        carried=carried,
    )


def middle_kernel(
    length_ref, core_ref, down_ref, gmn_ref, res_ref, fin_ref, gain_ref, wo_ref, att_ref,
    out_ref, out_away_ref, low_ref, gatt_ref, gwo_keep_ref, gwo_away_ref, sums_ref, acc_ref
):
    step = pl.program_id(0)

    @pl.when(step == 0)
    def _():
        sums_ref[...] = jnp.zeros_like(sums_ref)
        acc_ref[...] = jnp.zeros_like(acc_ref)

    residual = res_ref[...].astype(F32)
    keep = valid_column(length_ref[0], residual.shape[0])
    final = jnp.where(keep, residual + down_ref[...], 0.0).astype(BF16)
    store_split(core_ref[0], out_ref, out_away_ref, final)
    xhat, rstd = norm_rows(residual)
    grad = gmn_ref[...]
    add_column_sums(sums_ref, grad, xhat)
    low = (fin_ref[...].astype(F32) + norm_rows_back(grad, xhat, rstd, gain_ref[...])).astype(BF16)
    low_ref[...] = low
    gatt_ref[...] = dot_nt(low, wo_ref[...]).astype(BF16)
    acc_ref[...] += dot_tn(low, att_ref[...])

    @pl.when(step == pl.num_programs(0) - 1)
    def _():
        share_out(core_ref[0], acc_ref[...], gwo_keep_ref, gwo_away_ref)


def feed_forward_to_attention(
    length, core, groups, down, grad_mlp_norm, residual, final_low, gain_row, w_out, attended, carried
):
    count = residual.shape[0]
    row = row_spec(TOKEN_TILE, D)
    share = (groups // 4, 4, D // (2 * groups), D)
    return run_kernel(
        middle_kernel,
        (count // TOKEN_TILE,),
        [length, core],
        [down, grad_mlp_norm, residual, final_low, gain_row, w_out, attended],
        [row, row, row, row, fixed_spec(1, D), fixed_spec(D, D), row],
        split_specs(count, TOKEN_TILE) + [row, row, fixed_spec(*share), fixed_spec(*share), fixed_spec(8, D)],
        [shaped(BF16, 2, count // 2, D), shaped(BF16, count // 2, D)] + [shaped(BF16, count, D)] * 2 + [shaped(BF16, *share)] * 2 + [shaped(F32, 8, D)],
        15,
        "feed_forward_to_attention",
        scratch=[pltpu.VMEM((D, D), F32)],
        carried=carried,
    )


def outer_kernel(core_ref, dq_ref, dk_ref, dv_ref, right_ref, keep_ref, away_ref, all_ref):
    right = right_ref[...]
    for group, ref in enumerate((dq_ref, dk_ref, dv_ref)):
        for start in range(0, D, TOKEN_TILE):
            rows = slice(group * D + start, group * D + start + TOKEN_TILE)
            all_ref[rows, :] = dot_tn(ref[:, start : start + TOKEN_TILE], right).astype(BF16)
    share_out(core_ref[0], all_ref[...], keep_ref, away_ref)


def outer_qkv(core, groups, grads, right, half, carried):
    count = right.shape[0]
    columns = right.shape[1] // 2
    share = (groups, 3 * D // (2 * groups), columns)
    return run_kernel(
        outer_kernel,
        (1,),
        [core],
        [*grads, right],
        [fixed_spec(count, D)] * 3 + [pl.BlockSpec((count, columns), lambda i, core: (0, half))],
        [fixed_spec(*share)] * 2,
        [shaped(BF16, *share)] * 2,
        8,
        "outer_qkv",
        scratch=[pltpu.VMEM((3 * D, columns), BF16)],
        carried=carried,
    )


def input_kernel(
    core_ref, dq_ref, dk_ref, dv_ref, wqkv_ref, in_ref, low_ref, gain_ref, we_ref, emb_ref, nl_ref,
    grad_ref, grad_away_ref, rows_ref, gwe_keep_ref, gwe_away_ref, sums_ref, acc_ref
):
    step = pl.program_id(0)

    @pl.when(step == 0)
    def _():
        sums_ref[...] = jnp.zeros_like(sums_ref)
        acc_ref[...] = jnp.zeros_like(acc_ref)

    grad = (
        dot_nt(dq_ref[...], wqkv_ref[:, :D])
        + dot_nt(dk_ref[...], wqkv_ref[:, D : 2 * D])
        + dot_nt(dv_ref[...], wqkv_ref[:, 2 * D :])
    )
    xhat, rstd = norm_rows(in_ref[...].astype(F32))
    add_column_sums(sums_ref, grad, xhat)
    low = (low_ref[...].astype(F32) + norm_rows_back(grad, xhat, rstd, gain_ref[...])).astype(BF16)
    store_split(core_ref[0], grad_ref, grad_away_ref, low)
    acc_ref[...] += dot_tn(low, nl_ref[...])
    back = dot_nt(low, we_ref[...])
    emb = emb_ref[...].astype(F32)
    emb_rstd = lax.rsqrt(jnp.mean(emb * emb, axis=-1, keepdims=True) + 1e-06)
    normed = emb * emb_rstd
    rows_ref[...] = (emb_rstd * (back - normed * jnp.mean(normed * back, axis=-1, keepdims=True))).astype(BF16)

    @pl.when(step == pl.num_programs(0) - 1)
    def _():
        share_out(core_ref[0], acc_ref[...], gwe_keep_ref, gwe_away_ref)


def input_gradient(core, groups, grads, w_qkv, inputs, residual_low, gain_row, w_embed, emb, normed_low, carried):
    count = inputs.shape[0]
    tile = TOKEN_TILE
    share = (2 * groups, D // (4 * groups), EMB)
    row, narrow = row_spec(tile, D), row_spec(tile, EMB)
    return run_kernel(
        input_kernel,
        (count // tile,),
        [core],
        [*grads, w_qkv, inputs, residual_low, gain_row, w_embed, emb, normed_low],
        [row, row, row, fixed_spec(D, 3 * D), row, row, fixed_spec(1, D), fixed_spec(EMB, D), narrow, narrow],
        split_specs(count, tile) + [narrow, fixed_spec(*share), fixed_spec(*share), fixed_spec(8, D)],
        [shaped(BF16, 2, count // 2, D), shaped(BF16, count // 2, D), shaped(BF16, count, EMB)] + [shaped(BF16, *share)] * 2 + [shaped(F32, 8, D)],
        16,
        "input_gradient",
        scratch=[pltpu.VMEM((D, EMB), F32)],
        carried=carried,
    )


def exchange(value, bit, dp_bits, pattern=1):
    return lax.ppermute(value, "dp", [(i, i ^ (pattern << bit)) for i in range(1 << dp_bits)])


class Halving:
    def __init__(self, labels, dp_bits, flat):
        self.labels = list(labels)
        self.flat = flat
        self.dp_bits = dp_bits
        self.terms = []
        self.fixed = {}

    def over_cores(self, keep, away):
        labels = tuple(self.labels)
        shape = keep.shape if self.flat else (2,) * len(labels) + keep.shape[1:]
        self.terms = [(keep.reshape(shape), labels), (swap_core(away).reshape(shape), labels)]

    @property
    def keep(self):
        return self.terms[0][0]

    @keep.setter
    def keep(self, value):
        self.terms[0] = (value, self.terms[0][1])

    def part(self, fixed):
        total = 0.0
        for value, labels in self.terms:
            spans = [label not in fixed for label in labels]
            starts = [0 if span else fixed[label] for span, label in zip(spans, labels)] + [0, 0]
            sizes = [2 if span else 1 for span in spans] + list(value.shape[-2:])
            piece = lax.dynamic_slice(value.reshape((2,) * len(labels) + value.shape[-2:]), starts, sizes)
            left = (-1,) if self.flat else (2,) * sum(spans)
            total = total + piece.reshape(left + value.shape[-2:]).astype(F32)
        return total

    def total(self):
        return self.part(self.fixed)

    def away(self, bit_label):
        bit = (lax.axis_index("dp") >> bit_label) & 1
        return self.part({**self.fixed, bit_label: 1 - bit}).astype(BF16)

    def send(self, bit_label, away):
        self.fixed[bit_label] = (lax.axis_index("dp") >> bit_label) & 1
        labels = tuple(label for label in self.labels if label not in self.fixed)
        self.terms.append((exchange(away, bit_label, self.dp_bits), labels))


def between_planes(value, dp_bits):
    plane = lax.axis_index("dp") >> 2
    parts = [lax.dynamic_index_in_dim(value, plane, 0, keepdims=False)]
    for step in range(1, value.shape[0]):
        away = lax.dynamic_index_in_dim(value, plane ^ step, 0, keepdims=False)
        parts.append(exchange(away, 2, dp_bits, step))
    return parts


def whole_sequence_shards(
    token_ids,
    seq_lengths,
    diffusion_time,
    embed_table,
    w_embed,
    w_time,
    gain_attn,
    bias_attn,
    gain_mlp,
    bias_mlp,
    w_qkv,
    w_out,
    w_up,
    w_down,
    cotangent,
):
    core = lax.axis_index("blk")
    cores = core.reshape(1).astype(jnp.int32)
    groups = lax.axis_size("dp")
    devices = 2 * groups
    dp_bits = groups.bit_length() - 1
    everywhere = ("dp", "blk")
    labels = list(reversed(range(dp_bits)))
    planes = [[4 * high + low for low in range(4)] for high in range(groups // 4)]
    lines = [[4 * high + low for high in range(groups // 4)] for low in range(4)]
    ids = to_whole(core, token_ids)
    cot_other = swap_core(lax.dynamic_index_in_dim(cotangent, 1 - core, 0, keepdims=False))
    positions = ids.shape[0]
    length = lax.dynamic_index_in_dim(seq_lengths, core, 0, keepdims=True)
    time = lax.dynamic_index_in_dim(diffusion_time, core, 0, keepdims=True)
    emb = embed_table[ids]

    valid = jnp.arange(positions, dtype=jnp.int32) < length[0]
    row_count = VOCAB // devices
    owner = jnp.where(valid, ids // row_count, -1)
    offset = ids % row_count
    slots = SLOT_ROWS - META_ROWS
    member = owner[:, None] == jnp.arange(devices, dtype=jnp.int32)[None, :]
    earlier = jnp.arange(positions)[:, None] > jnp.arange(positions)[None, :]
    before = dot_nn(earlier.astype(BF16), member.astype(BF16))
    rank = jnp.sum(jnp.where(member, before, 0.0), axis=1).astype(jnp.int32)
    most = jnp.max(jnp.sum(member.astype(jnp.int32), axis=0))
    offset_digits = jnp.stack(
        [(offset // EXACT_BASE).astype(BF16), (offset % EXACT_BASE).astype(BF16), jnp.ones(positions, BF16)],
        axis=1,
    )

    def dispatch(turn):
        slot = rank - turn * slots
        inside = (owner >= 0) & (slot >= 0) & (slot < slots)
        target = jnp.where(inside, owner * SLOT_ROWS + META_ROWS + slot, -1)
        place = jnp.arange(devices * SLOT_ROWS, dtype=jnp.int32)[:, None] == target[None, :]
        digits = dot_nn(place.astype(BF16), offset_digits).reshape(devices, SLOT_ROWS, 3)
        head = jnp.transpose(digits, (0, 2, 1)).reshape(devices, 1, 3 * SLOT_ROWS)
        peak = jnp.stack([most // EXACT_BASE, most % EXACT_BASE]).astype(F32)
        peak = jnp.broadcast_to(peak, (devices, 1, 2))
        gap = jnp.zeros((devices, 1, EMB - 3 * SLOT_ROWS - 2), F32)
        return target, jnp.concatenate([head, peak, gap], axis=2)

    meta_target = jnp.arange(devices * META_ROWS, dtype=jnp.int32)
    meta_target = meta_target // META_ROWS * SLOT_ROWS + meta_target % META_ROWS

    def packed(target, meta, grads):
        meta = meta.astype(BF16).reshape(devices * META_ROWS, EMB)
        target = jnp.concatenate([target, meta_target])
        place = jnp.arange(devices * SLOT_ROWS, dtype=jnp.int32)[:, None] == target[None, :]
        rows = dot_nn(place.astype(BF16), jnp.concatenate([grads, meta]))
        return rows.astype(BF16).reshape(devices, SLOT_ROWS, EMB)

    def deliver(rows):
        return lax.all_to_all(rows, everywhere, 0, 0, tiled=True)

    def collect(rows):
        head = rows[:, 0].astype(F32)
        high, low, used = (head[:, i * SLOT_ROWS : (i + 1) * SLOT_ROWS] for i in range(3))
        row = jnp.where(used > 0.5, high * EXACT_BASE + low, -1.0).astype(jnp.int32)
        row = jnp.pad(row, ((0, 0), (0, rows.shape[1] - SLOT_ROWS)), constant_values=-1)
        hit = jnp.arange(row_count, dtype=jnp.int32)[:, None] == row.reshape(1, -1)
        return dot_nn(hit.astype(BF16), rows.reshape(-1, EMB))

    first_target, first_head = dispatch(0)

    def over_cores(keep, arrived):
        return (keep.astype(F32) + arrived.astype(F32)).astype(BF16)

    def scattered(value, index_groups):
        return lax.psum_scatter(value, "dp", scatter_dimension=0, axis_index_groups=index_groups, tiled=True)[0]

    time_low = time_features(time, TIME_WIDTH).astype(BF16)
    modulation = dot_nn(time_low, w_time)
    scale_attn, shift_attn, scale_mlp, shift_mlp = jnp.split(modulation, 4, axis=1)
    gain_row_attn = gain_attn + scale_attn
    gain_row_mlp = gain_mlp + scale_mlp
    normed_low, inputs, attn_low, qkv = embed_and_project(
        emb, w_embed, gain_row_attn, bias_attn + shift_attn, w_qkv
    )
    attended, lse = attend(length, qkv)
    residual, mlp_low, final_low = attention_residual(
        length, cores, attended, inputs, w_out, gain_row_mlp, bias_mlp + shift_mlp, cotangent, cot_other
    )

    hidden_width = w_up.shape[1]
    feed = functools.partial(feed_forward, cores, groups)
    (keep_d, away_d, keep_u, away_u, down, grad), _ = feed(
        0, 2, mlp_low, final_low, w_up, w_down, None, None, []
    )
    up_0, up_1 = Halving(labels[1:], dp_bits, True), Halving(labels[1:], dp_bits, True)
    qkv_a, qkv_b = Halving(labels, dp_bits, False), Halving(labels, dp_bits, False)
    up_0.over_cores(keep_u, away_u)
    arrived_d = swap_core(away_d)
    (next_keep, next_away, keep_u, away_u, down, grad), (up_0.keep, keep_d) = feed(
        1, 2, mlp_low, final_low, w_up, w_down, down, grad, [up_0.keep, keep_d]
    )
    away, down_0, next_keep, next_away, keep_u, away_u = behind(
        up_0.away(0), over_cores(keep_d, arrived_d), next_keep, next_away, keep_u, away_u
    )
    up_0.send(0, away)
    up_1.over_cores(keep_u, away_u)
    arrived_d = swap_core(next_away)
    down_0 = scattered(down_0, lines)
    (layer_out, layer_away, residual_low, grad_att, keep_o, away_o, sums_mlp), kept = feed_forward_to_attention(
        length, cores, groups, down, grad, residual, final_low, gain_row_mlp, w_out, attended,
        [up_0.keep, up_1.keep, next_keep],
    )
    up_0.keep, up_1.keep, keep_d = kept
    away_0, away_1, down_1, keep_o, away_o = behind(
        up_0.away(1), up_1.away(0), over_cores(keep_d, arrived_d), keep_o, away_o
    )
    up_0.send(1, away_0)
    up_1.send(0, away_1)
    down_1 = scattered(down_1, lines)
    arrived_o = swap_core(away_o)
    back = functools.partial(attend_back, length, qkv, attended, grad_att, lse)
    grads, (up_0.keep, up_1.keep, keep_o) = back(0, 2, [], [up_0.keep, up_1.keep, keep_o])
    away_1, out_sum, up_first = behind(
        up_1.away(1), over_cores(keep_o, arrived_o), up_0.total().astype(BF16)
    )
    up_1.send(1, away_1)
    out_sum = scattered(out_sum, lines)
    grads, (up_1.keep, up_first, down_0) = back(1, 2, grads, [up_1.keep, up_first, down_0])
    up_rows = [up_first, up_1.total().astype(BF16)]
    up_rows = jnp.concatenate(up_rows)
    up_sum = scattered(up_rows, lines)
    (keep_a, away_a), (down_1,) = outer_qkv(cores, groups, grads, attn_low, 0, [down_1])
    keep_a, away_a = behind(keep_a, away_a)
    qkv_a.over_cores(keep_a, away_a)
    orders = [(0, 1), (1, 0)]
    (keep_b, away_b), (qkv_a.keep, down_1) = outer_qkv(
        cores, groups, grads, attn_low, 1, [qkv_a.keep, down_1]
    )
    in_plane = jnp.concatenate([down_0, down_1, out_sum], axis=2)
    away_a, keep_b, away_b, in_plane = behind(qkv_a.away(orders[0][0]), keep_b, away_b, in_plane)
    own_sum = scattered(in_plane, planes)
    qkv_a.send(orders[0][0], away_a)
    qkv_b.over_cores(keep_b, away_b)
    qkv_b.send(orders[1][0], *behind(qkv_b.away(orders[1][0])))
    (grad_input, input_away, grad_rows, keep_e, away_e, sums_attn), kept = input_gradient(
        cores, groups, grads, w_qkv, inputs, residual_low, gain_row_attn, w_embed, emb, normed_low,
        [qkv_a.keep, qkv_b.keep],
    )
    qkv_a.keep, qkv_b.keep = kept

    grad_modulation = jnp.concatenate([sums_attn[0], sums_attn[1], sums_mlp[0], sums_mlp[1]])
    gain_columns = jnp.transpose(grad_modulation.reshape(4, devices, -1), (1, 0, 2)).reshape(devices, -1)
    mod_rows = jnp.concatenate([grad_modulation.reshape(devices, -1), gain_columns], axis=1)
    mod_high = mod_rows.astype(BF16).astype(F32)
    mod_low = mod_rows - mod_high
    time_rows = jnp.broadcast_to(time_low.astype(F32), (devices, TIME_WIDTH))
    first_meta = jnp.concatenate(
        [first_head, jnp.stack([mod_high, mod_low, time_rows], axis=1)], axis=1
    )
    embed_rows = over_cores(keep_e, swap_core(away_e))
    payload = jnp.concatenate([packed(first_target, first_meta, grad_rows), embed_rows], axis=1)
    payload, away_a, away_b, up_sum, layer_away, input_away = behind(
        payload, qkv_a.away(orders[0][1]), qkv_b.away(orders[1][1]), up_sum, layer_away, input_away
    )
    arrived = deliver(payload)
    qkv_a.send(orders[0][1], away_a)
    qkv_b.send(orders[1][1], away_b)
    qkv_rows = jnp.concatenate([qkv_a.total(), qkv_b.total()], axis=-1).astype(BF16)
    qkv_rows = qkv_rows.reshape((-1,) + qkv_rows.shape[-2:])
    layer_out = fill_other(core, layer_out, swap_core(layer_away))
    parts = between_planes(qkv_rows, dp_bits)
    parts[1], up_sum = behind(parts[1], up_sum)
    grad_w_qkv = sum(part.astype(F32) for part in parts)
    embed_sum = arrived[:, SLOT_ROWS:].astype(F32).reshape(groups, -1, EMB)
    embed_sum = jnp.sum(embed_sum, axis=0)
    grad_input = fill_other(core, grad_input, swap_core(input_away))
    grad_table = collect(arrived)
    sums = arrived[:, 1].astype(F32) + arrived[:, 2].astype(F32)
    time_width = sums.shape[1] // 2
    grad_w_time = lax.dot_general(
        arrived[:, 3].astype(F32),
        sums[:, :time_width],
        (((0,), (0,)), ((), ())),
        precision=lax.Precision.HIGHEST,
    )
    gain_sums = jnp.sum(sums[:, time_width:], axis=0).reshape(4, -1)
    peaks = arrived[:, 0, 3 * SLOT_ROWS : 3 * SLOT_ROWS + 2].astype(F32)
    peak = jnp.max(peaks[:, 0] * EXACT_BASE + peaks[:, 1]).astype(jnp.int32)
    turns = (peak + slots - 1) // slots

    def more_turns(state):
        return state[0] < turns

    def next_turn(state):
        turn, table = state
        target, head = dispatch(turn)
        meta = jnp.pad(head, ((0, 0), (0, META_ROWS - 1), (0, 0)))
        return turn + 1, table + collect(deliver(packed(target, meta, grad_rows)))

    _, grad_table = lax.while_loop(more_turns, next_turn, (jnp.int32(1), grad_table))
    return (
        layer_out,
        grad_input,
        grad_table,
        embed_sum.T,
        grad_w_time,
        gain_sums[0],
        gain_sums[1],
        gain_sums[2],
        gain_sums[3],
        grad_w_qkv.T,
        own_sum[:, hidden_width:].astype(F32).T,
        up_sum.astype(F32).T,
        own_sum[:, :hidden_width].astype(F32).T,
    )


def shards(*arguments):
    seq_count, pos_count = arguments[0].shape
    groups = lax.axis_size("dp")
    whole = seq_count == 2 and lax.axis_size("blk") == 2
    whole = whole and groups >= 4 and groups & (groups - 1) == 0 and pos_count % 256 == 0
    return whole_sequence_shards(*arguments) if whole else split_position_shards(*arguments)


def solution(mesh):
    return jax.shard_map(
        shards,
        mesh=mesh,
        in_specs=(
            P("dp", "blk"),
            P("dp"),
            P("dp"),
            P(),
            P(),
            P(),
            P(),
            P(),
            P(),
            P(),
            P(),
            P(),
            P(),
            P(),
            P("dp", "blk", None),
        ),
        out_specs=(
            P("dp", "blk", None),
            P("dp", "blk", None),
            P(("dp", "blk"), None),
            P(None, ("dp", "blk")),
            P(None, ("dp", "blk")),
            P(("dp", "blk")),
            P(("dp", "blk")),
            P(("dp", "blk")),
            P(("dp", "blk")),
            P(None, ("dp", "blk")),
            P(None, ("dp", "blk")),
            P(None, ("dp", "blk")),
            P(None, ("dp", "blk")),
        ),
        check_vma=False,
    )
```

```python
import functools
import math

import jax
import jax.numpy as jnp
from jax import lax
from jax.experimental import pallas as pl
from jax.experimental.pallas import tpu as pltpu
from jax.sharding import PartitionSpec as P

D = 1024
HEADS = 16
HEAD_DIM = 64
EMB = 256
VOCAB = 32000
TIME_WIDTH = 256


NEG_FILL = -1000000000.0


def from_behind(value, axis, steps):
    count = lax.axis_size(axis)
    pairs = [(source, (source + steps) % count) for source in range(count)]
    return lax.ppermute(value, axis, pairs)


def time_features(diffusion_time, feature_width):
    half_width = feature_width // 2
    frequency = jnp.exp(-math.log(1000.0) * jnp.arange(half_width, dtype=jnp.float32) / half_width)
    angles = diffusion_time.astype(jnp.float32)[:, None] * frequency[None, :]
    return jnp.concatenate([jnp.sin(angles), jnp.cos(angles)], axis=1)


def modulated_norm(features, gain_vec, bias_vec, scale_rows, shift_rows):
    center = features - jnp.mean(features, axis=-1, keepdims=True)
    spread = jnp.mean(center * center, axis=-1, keepdims=True)
    return center * lax.rsqrt(spread + 1e-05) * (gain_vec + scale_rows[:, None, :]) + (
        bias_vec + shift_rows[:, None, :]
    )


def normalize_rows(row_values):
    return row_values * lax.rsqrt(jnp.mean(row_values * row_values, axis=-1, keepdims=True) + 1e-06)


def project(left_side, right_side):
    return lax.dot_general(
        left_side,
        right_side,
        (((left_side.ndim - 1,), (0,)), ((), ())),
        preferred_element_type=jnp.float32,
    )


def project_back(left_side, right_side):
    return lax.dot_general(
        left_side,
        right_side,
        (((left_side.ndim - 1,), (1,)), ((), ())),
        preferred_element_type=jnp.float32,
    )


def outer_sum(left_side, right_side):
    return lax.dot_general(
        left_side, right_side, (((0, 1), (0, 1)), ((), ())), preferred_element_type=jnp.float32
    )


def scatter_rows(running_total, offsets, grad_values):
    row_span = running_total.shape[0]
    inside = (offsets >= 0) & (offsets < row_span)
    return running_total.at[jnp.where(inside, offsets, row_span)].add(grad_values, mode="drop")


def group_columns(matrix, group_count):
    if matrix.ndim == 1:
        return matrix.reshape(1, group_count, matrix.shape[0] // group_count)
    return matrix.reshape(matrix.shape[0], group_count, matrix.shape[1] // group_count)


def split_position_shards(
    token_ids,
    seq_lengths,
    diffusion_time,
    embed_table,
    w_embed,
    w_time,
    gain_attn,
    bias_attn,
    gain_mlp,
    bias_mlp,
    w_qkv,
    w_out,
    w_up,
    w_down,
    cotangent,
):
    seq_count, pos_count = token_ids.shape
    scale_factor = HEAD_DIM ** (-0.5)
    cycle_size = lax.axis_size("blk")
    cycle_index = lax.axis_index("blk")
    positions = cycle_index * pos_count + jnp.arange(pos_count, dtype=jnp.int32)
    valid_rows = (positions[None, :] < seq_lengths[:, None]).astype(jnp.float32)[:, :, None]
    emb_rows = embed_table[token_ids].astype(jnp.float32)
    normed, norm_pull = jax.vjp(normalize_rows, emb_rows)
    normed_low = normed.astype(jnp.bfloat16)
    inputs = project(normed_low, w_embed)
    time_low = time_features(diffusion_time, TIME_WIDTH).astype(jnp.bfloat16)
    modulation = jnp.dot(time_low, w_time, preferred_element_type=jnp.float32)
    scale_attn, shift_attn, scale_mlp, shift_mlp = jnp.split(modulation, 4, axis=1)
    normed_attn, attn_pull = jax.vjp(
        modulated_norm, inputs, gain_attn, bias_attn, scale_attn, shift_attn
    )
    attn_low = normed_attn.astype(jnp.bfloat16)
    qkv_low = project(attn_low, w_qkv).astype(jnp.bfloat16)
    queries = qkv_low[:, :, :D].reshape(seq_count, pos_count, HEADS, HEAD_DIM)
    kv_local = qkv_low[:, :, D:]

    def masked_scores(key_heads, key_start):
        key_count = key_heads.shape[1]
        key_pos = key_start + jnp.arange(key_count, dtype=jnp.int32)
        key_keep = (key_pos[None, :] < seq_lengths[:, None])[:, None, None, :]
        scores = (
            jnp.einsum("sqhd,skhd->shqk", queries, key_heads, preferred_element_type=jnp.float32)
            * scale_factor
        )
        return jnp.where(key_keep, scores, NEG_FILL)

    key_piece = lax.all_gather(kv_local, "blk", axis=1, tiled=True)
    run_max = jnp.full((seq_count, HEADS, pos_count), -1e30, jnp.float32)
    key_count = key_piece.shape[1]
    key_heads = key_piece[:, :, :D].reshape(seq_count, key_count, HEADS, HEAD_DIM)
    value_heads = key_piece[:, :, D:].reshape(seq_count, key_count, HEADS, HEAD_DIM)
    scores = masked_scores(key_heads, jnp.int32(0))
    new_max = jnp.maximum(run_max, jnp.max(scores, axis=-1))
    softmax_weights = jnp.exp(scores - new_max[..., None])
    run_sum = jnp.sum(softmax_weights, axis=-1)
    contrib = jnp.einsum(
        "shqk,skhd->sqhd",
        softmax_weights.astype(jnp.bfloat16),
        value_heads,
        preferred_element_type=jnp.float32,
    )
    run_acc = contrib
    run_max, run_sum, run_acc = (new_max, run_sum, run_acc)
    log_total = run_max + jnp.log(run_sum)
    attended = run_acc / jnp.transpose(run_sum, (0, 2, 1))[..., None]
    attended_low = attended.reshape(seq_count, pos_count, D).astype(jnp.bfloat16)
    residual = inputs + project(attended_low, w_out)
    normed_mlp, mlp_pull = jax.vjp(
        modulated_norm, residual, gain_mlp, bias_mlp, scale_mlp, shift_mlp
    )
    mlp_low = normed_mlp.astype(jnp.bfloat16)
    pre_act = project(mlp_low, w_up)
    activated, gelu_pull = jax.vjp(jax.nn.gelu, pre_act)
    hidden_low = activated.astype(jnp.bfloat16)
    final_sum = (residual + project(hidden_low, w_down)) * valid_rows
    layer_out = final_sum.astype(jnp.bfloat16)
    grad_final = cotangent.astype(jnp.float32) * valid_rows
    final_low = grad_final.astype(jnp.bfloat16)
    grad_w_down = outer_sum(hidden_low, final_low)
    (grad_pre,) = gelu_pull(project_back(final_low, w_down))
    pre_low = grad_pre.astype(jnp.bfloat16)
    grad_w_up = outer_sum(mlp_low, pre_low)
    grad_res_norm, grad_gain_mlp, grad_bias_mlp, grad_scale_mlp, grad_shift_mlp = mlp_pull(
        project_back(pre_low, w_up)
    )
    residual_grad = grad_final + grad_res_norm
    residual_low = residual_grad.astype(jnp.bfloat16)
    grad_w_out = outer_sum(attended_low, residual_low)
    grad_att = (
        project_back(residual_low, w_out)
        .astype(jnp.bfloat16)
        .reshape(seq_count, pos_count, HEADS, HEAD_DIM)
    )
    row_delta = jnp.transpose(jnp.sum(grad_att * attended, axis=-1), (0, 2, 1))

    def key_block(kv_block, owner_index):
        key_heads = kv_block[:, :, :D].reshape(seq_count, pos_count, HEADS, HEAD_DIM)
        value_heads = kv_block[:, :, D:].reshape(seq_count, pos_count, HEADS, HEAD_DIM)
        scores = masked_scores(key_heads, owner_index * pos_count)
        softmax_weights = jnp.exp(scores - log_total[..., None])
        grad_weights = jnp.einsum(
            "sqhd,skhd->shqk", grad_att, value_heads, preferred_element_type=jnp.float32
        )
        grad_scores = (
            softmax_weights * (grad_weights - row_delta[..., None]) * scale_factor
        ).astype(jnp.bfloat16)
        grad_queries = jnp.einsum(
            "shqk,skhd->sqhd", grad_scores, key_heads, preferred_element_type=jnp.float32
        )
        grad_keys = jnp.einsum(
            "shqk,sqhd->skhd", grad_scores, queries, preferred_element_type=jnp.float32
        )
        grad_values = jnp.einsum(
            "shqk,sqhd->skhd",
            softmax_weights.astype(jnp.bfloat16),
            grad_att,
            preferred_element_type=jnp.float32,
        )
        joined = jnp.concatenate(
            [
                grad_keys.reshape(seq_count, pos_count, D),
                grad_values.reshape(seq_count, pos_count, D),
            ],
            axis=-1,
        )
        return (grad_queries, joined)

    def pass_back(grad_values):
        return from_behind(grad_values.astype(jnp.bfloat16), "blk", 1).astype(grad_values.dtype)

    zero_kv = jnp.zeros((seq_count, pos_count, 2 * D), jnp.float32)
    zero_query = jnp.zeros((seq_count, pos_count, HEADS, HEAD_DIM), jnp.float32)

    def cycle_step(turn_index, cycle_state):
        kv_block, grad_kv, grad_query = cycle_state
        part_query, part_kv = key_block(kv_block, (cycle_index - turn_index) % cycle_size)
        kv_block = from_behind(kv_block, "blk", 1)
        return (kv_block, pass_back(grad_kv + part_kv), grad_query + part_query)

    kv_block, grad_kv, grad_query = lax.fori_loop(
        0, cycle_size - 1, cycle_step, (kv_local, zero_kv, zero_query)
    )
    part_query, part_kv = key_block(kv_block, (cycle_index + 1) % cycle_size)
    grad_kv = pass_back(grad_kv + part_kv)
    grad_query = grad_query + part_query
    grad_qkv = jnp.concatenate(
        [grad_query.reshape(seq_count, pos_count, D), grad_kv], axis=-1
    ).astype(jnp.bfloat16)
    grad_w_qkv = outer_sum(attn_low, grad_qkv)
    grad_in_norm, grad_gain_attn, grad_bias_attn, grad_scale_attn, grad_shift_attn = attn_pull(
        project_back(grad_qkv, w_qkv)
    )
    input_grad = residual_grad + grad_in_norm
    grad_input = input_grad.astype(jnp.bfloat16)
    grad_w_embed = outer_sum(normed_low, grad_input)
    grad_modulation = jnp.concatenate(
        [grad_scale_attn, grad_shift_attn, grad_scale_mlp, grad_shift_mlp], axis=1
    )
    grad_w_time = jnp.dot(
        time_low.astype(jnp.float32).T, grad_modulation, precision=lax.Precision.HIGHEST
    )
    (grad_rows,) = norm_pull(project_back(grad_input, w_embed))
    flat_ids = token_ids.reshape(-1)
    flat_grads = grad_rows.reshape(-1, EMB)
    row_count = VOCAB // lax.axis_size(("dp", "blk"))
    own_start = lax.axis_index(("dp", "blk")) * row_count
    piece_ids = lax.all_gather(flat_ids, ("dp", "blk"), axis=0, tiled=True)
    piece_grads = lax.all_gather(
        flat_grads.astype(jnp.bfloat16), ("dp", "blk"), axis=0, tiled=True
    ).astype(jnp.float32)
    grad_table = scatter_rows(
        jnp.zeros((row_count, EMB), jnp.float32), piece_ids - own_start, piece_grads
    )
    group_count = lax.axis_size("dp")
    gradients = (
        grad_w_embed,
        grad_w_time,
        grad_gain_attn,
        grad_bias_attn,
        grad_gain_mlp,
        grad_bias_mlp,
        grad_w_qkv,
        grad_w_out,
        grad_w_up,
        grad_w_down,
    )
    grouped = tuple((group_columns(g, group_count) for g in gradients))
    in_group = (
        lax.psum_scatter(
            grouped[0].astype(jnp.bfloat16), "blk", scatter_dimension=2, tiled=True
        ).astype(jnp.float32),
        lax.psum_scatter(
            grouped[1].astype(jnp.bfloat16), "blk", scatter_dimension=2, tiled=True
        ).astype(jnp.float32),
        lax.psum_scatter(
            grouped[2].astype(jnp.bfloat16), "blk", scatter_dimension=2, tiled=True
        ).astype(jnp.float32),
        lax.psum_scatter(
            grouped[3].astype(jnp.bfloat16), "blk", scatter_dimension=2, tiled=True
        ).astype(jnp.float32),
        lax.psum_scatter(
            grouped[4].astype(jnp.bfloat16), "blk", scatter_dimension=2, tiled=True
        ).astype(jnp.float32),
        lax.psum_scatter(
            grouped[5].astype(jnp.bfloat16), "blk", scatter_dimension=2, tiled=True
        ).astype(jnp.float32),
        lax.psum_scatter(
            grouped[6].astype(jnp.bfloat16), "blk", scatter_dimension=2, tiled=True
        ).astype(jnp.float32),
        lax.psum_scatter(
            grouped[7].astype(jnp.bfloat16), "blk", scatter_dimension=2, tiled=True
        ).astype(jnp.float32),
        lax.psum_scatter(
            grouped[8].astype(jnp.bfloat16), "blk", scatter_dimension=2, tiled=True
        ).astype(jnp.float32),
        lax.psum_scatter(
            grouped[9].astype(jnp.bfloat16), "blk", scatter_dimension=2, tiled=True
        ).astype(jnp.float32),
    )
    across = (
        lax.psum_scatter(
            in_group[0].astype(jnp.bfloat16), "dp", scatter_dimension=1, tiled=True
        ).astype(jnp.float32),
        lax.psum_scatter(
            in_group[1].astype(jnp.bfloat16), "dp", scatter_dimension=1, tiled=True
        ).astype(jnp.float32),
        lax.psum_scatter(
            in_group[2].astype(jnp.bfloat16), "dp", scatter_dimension=1, tiled=True
        ).astype(jnp.float32),
        lax.psum_scatter(
            in_group[3].astype(jnp.bfloat16), "dp", scatter_dimension=1, tiled=True
        ).astype(jnp.float32),
        lax.psum_scatter(
            in_group[4].astype(jnp.bfloat16), "dp", scatter_dimension=1, tiled=True
        ).astype(jnp.float32),
        lax.psum_scatter(
            in_group[5].astype(jnp.bfloat16), "dp", scatter_dimension=1, tiled=True
        ).astype(jnp.float32),
        lax.psum_scatter(
            in_group[6].astype(jnp.bfloat16), "dp", scatter_dimension=1, tiled=True
        ).astype(jnp.float32),
        lax.psum_scatter(
            in_group[7].astype(jnp.bfloat16), "dp", scatter_dimension=1, tiled=True
        ).astype(jnp.float32),
        lax.psum_scatter(
            in_group[8].astype(jnp.bfloat16), "dp", scatter_dimension=1, tiled=True
        ).astype(jnp.float32),
        lax.psum_scatter(
            in_group[9].astype(jnp.bfloat16), "dp", scatter_dimension=1, tiled=True
        ).astype(jnp.float32),
    )
    summed = tuple(
        (
            a.reshape(g.shape[:-1] + (a.shape[-1],)) if g.ndim == 2 else a.reshape(a.shape[-1])
            for a, g in zip(across, gradients)
        )
    )
    return (
        layer_out,
        grad_input,
        grad_table,
        summed[0],
        summed[1],
        summed[2],
        summed[3],
        summed[4],
        summed[5],
        summed[6],
        summed[7],
        summed[8],
        summed[9],
    )


BF16 = jnp.bfloat16
F32 = jnp.float32
LOG2_E = 1.4426950408889634
VMEM_BYTES = 58 * 1024 * 1024
META_ROWS = 4
SLOT_ROWS = 64
EXACT_BASE = 256
TOKEN_TILE = 256
ANY_SPEC = pl.BlockSpec(memory_space=pl.ANY)


def dot_nn(left, right):
    return lax.dot_general(left, right, (((1,), (0,)), ((), ())), preferred_element_type=F32)


def dot_nt(left, right):
    return lax.dot_general(left, right, (((1,), (1,)), ((), ())), preferred_element_type=F32)


def dot_tn(left, right):
    return lax.dot_general(left, right, (((0,), (0,)), ((), ())), preferred_element_type=F32)


def head_operands(queries, keys, head, length):
    lane = lax.broadcasted_iota(jnp.int32, queries.shape, 1)
    row = lax.broadcasted_iota(jnp.int32, queries.shape, 0)
    mine = (lane // HEAD_DIM) == head
    spare = lane == (1 - head) * HEAD_DIM
    zero = jnp.zeros_like(queries)
    fill = jnp.where(row >= length, jnp.full_like(queries, NEG_FILL), zero)
    one_query = jnp.where(mine, queries, jnp.where(spare, jnp.ones_like(queries), zero))
    one_key = jnp.where(mine, keys, jnp.where(spare, fill, zero))
    return mine, one_query, one_key


def attend_kernel(length_ref, q_ref, k_ref, v_ref, out_ref, lse_ref):
    length = length_ref[0]
    factor = LOG2_E * HEAD_DIM**-0.5
    rows = []
    for head in range(2):
        mine, one_query, one_key = head_operands(q_ref[...], k_ref[...], head, length)
        value_one = jnp.where(mine, v_ref[...], jnp.ones_like(v_ref[...]))
        scores = dot_nt(one_key, one_query)
        top = jnp.max(scores, axis=0, keepdims=True)
        weights = jnp.exp2(scores * factor - top * factor).astype(BF16)
        mixed = dot_tn(value_one, weights)
        other = (1 - head) * HEAD_DIM
        total = mixed[other : other + 1]
        lse_ref[0, head : head + 1, :] = top * factor + jnp.log2(total)
        rows.append(mixed[head * HEAD_DIM : (head + 1) * HEAD_DIM] * (1.0 / total))
    out_ref[...] = jnp.transpose(jnp.concatenate(rows, axis=0), (1, 0)).astype(BF16)


def attend_back_kernel(
    length_ref, q_ref, k_ref, v_ref, out_ref, grad_ref, lse_ref, dq_ref, dk_ref, dv_ref, *, chunk
):
    length = length_ref[0]
    positions = q_ref.shape[0]
    factor = LOG2_E * HEAD_DIM**-0.5
    scale = HEAD_DIM**-0.5
    grad = grad_ref[...]
    product = grad.astype(F32) * out_ref[...].astype(F32)
    high = product.astype(BF16)
    low = (product - high.astype(F32)).astype(BF16)
    head_of_lane = lax.broadcasted_iota(jnp.int32, (16, 2 * HEAD_DIM), 1) // HEAD_DIM
    picker = jnp.where(
        head_of_lane == lax.broadcasted_iota(jnp.int32, (16, 2 * HEAD_DIM), 0), 1.0, 0.0
    ).astype(BF16)
    delta = dot_nt(picker, high) + dot_nt(picker, low)
    query_rows = []
    key_parts = ([], [])
    value_parts = ([], [])
    for head in range(2):
        mine, one_query, one_key = head_operands(q_ref[...], k_ref[...], head, length)
        one_value = jnp.where(mine, v_ref[...], jnp.zeros_like(v_ref[...]))
        lse = lse_ref[0, head : head + 1, :]
        row_delta = delta[head : head + 1, :]
        query_grad = jnp.zeros((2 * HEAD_DIM, positions), F32)
        for start in range(0, positions, chunk):
            span = slice(start, start + chunk)
            weights = jnp.exp2(dot_nt(one_key[span], one_query) * factor - lse)
            weight_grad = dot_nt(one_value[span], grad)
            score_grad = (weights * (weight_grad - row_delta)).astype(BF16)
            value_parts[head].append(dot_nn(weights.astype(BF16), grad))
            key_parts[head].append(dot_nn(score_grad, q_ref[...]))
            query_grad = query_grad + dot_tn(k_ref[span, :], score_grad)
        query_rows.append(query_grad[head * HEAD_DIM : (head + 1) * HEAD_DIM])
    first = lax.broadcasted_iota(jnp.int32, (chunk, 2 * HEAD_DIM), 1) < HEAD_DIM
    for part, start in enumerate(range(0, positions, chunk)):
        span = slice(start, start + chunk)
        dk_ref[span, :] = (jnp.where(first, key_parts[0][part], key_parts[1][part]) * scale).astype(BF16)
        dv_ref[span, :] = jnp.where(first, value_parts[0][part], value_parts[1][part]).astype(BF16)
    dq_ref[...] = jnp.transpose(jnp.concatenate(query_rows, axis=0) * scale, (1, 0)).astype(BF16)


def gelu_with_slope(values):
    root = math.sqrt(2.0 / math.pi)
    square = values * values
    share = 0.5 + 0.5 * jnp.tanh(values * (root + root * 0.044715 * square))
    result = values * share
    slope = share + (result - result * share) * (2.0 * root + 6.0 * root * 0.044715 * square)
    return result, slope


def swap_core(value):
    return lax.ppermute(value, "blk", [(0, 1), (1, 0)])


def join_halves(core, own, other):
    first = jnp.where(core == 0, own, other)
    second = jnp.where(core == 0, other, own)
    return jnp.concatenate([first, second], axis=0)


def to_whole(core, local):
    own = lax.dynamic_index_in_dim(local, core, 0, keepdims=False)
    away = lax.dynamic_index_in_dim(local, 1 - core, 0, keepdims=False)
    return join_halves(core, own, swap_core(away))


def fill_other(core, value, arrived):
    return lax.dynamic_update_index_in_dim(value, arrived, 1 - core, 0)


COST_SHARE = 1.0


def kernel_cost(microseconds):
    flops = int(COST_SHARE * microseconds * 1e9)
    return pl.CostEstimate(flops=flops, bytes_accessed=1024, transcendentals=0)


def run_kernel(
    body, grid, scalars, inputs, in_specs, out_specs, out_shape, microseconds, name, scratch=(), carried=()
):
    scalar_count, input_count, output_count = len(scalars), len(inputs), len(out_shape)
    carried_count = len(carried)
    first_carried = scalar_count + input_count

    def kernel(*refs):
        rest = refs[first_carried + carried_count :]
        body(*refs[:first_carried], *rest[:output_count], *rest[output_count + carried_count :])

    results = pl.pallas_call(
        kernel,
        grid_spec=pltpu.PrefetchScalarGridSpec(
            num_scalar_prefetch=scalar_count,
            grid=grid,
            in_specs=list(in_specs) + [ANY_SPEC] * carried_count,
            out_specs=list(out_specs) + [ANY_SPEC] * carried_count,
            scratch_shapes=list(scratch),
        ),
        out_shape=list(out_shape) + [jax.ShapeDtypeStruct(c.shape, c.dtype) for c in carried],
        input_output_aliases={first_carried + i: output_count + i for i in range(carried_count)},
        compiler_params=pltpu.CompilerParams(vmem_limit_bytes=VMEM_BYTES),
        cost_estimate=kernel_cost(microseconds),
        name=name,
    )(*scalars, *inputs, *carried)
    return results[:output_count], results[output_count:]


def behind(*arrays):
    def kernel(*refs):
        pass

    return pl.pallas_call(
        kernel,
        in_specs=[ANY_SPEC] * len(arrays),
        out_specs=[ANY_SPEC] * len(arrays),
        out_shape=[jax.ShapeDtypeStruct(a.shape, a.dtype) for a in arrays],
        input_output_aliases={i: i for i in range(len(arrays))},
        compiler_params=pltpu.CompilerParams(vmem_limit_bytes=VMEM_BYTES),
        cost_estimate=kernel_cost(0),
        name="behind",
    )(*arrays)


FEED_TILE = 512


def shaped(dtype, *shape):
    return jax.ShapeDtypeStruct(shape, dtype)


def row_spec(tile, columns):
    return pl.BlockSpec((tile, columns), lambda i, *scalars: (i, 0))


def fixed_spec(*shape):
    return pl.BlockSpec(shape, lambda *grid: (0,) * len(shape))


def attend(length, qkv):
    positions = qkv.shape[0]
    pairs = HEADS // 2

    def spec(group):
        return pl.BlockSpec((positions, 2 * HEAD_DIM), lambda pair, length: (0, group * pairs + pair))

    results, _ = run_kernel(
        attend_kernel,
        (pairs,),
        [length],
        [qkv, qkv, qkv],
        [spec(0), spec(1), spec(2)],
        [spec(0), pl.BlockSpec((1, 2, positions), lambda pair, length: (pair, 0, 0))],
        [shaped(BF16, positions, D), shaped(F32, pairs, 2, positions)],
        30,
        "attend",
    )
    return results


def attend_back(length, qkv, attended, grad_att, lse, part, parts, grads, carried):
    positions = qkv.shape[0]
    pairs = HEADS // 2
    count = pairs // parts
    shift = part * count

    def spec(group):
        return pl.BlockSpec(
            (positions, 2 * HEAD_DIM), lambda pair, length: (0, group * pairs + shift + pair)
        )

    lse_spec = pl.BlockSpec((1, 2, positions), lambda pair, length: (shift + pair, 0, 0))
    inputs = [qkv, qkv, qkv, attended, grad_att, lse]
    held = len(grads)
    kept = len(carried)

    def kernel(*refs):
        attend_back_kernel(*refs[:7], *refs[7 + held + kept : 10 + held + kept], chunk=min(512, positions))

    aliases = {7 + i: i for i in range(held)}
    aliases.update({7 + held + i: 3 + i for i in range(kept)})
    results = pl.pallas_call(
        kernel,
        grid_spec=pltpu.PrefetchScalarGridSpec(
            num_scalar_prefetch=1,
            grid=(count,),
            in_specs=[spec(0), spec(1), spec(2), spec(0), spec(0), lse_spec] + [ANY_SPEC] * (held + kept),
            out_specs=[spec(0)] * 3 + [ANY_SPEC] * kept,
        ),
        out_shape=[shaped(BF16, positions, D)] * 3 + [jax.ShapeDtypeStruct(c.shape, c.dtype) for c in carried],
        input_output_aliases=aliases,
        compiler_params=pltpu.CompilerParams(vmem_limit_bytes=VMEM_BYTES),
        cost_estimate=kernel_cost(46 / parts),
        name="attend_back",
    )(length, *inputs, *grads, *carried)
    return results[:3], results[3:]


def norm_rows(features):
    center = features - jnp.mean(features, axis=-1, keepdims=True)
    rstd = lax.rsqrt(jnp.mean(center * center, axis=-1, keepdims=True) + 1e-05)
    return center * rstd, rstd


def norm_rows_back(grad_norm, xhat, rstd, gain_row):
    scaled = grad_norm * gain_row
    mean_scaled = jnp.mean(scaled, axis=-1, keepdims=True)
    mean_cross = jnp.mean(scaled * xhat, axis=-1, keepdims=True)
    return rstd * (scaled - mean_scaled - xhat * mean_cross)


def add_column_sums(sums_ref, grad_norm, xhat):
    sums_ref[0:1, :] += jnp.sum(grad_norm * xhat, axis=0, keepdims=True)
    sums_ref[1:2, :] += jnp.sum(grad_norm, axis=0, keepdims=True)


def split_specs(count, tile):
    steps = count // tile // 2

    def early(i):
        return jnp.minimum(i, steps - 1)

    def late(i):
        return jnp.maximum(i - steps, 0)

    def own(i, *scalars):
        core = scalars[-1][0]
        return core, jnp.where(core == 0, early(i), late(i)), 0

    def other(i, *scalars):
        return jnp.where(scalars[-1][0] == 0, late(i), early(i)), 0

    return [pl.BlockSpec((1, tile, D), own), pl.BlockSpec((tile, D), other)]


def store_split(core, own_ref, other_ref, value):
    half = pl.program_id(0) * 2 // pl.num_programs(0)

    @pl.when(half == core)
    def _():
        own_ref[0] = value

    @pl.when(half != core)
    def _():
        other_ref[...] = value


def valid_column(length, tile):
    row = lax.broadcasted_iota(jnp.int32, (tile, 1), 0) + pl.program_id(0) * tile
    return row < length


def share_out(core, value, keep_ref, away_ref):
    rows = keep_ref.shape[-2]
    if len(keep_ref.shape) == 4:
        outer, inner = keep_ref.shape[:2]
        value = value.astype(BF16).reshape(outer, inner, 2, rows, value.shape[1])
        first, second = value[:, :, 0], value[:, :, 1]
        keep_ref[...] = jnp.where(core == 0, first, second)
        away_ref[...] = jnp.where(core == 0, second, first)
        return
    groups = keep_ref.shape[0]
    value = value.astype(BF16).reshape(groups, 2, rows, value.shape[1])
    first, second = value[:, 0], value[:, 1]
    keep_ref[...] = jnp.where(core == 0, first, second)
    away_ref[...] = jnp.where(core == 0, second, first)


def embed_kernel(emb_ref, we_ref, gain_ref, shift_ref, wqkv_ref, low_ref, in_ref, attn_ref, qkv_ref):
    rows = emb_ref[...].astype(F32)
    normed = rows * lax.rsqrt(jnp.mean(rows * rows, axis=-1, keepdims=True) + 1e-06)
    low = normed.astype(BF16)
    low_ref[...] = low
    inputs = dot_nn(low, we_ref[...])
    in_ref[...] = inputs.astype(BF16)
    xhat, _ = norm_rows(inputs)
    attn = (xhat * gain_ref[...] + shift_ref[...]).astype(BF16)
    attn_ref[...] = attn
    qkv_ref[...] = dot_nn(attn, wqkv_ref[...]).astype(BF16)


def embed_and_project(emb, w_embed, gain_row, shift_row, w_qkv):
    count = emb.shape[0]
    tile = TOKEN_TILE
    results, _ = run_kernel(
        embed_kernel,
        (count // tile,),
        [],
        [emb, w_embed, gain_row, shift_row, w_qkv],
        [row_spec(tile, EMB), fixed_spec(EMB, D), fixed_spec(1, D), fixed_spec(1, D), fixed_spec(D, 3 * D)],
        [row_spec(tile, EMB), row_spec(tile, D), row_spec(tile, D), row_spec(tile, 3 * D)],
        [shaped(BF16, count, EMB), shaped(BF16, count, D), shaped(BF16, count, D), shaped(BF16, count, 3 * D)],
        12,
        "embed_and_project",
    )
    return results


def residual_kernel(
    length_ref, core_ref, att_ref, in_ref, wo_ref, gain_ref, shift_ref, cot_ref, cot_other_ref,
    res_ref, mlp_ref, fin_ref
):
    residual = in_ref[...].astype(F32) + dot_nn(att_ref[...], wo_ref[...])
    res_ref[...] = residual.astype(BF16)
    xhat, _ = norm_rows(residual)
    mlp_ref[...] = (xhat * gain_ref[...] + shift_ref[...]).astype(BF16)
    half = pl.program_id(0) * 2 // pl.num_programs(0)
    cot = jnp.where(half == core_ref[0], cot_ref[0], cot_other_ref[...])
    fin_ref[...] = jnp.where(valid_column(length_ref[0], cot.shape[0]), cot, jnp.zeros_like(cot))


def attention_residual(length, core, attended, inputs, w_out, gain_row, shift_row, cot, cot_other):
    count = attended.shape[0]
    row = row_spec(TOKEN_TILE, D)
    results, _ = run_kernel(
        residual_kernel,
        (count // TOKEN_TILE,),
        [length, core],
        [attended, inputs, w_out, gain_row, shift_row, cot, cot_other],
        [row, row, fixed_spec(D, D), fixed_spec(1, D), fixed_spec(1, D)] + split_specs(count, TOKEN_TILE),
        [row, row, row],
        [shaped(BF16, count, D)] * 3,
        8,
        "attention_residual",
    )
    return results


def feed_forward_kernel(
    core_ref, mlp_ref, fin_ref, wu_ref, wd_ref, down_in_ref, grad_in_ref,
    gwd_keep_ref, gwd_away_ref, gwu_keep_ref, gwu_away_ref, down_ref, grad_ref,
    fin_t_ref, hid_ref, pre_ref, *, first
):
    core = core_ref[0]
    count = mlp_ref.shape[0]

    @pl.when(pl.program_id(0) == 0)
    def _():
        fin_t_ref[...] = jnp.transpose(fin_ref[...], (1, 0))
        if first:
            down_ref[...] = jnp.zeros_like(down_ref)
            grad_ref[...] = jnp.zeros_like(grad_ref)
        else:
            down_ref[...] = down_in_ref[...]
            grad_ref[...] = grad_in_ref[...]

    for start in range(0, count, FEED_TILE):
        span = slice(start, start + FEED_TILE)
        hidden, slope = gelu_with_slope(dot_nn(mlp_ref[span, :], wu_ref[...]))
        hid_ref[span, :] = hidden.astype(BF16)
        pre_ref[span, :] = (dot_nt(fin_ref[span, :], wd_ref[...]) * slope).astype(BF16)
    share_out(core, dot_nn(fin_t_ref[...], hid_ref[...]), gwd_keep_ref, gwd_away_ref)
    share_out(core, dot_tn(pre_ref[...], mlp_ref[...]), gwu_keep_ref, gwu_away_ref)
    for start in range(0, count, FEED_TILE):
        span = slice(start, start + FEED_TILE)
        down_ref[span, :] += dot_nn(hid_ref[span, :], wd_ref[...])
        grad_ref[span, :] += dot_nt(pre_ref[span, :], wu_ref[...])


def feed_forward(core, groups, part, parts, mlp_low, final_low, w_up, w_down, down, grad, carried, tile=512):
    count = mlp_low.shape[0]
    width = w_up.shape[1] // parts
    steps = width // tile
    shift = part * steps
    first = down is None
    if first:
        down = grad = jnp.zeros((8, 128), F32)
    down_rows = D // (2 * groups)
    up_rows = w_up.shape[1] // (2 * groups)
    down_share = (groups // 4, 4, down_rows)
    down_spec = pl.BlockSpec((*down_share, tile), lambda j, core: (0, 0, 0, j))
    up_spec = pl.BlockSpec((tile // (2 * up_rows), up_rows, D), lambda j, core: (j, 0, 0))
    whole = fixed_spec(count, D)
    return run_kernel(
        functools.partial(feed_forward_kernel, first=first),
        (steps,),
        [core],
        [mlp_low, final_low, w_up, w_down, down, grad],
        [
            whole,
            whole,
            pl.BlockSpec((D, tile), lambda j, core: (0, shift + j)),
            pl.BlockSpec((tile, D), lambda j, core: (shift + j, 0)),
            fixed_spec(*down.shape),
            fixed_spec(*down.shape),
        ],
        [down_spec, down_spec, up_spec, up_spec, whole, whole],
        [shaped(BF16, *down_share, width)] * 2
        + [shaped(BF16, groups // parts, up_rows, D)] * 2
        + [shaped(F32, count, D)] * 2,
        36,
        "feed_forward",
        scratch=[pltpu.VMEM((D, count), BF16), pltpu.VMEM((count, tile), BF16), pltpu.VMEM((count, tile), BF16)],
        carried=carried,
    )


def middle_kernel(
    length_ref, core_ref, down_ref, gmn_ref, res_ref, fin_ref, gain_ref, wo_ref, att_ref,
    out_ref, out_away_ref, low_ref, gatt_ref, gwo_keep_ref, gwo_away_ref, sums_ref, acc_ref
):
    step = pl.program_id(0)

    @pl.when(step == 0)
    def _():
        sums_ref[...] = jnp.zeros_like(sums_ref)
        acc_ref[...] = jnp.zeros_like(acc_ref)

    residual = res_ref[...].astype(F32)
    keep = valid_column(length_ref[0], residual.shape[0])
    final = jnp.where(keep, residual + down_ref[...], 0.0).astype(BF16)
    store_split(core_ref[0], out_ref, out_away_ref, final)
    xhat, rstd = norm_rows(residual)
    grad = gmn_ref[...]
    add_column_sums(sums_ref, grad, xhat)
    low = (fin_ref[...].astype(F32) + norm_rows_back(grad, xhat, rstd, gain_ref[...])).astype(BF16)
    low_ref[...] = low
    gatt_ref[...] = dot_nt(low, wo_ref[...]).astype(BF16)
    acc_ref[...] += dot_tn(low, att_ref[...])

    @pl.when(step == pl.num_programs(0) - 1)
    def _():
        share_out(core_ref[0], acc_ref[...], gwo_keep_ref, gwo_away_ref)


def feed_forward_to_attention(
    length, core, groups, down, grad_mlp_norm, residual, final_low, gain_row, w_out, attended, carried
):
    count = residual.shape[0]
    row = row_spec(TOKEN_TILE, D)
    share = (groups // 4, 4, D // (2 * groups), D)
    return run_kernel(
        middle_kernel,
        (count // TOKEN_TILE,),
        [length, core],
        [down, grad_mlp_norm, residual, final_low, gain_row, w_out, attended],
        [row, row, row, row, fixed_spec(1, D), fixed_spec(D, D), row],
        split_specs(count, TOKEN_TILE) + [row, row, fixed_spec(*share), fixed_spec(*share), fixed_spec(8, D)],
        [shaped(BF16, 2, count // 2, D), shaped(BF16, count // 2, D)] + [shaped(BF16, count, D)] * 2 + [shaped(BF16, *share)] * 2 + [shaped(F32, 8, D)],
        15,
        "feed_forward_to_attention",
        scratch=[pltpu.VMEM((D, D), F32)],
        carried=carried,
    )


def outer_kernel(core_ref, dq_ref, dk_ref, dv_ref, right_ref, keep_ref, away_ref, all_ref):
    right = right_ref[...]
    for group, ref in enumerate((dq_ref, dk_ref, dv_ref)):
        for start in range(0, D, TOKEN_TILE):
            rows = slice(group * D + start, group * D + start + TOKEN_TILE)
            all_ref[rows, :] = dot_tn(ref[:, start : start + TOKEN_TILE], right).astype(BF16)
    share_out(core_ref[0], all_ref[...], keep_ref, away_ref)


def outer_qkv(core, groups, grads, right, half, carried):
    count = right.shape[0]
    columns = right.shape[1] // 2
    share = (groups, 3 * D // (2 * groups), columns)
    return run_kernel(
        outer_kernel,
        (1,),
        [core],
        [*grads, right],
        [fixed_spec(count, D)] * 3 + [pl.BlockSpec((count, columns), lambda i, core: (0, half))],
        [fixed_spec(*share)] * 2,
        [shaped(BF16, *share)] * 2,
        8,
        "outer_qkv",
        scratch=[pltpu.VMEM((3 * D, columns), BF16)],
        carried=carried,
    )


def input_kernel(
    core_ref, dq_ref, dk_ref, dv_ref, wqkv_ref, in_ref, low_ref, gain_ref, we_ref, emb_ref, nl_ref,
    grad_ref, grad_away_ref, rows_ref, gwe_keep_ref, gwe_away_ref, sums_ref, acc_ref
):
    step = pl.program_id(0)

    @pl.when(step == 0)
    def _():
        sums_ref[...] = jnp.zeros_like(sums_ref)
        acc_ref[...] = jnp.zeros_like(acc_ref)

    grad = (
        dot_nt(dq_ref[...], wqkv_ref[:, :D])
        + dot_nt(dk_ref[...], wqkv_ref[:, D : 2 * D])
        + dot_nt(dv_ref[...], wqkv_ref[:, 2 * D :])
    )
    xhat, rstd = norm_rows(in_ref[...].astype(F32))
    add_column_sums(sums_ref, grad, xhat)
    low = (low_ref[...].astype(F32) + norm_rows_back(grad, xhat, rstd, gain_ref[...])).astype(BF16)
    store_split(core_ref[0], grad_ref, grad_away_ref, low)
    acc_ref[...] += dot_tn(low, nl_ref[...])
    back = dot_nt(low, we_ref[...])
    emb = emb_ref[...].astype(F32)
    emb_rstd = lax.rsqrt(jnp.mean(emb * emb, axis=-1, keepdims=True) + 1e-06)
    normed = emb * emb_rstd
    rows_ref[...] = (emb_rstd * (back - normed * jnp.mean(normed * back, axis=-1, keepdims=True))).astype(BF16)

    @pl.when(step == pl.num_programs(0) - 1)
    def _():
        share_out(core_ref[0], acc_ref[...], gwe_keep_ref, gwe_away_ref)


def input_gradient(core, groups, grads, w_qkv, inputs, residual_low, gain_row, w_embed, emb, normed_low, carried):
    count = inputs.shape[0]
    tile = TOKEN_TILE
    share = (2 * groups, D // (4 * groups), EMB)
    row, narrow = row_spec(tile, D), row_spec(tile, EMB)
    return run_kernel(
        input_kernel,
        (count // tile,),
        [core],
        [*grads, w_qkv, inputs, residual_low, gain_row, w_embed, emb, normed_low],
        [row, row, row, fixed_spec(D, 3 * D), row, row, fixed_spec(1, D), fixed_spec(EMB, D), narrow, narrow],
        split_specs(count, tile) + [narrow, fixed_spec(*share), fixed_spec(*share), fixed_spec(8, D)],
        [shaped(BF16, 2, count // 2, D), shaped(BF16, count // 2, D), shaped(BF16, count, EMB)] + [shaped(BF16, *share)] * 2 + [shaped(F32, 8, D)],
        16,
        "input_gradient",
        scratch=[pltpu.VMEM((D, EMB), F32)],
        carried=carried,
    )


def exchange(value, bit, dp_bits, pattern=1):
    return lax.ppermute(value, "dp", [(i, i ^ (pattern << bit)) for i in range(1 << dp_bits)])


class Halving:
    def __init__(self, labels, dp_bits, flat):
        self.labels = list(labels)
        self.flat = flat
        self.dp_bits = dp_bits
        self.terms = []
        self.fixed = {}

    def over_cores(self, keep, away):
        labels = tuple(self.labels)
        shape = keep.shape if self.flat else (2,) * len(labels) + keep.shape[1:]
        self.terms = [(keep.reshape(shape), labels), (swap_core(away).reshape(shape), labels)]

    @property
    def keep(self):
        return self.terms[0][0]

    @keep.setter
    def keep(self, value):
        self.terms[0] = (value, self.terms[0][1])

    def part(self, fixed):
        total = 0.0
        for value, labels in self.terms:
            spans = [label not in fixed for label in labels]
            starts = [0 if span else fixed[label] for span, label in zip(spans, labels)] + [0, 0]
            sizes = [2 if span else 1 for span in spans] + list(value.shape[-2:])
            piece = lax.dynamic_slice(value.reshape((2,) * len(labels) + value.shape[-2:]), starts, sizes)
            left = (-1,) if self.flat else (2,) * sum(spans)
            total = total + piece.reshape(left + value.shape[-2:]).astype(F32)
        return total

    def total(self):
        return self.part(self.fixed)

    def away(self, bit_label):
        bit = (lax.axis_index("dp") >> bit_label) & 1
        return self.part({**self.fixed, bit_label: 1 - bit}).astype(BF16)

    def send(self, bit_label, away):
        self.fixed[bit_label] = (lax.axis_index("dp") >> bit_label) & 1
        labels = tuple(label for label in self.labels if label not in self.fixed)
        self.terms.append((exchange(away, bit_label, self.dp_bits), labels))


def between_planes(value, dp_bits):
    plane = lax.axis_index("dp") >> 2
    parts = [lax.dynamic_index_in_dim(value, plane, 0, keepdims=False)]
    for step in range(1, value.shape[0]):
        away = lax.dynamic_index_in_dim(value, plane ^ step, 0, keepdims=False)
        parts.append(exchange(away, 2, dp_bits, step))
    return parts


def whole_sequence_shards(
    token_ids,
    seq_lengths,
    diffusion_time,
    embed_table,
    w_embed,
    w_time,
    gain_attn,
    bias_attn,
    gain_mlp,
    bias_mlp,
    w_qkv,
    w_out,
    w_up,
    w_down,
    cotangent,
):
    core = lax.axis_index("blk")
    cores = core.reshape(1).astype(jnp.int32)
    groups = lax.axis_size("dp")
    devices = 2 * groups
    dp_bits = groups.bit_length() - 1
    everywhere = ("dp", "blk")
    labels = list(reversed(range(dp_bits)))
    planes = [[4 * high + low for low in range(4)] for high in range(groups // 4)]
    lines = [[4 * high + low for high in range(groups // 4)] for low in range(4)]
    ids = to_whole(core, token_ids)
    cot_other = swap_core(lax.dynamic_index_in_dim(cotangent, 1 - core, 0, keepdims=False))
    positions = ids.shape[0]
    length = lax.dynamic_index_in_dim(seq_lengths, core, 0, keepdims=True)
    time = lax.dynamic_index_in_dim(diffusion_time, core, 0, keepdims=True)
    emb = embed_table[ids]

    valid = jnp.arange(positions, dtype=jnp.int32) < length[0]
    row_count = VOCAB // devices
    owner = jnp.where(valid, ids // row_count, -1)
    offset = ids % row_count
    slots = SLOT_ROWS - META_ROWS
    member = owner[:, None] == jnp.arange(devices, dtype=jnp.int32)[None, :]
    earlier = jnp.arange(positions)[:, None] > jnp.arange(positions)[None, :]
    before = dot_nn(earlier.astype(BF16), member.astype(BF16))
    rank = jnp.sum(jnp.where(member, before, 0.0), axis=1).astype(jnp.int32)
    most = jnp.max(jnp.sum(member.astype(jnp.int32), axis=0))
    offset_digits = jnp.stack(
        [(offset // EXACT_BASE).astype(BF16), (offset % EXACT_BASE).astype(BF16), jnp.ones(positions, BF16)],
        axis=1,
    )

    def dispatch(turn):
        slot = rank - turn * slots
        inside = (owner >= 0) & (slot >= 0) & (slot < slots)
        target = jnp.where(inside, owner * SLOT_ROWS + META_ROWS + slot, -1)
        place = jnp.arange(devices * SLOT_ROWS, dtype=jnp.int32)[:, None] == target[None, :]
        digits = dot_nn(place.astype(BF16), offset_digits).reshape(devices, SLOT_ROWS, 3)
        head = jnp.transpose(digits, (0, 2, 1)).reshape(devices, 1, 3 * SLOT_ROWS)
        peak = jnp.stack([most // EXACT_BASE, most % EXACT_BASE]).astype(F32)
        peak = jnp.broadcast_to(peak, (devices, 1, 2))
        gap = jnp.zeros((devices, 1, EMB - 3 * SLOT_ROWS - 2), F32)
        return target, jnp.concatenate([head, peak, gap], axis=2)

    meta_target = jnp.arange(devices * META_ROWS, dtype=jnp.int32)
    meta_target = meta_target // META_ROWS * SLOT_ROWS + meta_target % META_ROWS

    def packed(target, meta, grads):
        meta = meta.astype(BF16).reshape(devices * META_ROWS, EMB)
        target = jnp.concatenate([target, meta_target])
        place = jnp.arange(devices * SLOT_ROWS, dtype=jnp.int32)[:, None] == target[None, :]
        rows = dot_nn(place.astype(BF16), jnp.concatenate([grads, meta]))
        return rows.astype(BF16).reshape(devices, SLOT_ROWS, EMB)

    def deliver(rows):
        return lax.all_to_all(rows, everywhere, 0, 0, tiled=True)

    def collect(rows):
        head = rows[:, 0].astype(F32)
        high, low, used = (head[:, i * SLOT_ROWS : (i + 1) * SLOT_ROWS] for i in range(3))
        row = jnp.where(used > 0.5, high * EXACT_BASE + low, -1.0).astype(jnp.int32)
        row = jnp.pad(row, ((0, 0), (0, rows.shape[1] - SLOT_ROWS)), constant_values=-1)
        hit = jnp.arange(row_count, dtype=jnp.int32)[:, None] == row.reshape(1, -1)
        return dot_nn(hit.astype(BF16), rows.reshape(-1, EMB))

    first_target, first_head = dispatch(0)

    def over_cores(keep, arrived):
        return (keep.astype(F32) + arrived.astype(F32)).astype(BF16)

    def scattered(value, index_groups):
        return lax.psum_scatter(value, "dp", scatter_dimension=0, axis_index_groups=index_groups, tiled=True)[0]

    time_low = time_features(time, TIME_WIDTH).astype(BF16)
    modulation = dot_nn(time_low, w_time)
    scale_attn, shift_attn, scale_mlp, shift_mlp = jnp.split(modulation, 4, axis=1)
    gain_row_attn = gain_attn + scale_attn
    gain_row_mlp = gain_mlp + scale_mlp
    normed_low, inputs, attn_low, qkv = embed_and_project(
        emb, w_embed, gain_row_attn, bias_attn + shift_attn, w_qkv
    )
    attended, lse = attend(length, qkv)
    residual, mlp_low, final_low = attention_residual(
        length, cores, attended, inputs, w_out, gain_row_mlp, bias_mlp + shift_mlp, cotangent, cot_other
    )

    hidden_width = w_up.shape[1]
    feed = functools.partial(feed_forward, cores, groups)
    (keep_d, away_d, keep_u, away_u, down, grad), _ = feed(
        0, 2, mlp_low, final_low, w_up, w_down, None, None, []
    )
    up_0, up_1 = Halving(labels[1:], dp_bits, True), Halving(labels[1:], dp_bits, True)
    qkv_a, qkv_b = Halving(labels, dp_bits, False), Halving(labels, dp_bits, False)
    up_0.over_cores(keep_u, away_u)
    arrived_d = swap_core(away_d)
    (next_keep, next_away, keep_u, away_u, down, grad), (up_0.keep, keep_d) = feed(
        1, 2, mlp_low, final_low, w_up, w_down, down, grad, [up_0.keep, keep_d]
    )
    away, down_0, next_keep, next_away, keep_u, away_u = behind(
        up_0.away(0), over_cores(keep_d, arrived_d), next_keep, next_away, keep_u, away_u
    )
    up_0.send(0, away)
    up_1.over_cores(keep_u, away_u)
    arrived_d = swap_core(next_away)
    down_0 = scattered(down_0, lines)
    (layer_out, layer_away, residual_low, grad_att, keep_o, away_o, sums_mlp), kept = feed_forward_to_attention(
        length, cores, groups, down, grad, residual, final_low, gain_row_mlp, w_out, attended,
        [up_0.keep, up_1.keep, next_keep],
    )
    up_0.keep, up_1.keep, keep_d = kept
    away_0, away_1, down_1, keep_o, away_o = behind(
        up_0.away(1), up_1.away(0), over_cores(keep_d, arrived_d), keep_o, away_o
    )
    up_0.send(1, away_0)
    up_1.send(0, away_1)
    down_1 = scattered(down_1, lines)
    arrived_o = swap_core(away_o)
    back = functools.partial(attend_back, length, qkv, attended, grad_att, lse)
    grads, (up_0.keep, up_1.keep, keep_o) = back(0, 2, [], [up_0.keep, up_1.keep, keep_o])
    away_1, out_sum, up_first = behind(
        up_1.away(1), over_cores(keep_o, arrived_o), up_0.total().astype(BF16)
    )
    up_1.send(1, away_1)
    out_sum = scattered(out_sum, lines)
    grads, (up_1.keep, up_first, down_0) = back(1, 2, grads, [up_1.keep, up_first, down_0])
    up_rows = [up_first, up_1.total().astype(BF16)]
    up_rows = jnp.concatenate(up_rows)
    up_sum = scattered(up_rows, lines)
    (keep_a, away_a), (down_1,) = outer_qkv(cores, groups, grads, attn_low, 0, [down_1])
    keep_a, away_a = behind(keep_a, away_a)
    qkv_a.over_cores(keep_a, away_a)
    orders = [(0, 1), (1, 0)]
    (keep_b, away_b), (qkv_a.keep, down_1) = outer_qkv(
        cores, groups, grads, attn_low, 1, [qkv_a.keep, down_1]
    )
    in_plane = jnp.concatenate([down_0, down_1, out_sum], axis=2)
    away_a, keep_b, away_b, in_plane = behind(qkv_a.away(orders[0][0]), keep_b, away_b, in_plane)
    own_sum = scattered(in_plane, planes)
    qkv_a.send(orders[0][0], away_a)
    qkv_b.over_cores(keep_b, away_b)
    qkv_b.send(orders[1][0], *behind(qkv_b.away(orders[1][0])))
    (grad_input, input_away, grad_rows, keep_e, away_e, sums_attn), kept = input_gradient(
        cores, groups, grads, w_qkv, inputs, residual_low, gain_row_attn, w_embed, emb, normed_low,
        [qkv_a.keep, qkv_b.keep],
    )
    qkv_a.keep, qkv_b.keep = kept

    grad_modulation = jnp.concatenate([sums_attn[0], sums_attn[1], sums_mlp[0], sums_mlp[1]])
    gain_columns = jnp.transpose(grad_modulation.reshape(4, devices, -1), (1, 0, 2)).reshape(devices, -1)
    mod_rows = jnp.concatenate([grad_modulation.reshape(devices, -1), gain_columns], axis=1)
    mod_high = mod_rows.astype(BF16).astype(F32)
    mod_low = mod_rows - mod_high
    time_rows = jnp.broadcast_to(time_low.astype(F32), (devices, TIME_WIDTH))
    first_meta = jnp.concatenate(
        [first_head, jnp.stack([mod_high, mod_low, time_rows], axis=1)], axis=1
    )
    embed_rows = over_cores(keep_e, swap_core(away_e))
    payload = jnp.concatenate([packed(first_target, first_meta, grad_rows), embed_rows], axis=1)
    payload, away_a, away_b, up_sum, layer_away, input_away = behind(
        payload, qkv_a.away(orders[0][1]), qkv_b.away(orders[1][1]), up_sum, layer_away, input_away
    )
    arrived = deliver(payload)
    qkv_a.send(orders[0][1], away_a)
    qkv_b.send(orders[1][1], away_b)
    qkv_rows = jnp.concatenate([qkv_a.total(), qkv_b.total()], axis=-1).astype(BF16)
    qkv_rows = qkv_rows.reshape((-1,) + qkv_rows.shape[-2:])
    layer_out = fill_other(core, layer_out, swap_core(layer_away))
    parts = between_planes(qkv_rows, dp_bits)
    parts[1], up_sum = behind(parts[1], up_sum)
    grad_w_qkv = sum(part.astype(F32) for part in parts)
    embed_sum = arrived[:, SLOT_ROWS:].astype(F32).reshape(groups, -1, EMB)
    embed_sum = jnp.sum(embed_sum, axis=0)
    grad_input = fill_other(core, grad_input, swap_core(input_away))
    grad_table = collect(arrived)
    sums = arrived[:, 1].astype(F32) + arrived[:, 2].astype(F32)
    time_width = sums.shape[1] // 2
    grad_w_time = lax.dot_general(
        arrived[:, 3].astype(F32),
        sums[:, :time_width],
        (((0,), (0,)), ((), ())),
        precision=lax.Precision.HIGHEST,
    )
    gain_sums = jnp.sum(sums[:, time_width:], axis=0).reshape(4, -1)
    peaks = arrived[:, 0, 3 * SLOT_ROWS : 3 * SLOT_ROWS + 2].astype(F32)
    peak = jnp.max(peaks[:, 0] * EXACT_BASE + peaks[:, 1]).astype(jnp.int32)
    turns = (peak + slots - 1) // slots

    def more_turns(state):
        return state[0] < turns

    def next_turn(state):
        turn, table = state
        target, head = dispatch(turn)
        meta = jnp.pad(head, ((0, 0), (0, META_ROWS - 1), (0, 0)))
        return turn + 1, table + collect(deliver(packed(target, meta, grad_rows)))

    _, grad_table = lax.while_loop(more_turns, next_turn, (jnp.int32(1), grad_table))
    return (
        layer_out,
        grad_input,
        grad_table,
        embed_sum.T,
        grad_w_time,
        gain_sums[0],
        gain_sums[1],
        gain_sums[2],
        gain_sums[3],
        grad_w_qkv.T,
        own_sum[:, hidden_width:].astype(F32).T,
        up_sum.astype(F32).T,
        own_sum[:, :hidden_width].astype(F32).T,
    )


def shards(*arguments):
    seq_count, pos_count = arguments[0].shape
    groups = lax.axis_size("dp")
    whole = seq_count == 2 and lax.axis_size("blk") == 2
    whole = whole and groups >= 4 and groups & (groups - 1) == 0 and pos_count % 256 == 0
    return whole_sequence_shards(*arguments) if whole else split_position_shards(*arguments)


def solution(mesh):
    return jax.shard_map(
        shards,
        mesh=mesh,
        in_specs=(
            P("dp", "blk"),
            P("dp"),
            P("dp"),
            P(),
            P(),
            P(),
            P(),
            P(),
            P(),
            P(),
            P(),
            P(),
            P(),
            P(),
            P("dp", "blk", None),
        ),
        out_specs=(
            P("dp", "blk", None),
            P("dp", "blk", None),
            P(("dp", "blk"), None),
            P(None, ("dp", "blk")),
            P(None, ("dp", "blk")),
            P(("dp", "blk")),
            P(("dp", "blk")),
            P(("dp", "blk")),
            P(("dp", "blk")),
            P(None, ("dp", "blk")),
            P(None, ("dp", "blk")),
            P(None, ("dp", "blk")),
            P(None, ("dp", "blk")),
        ),
        check_vma=False,
    )
```
